512 devices in a mesh: lat: 128 (over z, y, core), lon: 4 (over x).
Axes of the slice: x: 4, y: 4, z: 16, core: 2. Of those that a mesh axis runs over, the one named last changes fastest.
Arguments:
- grid: bfloat16 [256, 512, 384], P('lat', 'lon'), may hold values from -6 to 6
- cotangent: bfloat16 [256, 512, 384], P('lat', 'lon'), may hold values from -6 to 6
- spectral_weight: bfloat16 [2, 256, 384, 384], P(None, 'lat', None, 'lon'), may hold values from -0.21875 to 0.21875
- w_in: bfloat16 [384, 768], replicated, may hold values from -0.3125 to 0.3125
- w_out: bfloat16 [768, 384], replicated, may hold values from -0.21875 to 0.21875
Outputs:
- block_output: bfloat16 [256, 512, 384], P('lat', 'lon')
- grad_input: bfloat16 [256, 512, 384], P('lat', 'lon')
- grad_spectral: float32 [2, 256, 384, 384], P(None, 'lat', 'lon')
- grad_w_in: float32 [294912], P(('lat', 'lon'))
- grad_w_out: float32 [294912], P(('lat', 'lon'))
The draws below stay inside these ranges and needn't reach their ends.
All inputs are finite; a program needn't handle non-finite values.
Results may differ from the reference program's by a relative error of at most 0.019.
Values may be sent and summed in bfloat16 or wider, within the bound.
No kernel may reach another device: no remote copies, remote signals or barrier semaphores. Data moves between devices by JAX's collectives and lax.ppermute only.
A program may use at most 64 MiB of HBM per device.

```python
import math
import jax
import jax.numpy as jnp
from jax import lax

C = 384
HID = 768
NLAT = 256
M = 256
L = 256
NLON = 512


def levels(key, extent, pieces, least, top_value):
    def one(position, blocks):
        draws = jax.random.uniform(jax.random.fold_in(jax.random.fold_in(key, 6), position), (blocks,), jnp.float32, least / len(pieces), top_value / len(pieces))
        return jnp.repeat(jnp.exp(draws), extent[position] // blocks).reshape((-1,) + (1,) * (len(extent) - position - 1))

    factor_of = one(*pieces[0])
    for cut in pieces[1:]:
        factor_of = factor_of * one(*cut)
    return factor_of


def normal_values(key, shape, spread, most, pieces=(), kind=jnp.bfloat16):
    loudness = levels(key, shape, pieces, -0.22, 0.18) if pieces else 1.0
    array = jax.random.normal(key, shape, jnp.float32) * spread * loudness
    return jnp.minimum(jnp.maximum(array, -most), most).astype(kind)


def setup_inputs(seed: int = 0) -> dict:
    key_of = jax.random.split(jax.random.key(seed), 6)
    return {
        "grid": normal_values(key_of[0], (NLAT, NLON, C), 1.0, 6.0, ((0, 128), (1, 4))),
        "cotangent": normal_values(key_of[1], (NLAT, NLON, C), 1.0, 6.0, ((0, 128), (1, 4))),
        "spectral_weight": normal_values(key_of[2], (2, L, C, C), (2 * C) ** -0.5, 0.21875, ((1, 128), (3, 4))),
        "w_in": normal_values(key_of[3], (C, HID), C ** -0.5, 0.3125),
        "w_out": normal_values(key_of[4], (HID, C), HID ** -0.5, 0.21875),
    }


def lat_geometry(nlat, nlon):
    rows = jnp.arange(nlat, dtype=jnp.float32)
    theta = math.pi * (rows + 0.5) / nlat
    sines = jnp.sin(theta)
    weights = math.pi / nlat * sines * (2.0 * math.pi / nlon)
    return (jnp.cos(theta), jnp.log(sines), weights)

def fourier_tables(nlon, modes):
    lon_ids = jnp.arange(nlon, dtype=jnp.int32)[:, None]
    mode_ids = jnp.arange(modes, dtype=jnp.int32)[None, :]
    phase = (lon_ids * mode_ids % nlon).astype(jnp.float32)
    angle = 2.0 * math.pi / nlon * phase
    cosine = jnp.cos(angle).astype(jnp.bfloat16)
    sine = jnp.sin(angle).astype(jnp.bfloat16)
    factor = jnp.where(mode_ids == 0, 1.0, 2.0).astype(jnp.float32)
    cos_syn = (cosine.astype(jnp.float32) * factor).astype(jnp.bfloat16)
    sin_syn = (sine.astype(jnp.float32) * factor).astype(jnp.bfloat16)
    return (cosine, sine, cos_syn, sin_syn)

def combine_steps(earlier, later):
    e11, e12, e21, e22, escale = earlier
    l11, l12, l21, l22, lscale = later
    m11 = l11 * e11 + l12 * e21
    m12 = l11 * e12 + l12 * e22
    m21 = l21 * e11 + l22 * e21
    m22 = l21 * e12 + l22 * e22
    largest = jnp.maximum(jnp.maximum(jnp.abs(m11), jnp.abs(m12)), jnp.maximum(jnp.abs(m21), jnp.abs(m22)))
    return (m11 / largest, m12 / largest, m21 / largest, m22 / largest, escale + lscale + jnp.log(largest))

def legendre_rows(order, degrees, cosv, logsin, limit):
    level = degrees[:, None]
    active = level >= order + 2.0
    safe = jnp.where(active, level, order + 2.0)
    alpha = jnp.sqrt((4.0 * safe * safe - 1.0) / (safe * safe - order * order))
    beta = jnp.sqrt(((safe - 1.0) * (safe - 1.0) - order * order) / (4.0 * (safe - 1.0) * (safe - 1.0) - 1.0))
    ones = jnp.ones_like(level * cosv)
    zeros = jnp.zeros_like(ones)
    step11 = jnp.where(active, alpha * cosv, ones)
    step12 = jnp.where(active, -alpha * beta * ones, zeros)
    step21 = jnp.where(active, ones, zeros)
    step22 = jnp.where(active, zeros, ones)
    m11, m12, m21, m22, scale = lax.associative_scan(combine_steps, (step11, step12, step21, step22, zeros), axis=0)
    log_start = 0.5 * (jnp.log((2.0 * order + 1.0) / (4.0 * math.pi)) + lax.lgamma(2.0 * order + 1.0) - 2.0 * lax.lgamma(order + 1.0) - order * math.log(4.0)) + order * logsin
    first = jnp.sqrt(2.0 * order + 3.0) * cosv
    value = (m11 * first + m12) * jnp.exp(scale + log_start)
    value = jnp.where(level >= order + 1.0, value, jnp.where(level == order, jnp.exp(log_start) * ones, zeros))
    return jnp.where(level < limit, value, zeros)

def gelu_value(values):
    return 0.5 * values * (1.0 + lax.erf(values * (1.0 / math.sqrt(2.0))))

def gelu_slope(values):
    return 0.5 * (1.0 + lax.erf(values * (1.0 / math.sqrt(2.0)))) + values * jnp.exp(-0.5 * values * values) * (1.0 / math.sqrt(2.0 * math.pi))

def reference(grid, cotangent, spectral_weight, w_in, w_out):
    highest = lax.Precision.HIGHEST
    cosv, logsin, quad = lat_geometry(NLAT, NLON)
    cosine, sine, cos_syn, sin_syn = fourier_tables(NLON, M)
    degrees = jnp.arange(L, dtype=jnp.float32)

    def one_table(order):
        return legendre_rows(order, degrees, cosv, logsin, L).astype(jnp.bfloat16)
    tables = lax.map(one_table, jnp.arange(M, dtype=jnp.float32))

    def analyze(pair):
        table, data = pair
        return jnp.dot(table, data, preferred_element_type=jnp.float32).astype(jnp.bfloat16)

    def synthesize(pair):
        table, coef = pair
        return lax.dot_general(table, coef, (((0,), (0,)), ((), ())), preferred_element_type=jnp.float32).astype(jnp.bfloat16)
    grid_wide = grid.astype(jnp.float32)
    four_re = jnp.einsum('jkc,km->mjc', grid_wide, cosine.astype(jnp.float32), precision=highest) * quad[None, :, None]
    four_im = -jnp.einsum('jkc,km->mjc', grid_wide, sine.astype(jnp.float32), precision=highest) * quad[None, :, None]
    four = jnp.concatenate([four_re, four_im], axis=2).astype(jnp.bfloat16)
    spectrum = lax.map(analyze, (tables, four))

    def mix(item):
        degree, weight_re, weight_im = item
        rows = lax.dynamic_index_in_dim(spectrum, degree, 1, keepdims=False)
        part_re = rows[:, :C]
        part_im = rows[:, C:]
        out_re = jnp.dot(part_re, weight_re, preferred_element_type=jnp.float32) - jnp.dot(part_im, weight_im, preferred_element_type=jnp.float32)
        out_im = jnp.dot(part_re, weight_im, preferred_element_type=jnp.float32) + jnp.dot(part_im, weight_re, preferred_element_type=jnp.float32)
        return jnp.concatenate([out_re, out_im], axis=1).astype(jnp.bfloat16)
    mixed = lax.map(mix, (jnp.arange(L, dtype=jnp.int32), spectral_weight[0], spectral_weight[1]))
    fields = lax.map(synthesize, (tables, jnp.swapaxes(mixed, 0, 1))).astype(jnp.float32)
    wave = jnp.einsum('mjc,km->jkc', fields[:, :, :C], cos_syn.astype(jnp.float32), precision=highest) - jnp.einsum('mjc,km->jkc', fields[:, :, C:], sin_syn.astype(jnp.float32), precision=highest)
    wave = lax.optimization_barrier(wave.astype(jnp.bfloat16)).astype(jnp.float32)
    hidden = (grid_wide + wave).astype(jnp.bfloat16)
    rows_all = hidden.reshape(NLAT * NLON, C)
    pre = jnp.dot(rows_all, w_in, preferred_element_type=jnp.float32)
    act = gelu_value(pre).astype(jnp.bfloat16)
    block_output = (rows_all.astype(jnp.float32) + jnp.dot(act, w_out, preferred_element_type=jnp.float32)).astype(jnp.bfloat16)
    back = cotangent.reshape(NLAT * NLON, C)
    act_grad = jnp.dot(back, w_out.T, preferred_element_type=jnp.float32)
    pre_grad = (act_grad * gelu_slope(pre)).astype(jnp.bfloat16)
    hidden_grad = (back.astype(jnp.float32) + jnp.dot(pre_grad, w_in.T, preferred_element_type=jnp.float32)).astype(jnp.bfloat16)
    grad_w_out = jnp.dot(act.T, back, preferred_element_type=jnp.float32)
    grad_w_in = jnp.dot(rows_all.T, pre_grad, preferred_element_type=jnp.float32)
    grad_grid = hidden_grad.reshape(NLAT, NLON, C).astype(jnp.float32)
    field_re = jnp.einsum('jkc,km->mjc', grad_grid, cos_syn.astype(jnp.float32), precision=highest)
    field_im = -jnp.einsum('jkc,km->mjc', grad_grid, sin_syn.astype(jnp.float32), precision=highest)
    field_grad = jnp.concatenate([field_re, field_im], axis=2).astype(jnp.bfloat16)
    mixed_grad = lax.map(analyze, (tables, field_grad))

    def unmix(item):
        degree, weight_re, weight_im = item
        grads = lax.dynamic_index_in_dim(mixed_grad, degree, 1, keepdims=False)
        rows = lax.dynamic_index_in_dim(spectrum, degree, 1, keepdims=False)
        grad_re = grads[:, :C]
        grad_im = grads[:, C:]
        spec_re = rows[:, :C]
        spec_im = rows[:, C:]
        back_re = jnp.dot(grad_re, weight_re.T, preferred_element_type=jnp.float32) + jnp.dot(grad_im, weight_im.T, preferred_element_type=jnp.float32)
        back_im = jnp.dot(grad_im, weight_re.T, preferred_element_type=jnp.float32) - jnp.dot(grad_re, weight_im.T, preferred_element_type=jnp.float32)
        weight_grad_re = jnp.dot(spec_re.T, grad_re, preferred_element_type=jnp.float32) + jnp.dot(spec_im.T, grad_im, preferred_element_type=jnp.float32)
        weight_grad_im = jnp.dot(spec_re.T, grad_im, preferred_element_type=jnp.float32) - jnp.dot(spec_im.T, grad_re, preferred_element_type=jnp.float32)
        return (jnp.concatenate([back_re, back_im], axis=1).astype(jnp.bfloat16), jnp.stack([weight_grad_re, weight_grad_im]))
    spectrum_grad, weight_grads = lax.map(unmix, (jnp.arange(L, dtype=jnp.int32), spectral_weight[0], spectral_weight[1]))
    four_grad = lax.map(synthesize, (tables, jnp.swapaxes(spectrum_grad, 0, 1))).astype(jnp.float32)
    wave_back = (jnp.einsum('mjc,km->jkc', four_grad[:, :, :C], cosine.astype(jnp.float32), precision=highest) - jnp.einsum('mjc,km->jkc', four_grad[:, :, C:], sine.astype(jnp.float32), precision=highest)) * quad[:, None, None]
    wave_back = lax.optimization_barrier(wave_back.astype(jnp.bfloat16)).astype(jnp.float32)
    grad_input = (grad_grid + wave_back).astype(jnp.bfloat16)
    grad_spectral = jnp.swapaxes(weight_grads, 0, 1)
    return (block_output.reshape(NLAT, NLON, C), grad_input, grad_spectral, grad_w_in.reshape(-1), grad_w_out.reshape(-1))
```

```python
import math

import jax
import jax.numpy as jnp
import ml_dtypes
import numpy as np
from jax import lax
from jax.sharding import PartitionSpec as P


def legendre_table(size):
    theta = math.pi * (np.arange(size) + 0.5) / size
    cosv, sinv = np.cos(theta), np.sin(theta)
    order = np.arange(size, dtype=np.float64)[:, None]
    start = np.empty((size, size))
    start[0] = math.sqrt(1.0 / (4.0 * math.pi))
    for m in range(1, size):
        start[m] = start[m - 1] * math.sqrt((2 * m + 1) / (2.0 * m)) * sinv
    table = np.zeros((size, size, size), dtype=ml_dtypes.bfloat16)
    before = np.zeros((size, size))
    now = np.zeros((size, size))
    for level in range(size):
        safe = np.where(order < level, order, 0.0)
        alpha = np.sqrt((4.0 * level * level - 1.0) / (level * level - safe * safe)) if level else 0.0
        beta = (
            np.sqrt(((level - 1.0) ** 2 - safe * safe).clip(0) / (4.0 * (level - 1.0) ** 2 - 1.0))
            if level > 1
            else 0.0
        )
        value = np.where(order < level, alpha * (cosv * now - beta * before), 0.0)
        value[level] = start[level]
        table[:, level, :] = value.astype(np.float32).astype(ml_dtypes.bfloat16)
        before, now = now, value
    return table


def quadrature(nlat, nlon):
    theta = math.pi * (np.arange(nlat) + 0.5) / nlat
    return (math.pi / nlat * np.sin(theta) * (2.0 * math.pi / nlon)).astype(np.float32)


def fourier_tables(nlon, modes, lat_count):
    phase = np.arange(nlon)[:, None] * np.arange(modes)[None, :] % nlon
    angle = 2.0 * math.pi / nlon * phase
    cosine = np.cos(angle).astype(np.float32).astype(ml_dtypes.bfloat16)
    sine = np.sin(angle).astype(np.float32).astype(ml_dtypes.bfloat16)
    pair = np.stack([cosine, -sine]).reshape(2, nlon, modes // lat_count, lat_count)
    plain = pair.transpose(1, 2, 0, 3).reshape(nlon, 2 * modes)
    factor = np.where(np.arange(modes) == 0, 1.0, 2.0).astype(np.float32)
    doubled = np.stack([cosine, -sine]).astype(np.float32) * factor
    doubled = doubled.astype(ml_dtypes.bfloat16).reshape(2, nlon, modes // lat_count, lat_count)
    doubled = doubled.transpose(1, 2, 0, 3).reshape(nlon, 2 * modes)
    return plain, doubled


def gelu_parts(values):
    half = 0.5 * (1.0 + lax.erf(values * (1.0 / math.sqrt(2.0))))
    slope = half + values * jnp.exp(-0.5 * values * values) * (1.0 / math.sqrt(2.0 * math.pi))
    return values * half, slope


def swap_blocks(values, axis):
    return lax.all_to_all(values, axis, split_axis=0, concat_axis=0, tiled=True)


def body(table_all, plain, doubled, quad, grid, cotangent, spectral_weight, w_in, w_out):
    lat_count = lax.axis_size("lat")
    lon_count = lax.axis_size("lon")
    lat_index = lax.axis_index("lat")
    lon_index = lax.axis_index("lon")
    rows, lon_rows, width = grid.shape
    quarter = width // lon_count
    total_lat = rows * lat_count
    total_lon = lon_rows * lon_count
    parts = 2 * rows
    packed = parts * quarter
    tables = lax.dynamic_index_in_dim(table_all, lat_index, 0, keepdims=False)
    local_quad = lax.dynamic_slice_in_dim(quad, lat_index * rows, rows)
    quad_lanes = jnp.repeat(local_quad, quarter)[None, :]
    first_half = (jnp.arange(packed) < packed // 2)[None, :]

    def lon_split(values):
        values = values.reshape(rows, lon_rows, lon_count, quarter).transpose(2, 1, 0, 3)
        got = swap_blocks(values.reshape(lon_count, lon_rows, rows * quarter), "lon")
        return got.reshape(total_lon, rows * quarter)

    def lon_merge(values):
        got = swap_blocks(values.reshape(lon_count, lon_rows, rows * quarter), "lon")
        got = got.reshape(lon_count, lon_rows, rows, quarter).transpose(2, 1, 0, 3)
        return got.reshape(rows * lon_rows, width)

    def to_fourier(values, matrix, scale):
        out = lax.dot_general(
            matrix, values, (((0,), (0,)), ((), ())), preferred_element_type=jnp.float32
        )
        if scale is not None:
            out = out * scale
        out = out.astype(jnp.bfloat16).reshape(parts, lat_count, rows, quarter)
        return out.transpose(1, 2, 0, 3).reshape(lat_count, rows, packed)

    def from_fourier(values, matrix, scale):
        values = values.reshape(lat_count, rows, parts, quarter).transpose(2, 0, 1, 3)
        values = values.reshape(parts * lat_count, rows * quarter)
        out = jnp.dot(matrix, values, preferred_element_type=jnp.float32)
        if scale is not None:
            out = out * scale
        return out.astype(jnp.bfloat16)

    def analyze(values):
        values = values.reshape(total_lat, packed)
        low = jnp.dot(tables[0], values, preferred_element_type=jnp.float32)
        high = jnp.dot(tables[1], values, preferred_element_type=jnp.float32)
        out = jnp.where(first_half, low, high).astype(jnp.bfloat16)
        return out.reshape(lat_count, rows, packed)

    def synthesize(values):
        values = values.reshape(total_lat, packed)
        dims = (((0,), (0,)), ((), ()))
        low = lax.dot_general(tables[0], values, dims, preferred_element_type=jnp.float32)
        high = lax.dot_general(tables[1], values, dims, preferred_element_type=jnp.float32)
        out = jnp.where(first_half, low, high).astype(jnp.bfloat16)
        return out.reshape(lat_count, rows, packed)

    def block_weights(weights):
        w_re, w_im = weights[:, 0], weights[:, 1]
        top = jnp.concatenate([w_re, w_im], axis=3)
        low = jnp.concatenate([-w_im, w_re], axis=3)
        one = jnp.concatenate([top, low], axis=2)
        zero = jnp.zeros_like(one)
        return jnp.concatenate(
            [jnp.concatenate([one, zero], axis=3), jnp.concatenate([zero, one], axis=3)], axis=2
        )

    with jax.named_scope("weights"):
        by_input = spectral_weight.reshape(2, rows, lon_count, quarter, quarter)
        by_input = by_input.transpose(2, 0, 1, 3, 4)
        mix_weights = block_weights(by_input)
        unmix_weights = block_weights(swap_blocks(by_input, "lon"))
    with jax.named_scope("forward_analysis"):
        spread = lon_split(grid)
        four = to_fourier(spread, plain, quad_lanes)
        spectrum = swap_blocks(analyze(swap_blocks(four, "lat")), "lat")
    with jax.named_scope("mix"):
        piece = lax.all_gather(spectrum, "lon", axis=0)
        mixed = jnp.einsum(
            "xplk,xlkn->pln", piece, mix_weights, preferred_element_type=jnp.float32
        ).astype(jnp.bfloat16)
    with jax.named_scope("forward_synthesis"):
        fields = swap_blocks(synthesize(swap_blocks(mixed, "lat")), "lat")
        wave_rows = lon_merge(from_fourier(fields, doubled, None))
    with jax.named_scope("pointwise"):
        flat_grid = grid.reshape(-1, width)
        hidden = (flat_grid.astype(jnp.float32) + wave_rows.astype(jnp.float32)).astype(
            jnp.bfloat16
        )
        back = cotangent.reshape(-1, width)
        act_grad = lax.dot_general(
            back, w_out, (((1,), (1,)), ((), ())), preferred_element_type=jnp.float32
        )
        pre = jnp.dot(hidden, w_in, preferred_element_type=jnp.float32)
        value, slope = gelu_parts(pre)
        act = value.astype(jnp.bfloat16)
        pre_grad = (act_grad * slope).astype(jnp.bfloat16)
        hidden_grad = (
            back.astype(jnp.float32)
            + lax.dot_general(
                pre_grad, w_in, (((1,), (1,)), ((), ())), preferred_element_type=jnp.float32
            )
        ).astype(jnp.bfloat16)
        block_output = (
            hidden.astype(jnp.float32) + jnp.dot(act, w_out, preferred_element_type=jnp.float32)
        ).astype(jnp.bfloat16)
    with jax.named_scope("pointwise_weights"):
        over_rows = (((0,), (0,)), ((), ()))
        out_part = lax.dot_general(act, back, over_rows, preferred_element_type=jnp.float32)
        in_part = lax.dot_general(hidden, pre_grad, over_rows, preferred_element_type=jnp.float32)
        in_part = in_part.reshape(out_part.shape)
        even = lat_index % 2 == 0
        keep = jnp.where(even, in_part, out_part)
        give = jnp.where(even, out_part, in_part)
        partner = [(i, i ^ 1) for i in range(lat_count)]
        keep = keep + lax.ppermute(give, "lat", partner)
        keep = lax.psum(keep, "lon").reshape(lat_count, -1)
        chunk = keep.shape[1] // lon_count
        keep = lax.dynamic_slice_in_dim(keep, lon_index * chunk, chunk, axis=1)
        keep = keep.astype(jnp.bfloat16)
        room = -(-chunk // (rows * 128)) * rows * 128
        extra = jnp.pad(keep, ((0, 0), (0, room - chunk))).reshape(lat_count, rows, -1)
    with jax.named_scope("backward_analysis"):
        grad_spread = lon_split(hidden_grad.reshape(grid.shape))
        field_grad = to_fourier(grad_spread, doubled, None)
        mixed_grad = swap_blocks(analyze(swap_blocks(field_grad, "lat")), "lat")
    with jax.named_scope("unmix"):
        piece = lax.all_gather(mixed_grad, "lon", axis=0)
        spectrum_grad = jnp.einsum(
            "xplk,xlnk->pln", piece, unmix_weights, preferred_element_type=jnp.float32
        ).astype(jnp.bfloat16)
        outer = jnp.einsum("pln,xplk->xlnk", spectrum, piece, preferred_element_type=jnp.float32)
        half = packed // 2
        outer = outer[:, :, :half, :half] + outer[:, :, half:, half:]
        grad_re = outer[:, :, :quarter, :quarter] + outer[:, :, quarter:, quarter:]
        grad_im = outer[:, :, :quarter, quarter:] - outer[:, :, quarter:, :quarter]
        grad_spectral = jnp.stack([grad_re, grad_im]).transpose(0, 2, 3, 1, 4)
        grad_spectral = grad_spectral.reshape(2, rows, quarter, width)
    with jax.named_scope("backward_synthesis"):
        four_grad = synthesize(swap_blocks(spectrum_grad, "lat"))
        got = swap_blocks(jnp.concatenate([four_grad, extra], axis=2), "lat")
        sums = got[:, :, packed:].reshape(lat_count // 2, 2, room)[:, :, :chunk]
        sums = jnp.sum(sums.astype(jnp.float32), axis=0)
        wave_grad = lon_merge(from_fourier(got[:, :, :packed], plain, quad_lanes))
        grad_input = (hidden_grad.astype(jnp.float32) + wave_grad.astype(jnp.float32)).astype(
            jnp.bfloat16
        )
    return (
        block_output.reshape(grid.shape),
        grad_input.reshape(grid.shape),
        grad_spectral,
        sums[0],
        sums[1],
    )


def solution(mesh):
    in_specs = (P("lat", "lon", None), P("lat", "lon", None), P(None, "lat", None, "lon"), P(), P())
    out_specs = (
        P("lat", "lon", None),
        P("lat", "lon", None),
        P(None, "lat", "lon", None),
        P(("lat", "lon")),
        P(("lat", "lon")),
    )
    lat_count = mesh.shape["lat"]

    def call(grid, cotangent, spectral_weight, w_in, w_out):
        nlat, nlon, _ = grid.shape
        table = legendre_table(nlat).reshape(nlat // lat_count, lat_count, nlat, nlat)
        table = np.ascontiguousarray(table.swapaxes(0, 1))
        plain, doubled = fourier_tables(nlon, nlat, lat_count)
        quad = quadrature(nlat, nlon)
        mapped = jax.shard_map(
            body,
            mesh=mesh,
            in_specs=(P(), P(), P(), P()) + in_specs,
            out_specs=out_specs,
            check_vma=False,
        )
        return mapped(table, plain, doubled, quad, grid, cotangent, spectral_weight, w_in, w_out)

    return call
```

```python
import math

import jax
import jax.numpy as jnp
import ml_dtypes
import numpy as np
from jax import lax
from jax.sharding import PartitionSpec as P


def legendre_table(size):
    theta = math.pi * (np.arange(size) + 0.5) / size
    cosv, sinv = np.cos(theta), np.sin(theta)
    order = np.arange(size, dtype=np.float64)[:, None]
    start = np.empty((size, size))
    start[0] = math.sqrt(1.0 / (4.0 * math.pi))
    for m in range(1, size):
        start[m] = start[m - 1] * math.sqrt((2 * m + 1) / (2.0 * m)) * sinv
    table = np.zeros((size, size, size), dtype=ml_dtypes.bfloat16)
    before = np.zeros((size, size))
    now = np.zeros((size, size))
    for level in range(size):
        safe = np.where(order < level, order, 0.0)
        alpha = np.sqrt((4.0 * level * level - 1.0) / (level * level - safe * safe)) if level else 0.0
        beta = (
            np.sqrt(((level - 1.0) ** 2 - safe * safe).clip(0) / (4.0 * (level - 1.0) ** 2 - 1.0))
            if level > 1
            else 0.0
        )
        value = np.where(order < level, alpha * (cosv * now - beta * before), 0.0)
        value[level] = start[level]
        table[:, level, :] = value.astype(np.float32).astype(ml_dtypes.bfloat16)
        before, now = now, value
    return table


def quadrature(nlat, nlon):
    theta = math.pi * (np.arange(nlat) + 0.5) / nlat
    return (math.pi / nlat * np.sin(theta) * (2.0 * math.pi / nlon)).astype(np.float32)


def fourier_tables(nlon, modes, lat_count):
    phase = np.arange(nlon)[:, None] * np.arange(modes)[None, :] % nlon
    angle = 2.0 * math.pi / nlon * phase
    cosine = np.cos(angle).astype(np.float32).astype(ml_dtypes.bfloat16)
    sine = np.sin(angle).astype(np.float32).astype(ml_dtypes.bfloat16)
    pair = np.stack([cosine, -sine]).reshape(2, nlon, modes // lat_count, lat_count)
    plain = pair.transpose(1, 2, 0, 3).reshape(nlon, 2 * modes)
    factor = np.where(np.arange(modes) == 0, 1.0, 2.0).astype(np.float32)
    doubled = np.stack([cosine, -sine]).astype(np.float32) * factor
    doubled = doubled.astype(ml_dtypes.bfloat16).reshape(2, nlon, modes // lat_count, lat_count)
    doubled = doubled.transpose(1, 2, 0, 3).reshape(nlon, 2 * modes)
    return plain, doubled


def gelu_parts(values):
    half = 0.5 * (1.0 + lax.erf(values * (1.0 / math.sqrt(2.0))))
    slope = half + values * jnp.exp(-0.5 * values * values) * (1.0 / math.sqrt(2.0 * math.pi))
    return values * half, slope


def swap_blocks(values, axis):
    return lax.all_to_all(values, axis, split_axis=0, concat_axis=0, tiled=True)


def lon_exchange(blocks, lon_index, lon_count):
    doubled = jnp.concatenate([blocks, blocks])
    moved = [lax.dynamic_index_in_dim(blocks, lon_index, 0, keepdims=False)]
    for shift in range(1, lon_count):
        block = lax.dynamic_index_in_dim(doubled, lon_index + shift, 0, keepdims=False)
        pairs = [(i, (i + shift) % lon_count) for i in range(lon_count)]
        moved.append(lax.ppermute(block, "lon", pairs))
    backwards = jnp.stack(moved[::-1] * 2)
    first = lon_count - 1 - lon_index
    return lax.dynamic_slice_in_dim(backwards, first, lon_count, 0)


def halve_over_devices(values, lat_index, lon_index, lat_count, lon_count):
    count, size = values.shape
    chunk = size // (lat_count * lon_count)
    lat_bits = lat_count.bit_length() - 1

    def step(values, axis, index, size, mask, bit, outer, inner):
        values = values.reshape(outer, 2, *inner)
        high = (index >> bit) & 1 == 1
        keep = jnp.where(high, values[:, 1], values[:, 0])
        give = jnp.where(high, values[:, 0], values[:, 1]).astype(jnp.bfloat16)
        got = lax.ppermute(give, axis, [(i, i ^ mask) for i in range(size)])
        return keep + got.astype(jnp.float32)

    rest = count * lat_count // 2
    values = step(values, "lat", lat_index, lat_count, 1, 0, rest, (lon_count * chunk,))
    inner = lon_count
    mask = lon_count - 1
    while inner > 1:
        inner //= 2
        values = step(
            values, "lon", lon_index, lon_count, mask, inner.bit_length() - 1, rest, (inner * chunk,)
        )
        mask >>= 1
    outer = rest // 4
    values = step(values, "lat", lat_index, lat_count, 6, 2, outer, (2, chunk))
    values = step(values, "lat", lat_index, lat_count, 2, 1, outer, (chunk,))
    for bit in range(lat_bits - 1, 2, -1):
        outer = count
        rows = 1 << (bit - 3)
        values = step(values, "lat", lat_index, lat_count, 1 << bit, bit, outer, (rows, chunk))
    return values.reshape(count, chunk)


def body(table_all, plain, doubled, quad, grid, cotangent, spectral_weight, w_in, w_out):
    lat_count = lax.axis_size("lat")
    lon_count = lax.axis_size("lon")
    lat_index = lax.axis_index("lat")
    lon_index = lax.axis_index("lon")
    rows, lon_rows, width = grid.shape
    quarter = width // lon_count
    total_lat = rows * lat_count
    total_lon = lon_rows * lon_count
    parts = 2 * rows
    packed = parts * quarter
    tables = lax.dynamic_index_in_dim(table_all, lat_index, 0, keepdims=False)
    local_quad = lax.dynamic_slice_in_dim(quad, lat_index * rows, rows)
    quad_lanes = jnp.repeat(local_quad, quarter)[None, :]
    first_half = (jnp.arange(packed) < packed // 2)[None, :]

    def lon_split(values):
        values = values.reshape(rows, lon_rows, lon_count, quarter).transpose(2, 1, 0, 3)
        got = swap_blocks(values.reshape(lon_count, lon_rows, rows * quarter), "lon")
        return got.reshape(total_lon, rows * quarter)

    def lon_merge(values):
        got = swap_blocks(values.reshape(lon_count, lon_rows, rows * quarter), "lon")
        got = got.reshape(lon_count, lon_rows, rows, quarter).transpose(2, 1, 0, 3)
        return got.reshape(rows * lon_rows, width)

    def to_fourier(values, matrix, scale):
        out = lax.dot_general(
            matrix, values, (((0,), (0,)), ((), ())), preferred_element_type=jnp.float32
        )
        if scale is not None:
            out = out * scale
        out = out.astype(jnp.bfloat16).reshape(parts, lat_count, rows, quarter)
        return out.transpose(1, 2, 0, 3).reshape(lat_count, rows, packed)

    def from_fourier(values, matrix, scale):
        values = values.reshape(lat_count, rows, parts, quarter).transpose(2, 0, 1, 3)
        values = values.reshape(parts * lat_count, rows * quarter)
        out = jnp.dot(matrix, values, preferred_element_type=jnp.float32)
        if scale is not None:
            out = out * scale
        return out.astype(jnp.bfloat16)

    def analyze(values):
        values = values.reshape(total_lat, packed)
        low = jnp.dot(tables[0], values, preferred_element_type=jnp.float32)
        high = jnp.dot(tables[1], values, preferred_element_type=jnp.float32)
        out = jnp.where(first_half, low, high).astype(jnp.bfloat16)
        return out.reshape(lat_count, rows, packed)

    def synthesize(values):
        values = values.reshape(total_lat, packed)
        dims = (((0,), (0,)), ((), ()))
        low = lax.dot_general(tables[0], values, dims, preferred_element_type=jnp.float32)
        high = lax.dot_general(tables[1], values, dims, preferred_element_type=jnp.float32)
        out = jnp.where(first_half, low, high).astype(jnp.bfloat16)
        return out.reshape(lat_count, rows, packed)

    def block_weights(weights):
        w_re, w_im = weights[:, 0], weights[:, 1]
        top = jnp.concatenate([w_re, w_im], axis=3)
        low = jnp.concatenate([-w_im, w_re], axis=3)
        one = jnp.concatenate([top, low], axis=2)
        zero = jnp.zeros_like(one)
        return jnp.concatenate(
            [jnp.concatenate([one, zero], axis=3), jnp.concatenate([zero, one], axis=3)], axis=2
        )

    with jax.named_scope("weights"):
        by_input = spectral_weight.reshape(2, rows, lon_count, quarter, quarter)
        by_input = by_input.transpose(2, 0, 1, 3, 4)
        mix_weights = block_weights(by_input)
        unmix_weights = block_weights(lon_exchange(by_input, lon_index, lon_count))
    with jax.named_scope("forward_analysis"):
        spread = lon_split(grid)
        four = to_fourier(spread, plain, quad_lanes)
        spectrum = swap_blocks(analyze(swap_blocks(four, "lat")), "lat")
    with jax.named_scope("mix"):
        piece = lax.all_gather(spectrum, "lon", axis=0)
        mixed = jnp.einsum(
            "xplk,xlkn->pln", piece, mix_weights, preferred_element_type=jnp.float32
        ).astype(jnp.bfloat16)
    with jax.named_scope("forward_synthesis"):
        fields = swap_blocks(synthesize(swap_blocks(mixed, "lat")), "lat")
        wave_rows = lon_merge(from_fourier(fields, doubled, None))
    with jax.named_scope("pointwise"):
        flat_grid = grid.reshape(-1, width)
        hidden = (flat_grid.astype(jnp.float32) + wave_rows.astype(jnp.float32)).astype(
            jnp.bfloat16
        )
        back = cotangent.reshape(-1, width)
        act_grad = lax.dot_general(
            back, w_out, (((1,), (1,)), ((), ())), preferred_element_type=jnp.float32
        )
        pre = jnp.dot(hidden, w_in, preferred_element_type=jnp.float32)
        value, slope = gelu_parts(pre)
        act = value.astype(jnp.bfloat16)
        pre_grad = (act_grad * slope).astype(jnp.bfloat16)
        hidden_grad = (
            back.astype(jnp.float32)
            + lax.dot_general(
                pre_grad, w_in, (((1,), (1,)), ((), ())), preferred_element_type=jnp.float32
            )
        ).astype(jnp.bfloat16)
        block_output = (
            hidden.astype(jnp.float32) + jnp.dot(act, w_out, preferred_element_type=jnp.float32)
        ).astype(jnp.bfloat16)
    with jax.named_scope("pointwise_weights"):
        over_rows = (((0,), (0,)), ((), ()))
        out_part = lax.dot_general(act, back, over_rows, preferred_element_type=jnp.float32)
        in_part = lax.dot_general(hidden, pre_grad, over_rows, preferred_element_type=jnp.float32)
        parts_all = jnp.stack([in_part.reshape(-1), out_part.reshape(-1)])
        sums = halve_over_devices(parts_all, lat_index, lon_index, lat_count, lon_count)
    with jax.named_scope("backward_analysis"):
        grad_spread = lon_split(hidden_grad.reshape(grid.shape))
        field_grad = to_fourier(grad_spread, doubled, None)
        mixed_grad = swap_blocks(analyze(swap_blocks(field_grad, "lat")), "lat")
    with jax.named_scope("unmix"):
        piece = lax.all_gather(mixed_grad, "lon", axis=0)
        spectrum_grad = jnp.einsum(
            "xplk,xlnk->pln", piece, unmix_weights, preferred_element_type=jnp.float32
        ).astype(jnp.bfloat16)
        outer = jnp.einsum("pln,xplk->xlnk", spectrum, piece, preferred_element_type=jnp.float32)
        half = packed // 2
        outer = outer[:, :, :half, :half] + outer[:, :, half:, half:]
        grad_re = outer[:, :, :quarter, :quarter] + outer[:, :, quarter:, quarter:]
        grad_im = outer[:, :, :quarter, quarter:] - outer[:, :, quarter:, :quarter]
        grad_spectral = jnp.stack([grad_re, grad_im]).transpose(0, 2, 3, 1, 4)
        grad_spectral = grad_spectral.reshape(2, rows, quarter, width)
    with jax.named_scope("backward_synthesis"):
        four_grad = swap_blocks(synthesize(swap_blocks(spectrum_grad, "lat")), "lat")
        wave_grad = lon_merge(from_fourier(four_grad, plain, quad_lanes))
        grad_input = (hidden_grad.astype(jnp.float32) + wave_grad.astype(jnp.float32)).astype(
            jnp.bfloat16
        )
    return (
        block_output.reshape(grid.shape),
        grad_input.reshape(grid.shape),
        grad_spectral,
        sums[0],
        sums[1],
    )


def solution(mesh):
    in_specs = (P("lat", "lon", None), P("lat", "lon", None), P(None, "lat", None, "lon"), P(), P())
    out_specs = (
        P("lat", "lon", None),
        P("lat", "lon", None),
        P(None, "lat", "lon", None),
        P(("lat", "lon")),
        P(("lat", "lon")),
    )
    lat_count = mesh.shape["lat"]

    def call(grid, cotangent, spectral_weight, w_in, w_out):
        nlat, nlon, _ = grid.shape
        table = legendre_table(nlat).reshape(nlat // lat_count, lat_count, nlat, nlat)
        table = np.ascontiguousarray(table.swapaxes(0, 1))
        plain, doubled = fourier_tables(nlon, nlat, lat_count)
        quad = quadrature(nlat, nlon)
        mapped = jax.shard_map(
            body,
            mesh=mesh,
            in_specs=(P(), P(), P(), P()) + in_specs,
            out_specs=out_specs,
            check_vma=False,
        )
        return mapped(table, plain, doubled, quad, grid, cotangent, spectral_weight, w_in, w_out)

    return call
```

```python
import math

import jax
import jax.numpy as jnp
import ml_dtypes
import numpy as np
from jax import lax
from jax.sharding import PartitionSpec as P


def legendre_table(size):
    theta = math.pi * (np.arange(size) + 0.5) / size
    cosv, sinv = np.cos(theta), np.sin(theta)
    order = np.arange(size, dtype=np.float64)[:, None]
    start = np.empty((size, size))
    start[0] = math.sqrt(1.0 / (4.0 * math.pi))
    for m in range(1, size):
        start[m] = start[m - 1] * math.sqrt((2 * m + 1) / (2.0 * m)) * sinv
    table = np.zeros((size, size, size), dtype=ml_dtypes.bfloat16)
    before = np.zeros((size, size))
    now = np.zeros((size, size))
    for level in range(size):
        safe = np.where(order < level, order, 0.0)
        alpha = np.sqrt((4.0 * level * level - 1.0) / (level * level - safe * safe)) if level else 0.0
        beta = (
            np.sqrt(((level - 1.0) ** 2 - safe * safe).clip(0) / (4.0 * (level - 1.0) ** 2 - 1.0))
            if level > 1
            else 0.0
        )
        value = np.where(order < level, alpha * (cosv * now - beta * before), 0.0)
        value[level] = start[level]
        table[:, level, :] = value.astype(np.float32).astype(ml_dtypes.bfloat16)
        before, now = now, value
    return table


def quadrature(nlat, nlon):
    theta = math.pi * (np.arange(nlat) + 0.5) / nlat
    return (math.pi / nlat * np.sin(theta) * (2.0 * math.pi / nlon)).astype(np.float32)


def fourier_tables(nlon, modes, lat_count):
    phase = np.arange(nlon)[:, None] * np.arange(modes)[None, :] % nlon
    angle = 2.0 * math.pi / nlon * phase
    cosine = np.cos(angle).astype(np.float32).astype(ml_dtypes.bfloat16)
    sine = np.sin(angle).astype(np.float32).astype(ml_dtypes.bfloat16)
    pair = np.stack([cosine, -sine]).reshape(2, nlon, modes // lat_count, lat_count)
    plain = pair.transpose(1, 2, 0, 3).reshape(nlon, 2 * modes)
    factor = np.where(np.arange(modes) == 0, 1.0, 2.0).astype(np.float32)
    doubled = np.stack([cosine, -sine]).astype(np.float32) * factor
    doubled = doubled.astype(ml_dtypes.bfloat16).reshape(2, nlon, modes // lat_count, lat_count)
    doubled = doubled.transpose(1, 2, 0, 3).reshape(nlon, 2 * modes)
    return plain, doubled


def gelu_parts(values):
    half = 0.5 * (1.0 + lax.erf(values * (1.0 / math.sqrt(2.0))))
    slope = half + values * jnp.exp(-0.5 * values * values) * (1.0 / math.sqrt(2.0 * math.pi))
    return values * half, slope


def swap_blocks(values, axis):
    return lax.all_to_all(values, axis, split_axis=0, concat_axis=0, tiled=True)


def lon_exchange(blocks, lon_index, lon_count):
    doubled = jnp.concatenate([blocks, blocks])
    moved = [lax.dynamic_index_in_dim(blocks, lon_index, 0, keepdims=False)]
    for shift in range(1, lon_count):
        block = lax.dynamic_index_in_dim(doubled, lon_index + shift, 0, keepdims=False)
        pairs = [(i, (i + shift) % lon_count) for i in range(lon_count)]
        moved.append(lax.ppermute(block, "lon", pairs))
    backwards = jnp.stack(moved[::-1] * 2)
    first = lon_count - 1 - lon_index
    return lax.dynamic_slice_in_dim(backwards, first, lon_count, 0)


def halve(values, axis, index, mask, bit):
    size = lax.axis_size(axis)
    width = values.shape[-1] // 2
    high = (index >> bit) & 1 == 1
    keep = jnp.where(high, values[:, width:], values[:, :width])
    give = jnp.where(high, values[:, :width], values[:, width:]).astype(jnp.bfloat16)
    return keep, lax.ppermute(give, axis, [(i, i ^ mask) for i in range(size)])


def add_swapped(pair):
    keep, got = pair
    return keep + got.astype(jnp.float32)


def body(table_all, plain, doubled, quad, grid, cotangent, spectral_weight, w_in, w_out):
    lat_count = lax.axis_size("lat")
    lon_count = lax.axis_size("lon")
    lat_index = lax.axis_index("lat")
    lon_index = lax.axis_index("lon")
    rows, lon_rows, width = grid.shape
    quarter = width // lon_count
    total_lat = rows * lat_count
    total_lon = lon_rows * lon_count
    parts = 2 * rows
    packed = parts * quarter
    tables = lax.dynamic_index_in_dim(table_all, lat_index, 0, keepdims=False)
    local_quad = lax.dynamic_slice_in_dim(quad, lat_index * rows, rows)
    quad_lanes = jnp.repeat(local_quad, quarter)[None, :]
    first_half = (jnp.arange(packed) < packed // 2)[None, :]

    def lon_split(values):
        values = values.reshape(rows, lon_rows, lon_count, quarter).transpose(2, 1, 0, 3)
        got = swap_blocks(values.reshape(lon_count, lon_rows, rows * quarter), "lon")
        return got.reshape(total_lon, rows * quarter)

    def lon_merge(values):
        got = swap_blocks(values.reshape(lon_count, lon_rows, rows * quarter), "lon")
        got = got.reshape(lon_count, lon_rows, rows, quarter).transpose(2, 1, 0, 3)
        return got.reshape(rows * lon_rows, width)

    def to_fourier(values, matrix, scale):
        out = lax.dot_general(
            matrix, values, (((0,), (0,)), ((), ())), preferred_element_type=jnp.float32
        )
        if scale is not None:
            out = out * scale
        out = out.astype(jnp.bfloat16).reshape(parts, lat_count, rows, quarter)
        return out.transpose(1, 2, 0, 3).reshape(lat_count, rows, packed)

    def from_fourier(values, matrix, scale):
        values = values.reshape(lat_count, rows, parts, quarter).transpose(2, 0, 1, 3)
        values = values.reshape(parts * lat_count, rows * quarter)
        out = jnp.dot(matrix, values, preferred_element_type=jnp.float32)
        if scale is not None:
            out = out * scale
        return out.astype(jnp.bfloat16)

    def analyze(values):
        values = values.reshape(total_lat, packed)
        low = jnp.dot(tables[0], values, preferred_element_type=jnp.float32)
        high = jnp.dot(tables[1], values, preferred_element_type=jnp.float32)
        out = jnp.where(first_half, low, high).astype(jnp.bfloat16)
        return out.reshape(lat_count, rows, packed)

    def synthesize(values):
        values = values.reshape(total_lat, packed)
        dims = (((0,), (0,)), ((), ()))
        low = lax.dot_general(tables[0], values, dims, preferred_element_type=jnp.float32)
        high = lax.dot_general(tables[1], values, dims, preferred_element_type=jnp.float32)
        out = jnp.where(first_half, low, high).astype(jnp.bfloat16)
        return out.reshape(lat_count, rows, packed)

    def block_weights(weights):
        w_re, w_im = weights[:, 0], weights[:, 1]
        top = jnp.concatenate([w_re, w_im], axis=3)
        low = jnp.concatenate([-w_im, w_re], axis=3)
        one = jnp.concatenate([top, low], axis=2)
        zero = jnp.zeros_like(one)
        return jnp.concatenate(
            [jnp.concatenate([one, zero], axis=3), jnp.concatenate([zero, one], axis=3)], axis=2
        )

    with jax.named_scope("weights"):
        by_input = spectral_weight.reshape(2, rows, lon_count, quarter, quarter)
        by_input = by_input.transpose(2, 0, 1, 3, 4)
        mix_weights = block_weights(by_input)
        unmix_weights = block_weights(lon_exchange(by_input, lon_index, lon_count))
    with jax.named_scope("forward_analysis"):
        spread = lon_split(grid)
        four = to_fourier(spread, plain, quad_lanes)
        spectrum = swap_blocks(analyze(swap_blocks(four, "lat")), "lat")
    with jax.named_scope("mix"):
        piece = lax.all_gather(spectrum, "lon", axis=0)
        mixed = jnp.einsum(
            "xplk,xlkn->pln", piece, mix_weights, preferred_element_type=jnp.float32
        ).astype(jnp.bfloat16)
    with jax.named_scope("forward_synthesis"):
        fields = swap_blocks(synthesize(swap_blocks(mixed, "lat")), "lat")
        wave_rows = lon_merge(from_fourier(fields, doubled, None))
    with jax.named_scope("pointwise"):
        flat_grid = grid.reshape(-1, width)
        hidden = (flat_grid.astype(jnp.float32) + wave_rows.astype(jnp.float32)).astype(
            jnp.bfloat16
        )
        back = cotangent.reshape(-1, width)
        act_grad = lax.dot_general(
            back, w_out, (((1,), (1,)), ((), ())), preferred_element_type=jnp.float32
        )
        pre = jnp.dot(hidden, w_in, preferred_element_type=jnp.float32)
        value, slope = gelu_parts(pre)
        act = value.astype(jnp.bfloat16)
        pre_grad = (act_grad * slope).astype(jnp.bfloat16)
        hidden_grad = (
            back.astype(jnp.float32)
            + lax.dot_general(
                pre_grad, w_in, (((1,), (1,)), ((), ())), preferred_element_type=jnp.float32
            )
        ).astype(jnp.bfloat16)
        block_output = (
            hidden.astype(jnp.float32) + jnp.dot(act, w_out, preferred_element_type=jnp.float32)
        ).astype(jnp.bfloat16)
    with jax.named_scope("backward_analysis"):
        grad_spread = lon_split(hidden_grad.reshape(grid.shape))
        field_grad = to_fourier(grad_spread, doubled, None)
        field_grad, hidden, pre_grad, act = lax.optimization_barrier(
            (field_grad, hidden, pre_grad, act)
        )
        field_grad = swap_blocks(field_grad, "lat")
    with jax.named_scope("pointwise_weights"):
        over_rows = (((0,), (0,)), ((), ()))
        out_part = lax.dot_general(act, back, over_rows, preferred_element_type=jnp.float32)
        in_part = lax.dot_general(hidden, pre_grad, over_rows, preferred_element_type=jnp.float32)
        in_part = in_part.reshape(out_part.shape)
        even = lat_index % 2 == 0
        keep = jnp.where(even, in_part, out_part)
        give = jnp.where(even, out_part, in_part).astype(jnp.bfloat16)
        got = lax.ppermute(give, "lat", [(i, i ^ 1) for i in range(lat_count)])
        sums = add_swapped((keep, got)).reshape(lat_count, -1)
        sums = halve(sums, "lon", lon_index, 3, 1)
    with jax.named_scope("backward_analysis"):
        field_grad, keep = lax.optimization_barrier((field_grad, sums[0]))
        mixed_grad = analyze(field_grad)
        mixed_grad, keep, got = lax.optimization_barrier((mixed_grad, keep, sums[1]))
        mixed_grad = swap_blocks(mixed_grad, "lat")
    with jax.named_scope("pointwise_weights"):
        sums = halve(add_swapped((keep, got)), "lon", lon_index, 1, 0)
        sums = halve(add_swapped(sums), "lat", lat_index, 6, 2)
    with jax.named_scope("backward_analysis"):
        mixed_grad, keep = lax.optimization_barrier((mixed_grad, sums[0]))
        wait = sums[1]
    with jax.named_scope("unmix"):
        piece = lax.all_gather(mixed_grad, "lon", axis=0)
        spectrum_grad = jnp.einsum(
            "xplk,xlnk->pln", piece, unmix_weights, preferred_element_type=jnp.float32
        ).astype(jnp.bfloat16)
        outer = jnp.einsum("pln,xplk->xlnk", spectrum, piece, preferred_element_type=jnp.float32)
        half = packed // 2
        outer = outer[:, :, :half, :half] + outer[:, :, half:, half:]
        grad_re = outer[:, :, :quarter, :quarter] + outer[:, :, quarter:, quarter:]
        grad_im = outer[:, :, :quarter, quarter:] - outer[:, :, quarter:, :quarter]
        grad_spectral = jnp.stack([grad_re, grad_im]).transpose(0, 2, 3, 1, 4)
        grad_spectral = grad_spectral.reshape(2, rows, quarter, width)
    with jax.named_scope("backward_synthesis"):
        spectrum_grad, keep, got = lax.optimization_barrier((spectrum_grad, keep, wait))
        spectrum_grad = swap_blocks(spectrum_grad, "lat")
        sums = halve(add_swapped((keep, got)), "lat", lat_index, 2, 1)
        chunk = sums[0].shape[1]
        room = -(-chunk // (rows * 128)) * rows * 128
        extra = jnp.pad(add_swapped(sums).astype(jnp.bfloat16), ((0, 0), (0, room - chunk)))
        spectrum_grad, extra = lax.optimization_barrier((spectrum_grad, extra))
        four_grad = synthesize(spectrum_grad)
        extra = extra.reshape(lat_count, rows, room // rows)
        got = swap_blocks(jnp.concatenate([four_grad, extra], axis=2), "lat")
        sums = got[:, :, packed:].reshape(lat_count // 8, 4, 2, room)[..., :chunk]
        sums = jnp.sum(sums.astype(jnp.float32), axis=0).swapaxes(0, 1).reshape(2, -1)
        wave_grad = lon_merge(from_fourier(got[:, :, :packed], plain, quad_lanes))
        grad_input = (hidden_grad.astype(jnp.float32) + wave_grad.astype(jnp.float32)).astype(
            jnp.bfloat16
        )
    return (
        block_output.reshape(grid.shape),
        grad_input.reshape(grid.shape),
        grad_spectral,
        sums[0],
        sums[1],
    )


def solution(mesh):
    in_specs = (P("lat", "lon", None), P("lat", "lon", None), P(None, "lat", None, "lon"), P(), P())
    out_specs = (
        P("lat", "lon", None),
        P("lat", "lon", None),
        P(None, "lat", "lon", None),
        P(("lat", "lon")),
        P(("lat", "lon")),
    )
    lat_count = mesh.shape["lat"]

    def call(grid, cotangent, spectral_weight, w_in, w_out):
        nlat, nlon, _ = grid.shape
        table = legendre_table(nlat).reshape(nlat // lat_count, lat_count, nlat, nlat)
        table = np.ascontiguousarray(table.swapaxes(0, 1))
        plain, doubled = fourier_tables(nlon, nlat, lat_count)
        quad = quadrature(nlat, nlon)
        mapped = jax.shard_map(
            body,
            mesh=mesh,
            in_specs=(P(), P(), P(), P()) + in_specs,
            out_specs=out_specs,
            check_vma=False,
        )
        return mapped(table, plain, doubled, quad, grid, cotangent, spectral_weight, w_in, w_out)

    return call
```

```python
import math

import jax
import jax.numpy as jnp
import ml_dtypes
import numpy as np
from jax import lax
from jax.sharding import PartitionSpec as P


def legendre_table(size):
    theta = math.pi * (np.arange(size) + 0.5) / size
    cosv, sinv = np.cos(theta), np.sin(theta)
    order = np.arange(size, dtype=np.float64)[:, None]
    start = np.empty((size, size))
    start[0] = math.sqrt(1.0 / (4.0 * math.pi))
    for m in range(1, size):
        start[m] = start[m - 1] * math.sqrt((2 * m + 1) / (2.0 * m)) * sinv
    table = np.zeros((size, size, size), dtype=ml_dtypes.bfloat16)
    before = np.zeros((size, size))
    now = np.zeros((size, size))
    for level in range(size):
        safe = np.where(order < level, order, 0.0)
        alpha = np.sqrt((4.0 * level * level - 1.0) / (level * level - safe * safe)) if level else 0.0
        beta = (
            np.sqrt(((level - 1.0) ** 2 - safe * safe).clip(0) / (4.0 * (level - 1.0) ** 2 - 1.0))
            if level > 1
            else 0.0
        )
        value = np.where(order < level, alpha * (cosv * now - beta * before), 0.0)
        value[level] = start[level]
        table[:, level, :] = value.astype(np.float32).astype(ml_dtypes.bfloat16)
        before, now = now, value
    return table


def quadrature(nlat, nlon):
    theta = math.pi * (np.arange(nlat) + 0.5) / nlat
    return (math.pi / nlat * np.sin(theta) * (2.0 * math.pi / nlon)).astype(np.float32)


def fourier_tables(nlon, modes, lon_count):
    phase = np.arange(nlon)[:, None] * np.arange(modes)[None, :] % nlon
    angle = 2.0 * math.pi / nlon * phase
    pair = np.stack([np.cos(angle), -np.sin(angle)]).astype(np.float32).astype(ml_dtypes.bfloat16)
    factor = np.where(np.arange(modes) == 0, 1.0, 2.0).astype(np.float32)
    doubled = (pair.astype(np.float32) * factor).astype(ml_dtypes.bfloat16)

    def arrange(values):
        values = values.reshape(2, nlon, lon_count, modes // lon_count).transpose(2, 1, 0, 3)
        return np.ascontiguousarray(values.reshape(lon_count, nlon, -1))

    return arrange(pair), arrange(doubled)


def gelu_parts(values):
    half = 0.5 * (1.0 + lax.erf(values * (1.0 / math.sqrt(2.0))))
    slope = half + values * jnp.exp(-0.5 * values * values) * (1.0 / math.sqrt(2.0 * math.pi))
    return values * half, slope


def swap_blocks(values, axis):
    return lax.all_to_all(values, axis, split_axis=0, concat_axis=0, tiled=True)


def lon_gather_async(block, lon_index, lon_count):
    moved = [block]
    for shift in range(1, lon_count):
        pairs = [(i, (i + shift) % lon_count) for i in range(lon_count)]
        moved.append(lax.ppermute(block, "lon", pairs))
    backwards = jnp.stack(moved[::-1] + moved[:0:-1])
    return lax.dynamic_slice_in_dim(backwards, lon_count - 1 - lon_index, lon_count, 0)


def halve(values, axis, index, mask, bit):
    size = lax.axis_size(axis)
    width = values.shape[-1] // 2
    high = (index >> bit) & 1 == 1
    keep = jnp.where(high, values[:, width:], values[:, :width])
    give = jnp.where(high, values[:, :width], values[:, width:]).astype(jnp.bfloat16)
    return keep, lax.ppermute(give, axis, [(i, i ^ mask) for i in range(size)])


def add_swapped(pair):
    keep, got = pair
    return keep + got.astype(jnp.float32)


def body(table_all, plain_all, doubled_all, quad, grid, cotangent, spectral_weight, w_in, w_out):
    lat_count = lax.axis_size("lat")
    lon_count = lax.axis_size("lon")
    lat_index = lax.axis_index("lat")
    lon_index = lax.axis_index("lon")
    rows, lon_rows, width = grid.shape
    quarter = width // lon_count
    total_lat = rows * lat_count
    total_lon = lon_rows * lon_count
    half = lat_count // 2
    order = lon_index * half + lat_index % half
    table = lax.dynamic_index_in_dim(table_all, order, 0, keepdims=False)
    plain = lax.dynamic_index_in_dim(plain_all, lon_index, 0, keepdims=False)
    doubled = lax.dynamic_index_in_dim(doubled_all, lon_index, 0, keepdims=False)
    local_quad = lax.dynamic_slice_in_dim(quad, lat_index * rows, rows)
    quad_lanes = jnp.repeat(local_quad, width)[None, :]

    def lon_gather(values):
        values = values.transpose(1, 0, 2).reshape(lon_rows, rows * width)
        return lax.all_gather(values, "lon", axis=0, tiled=True)

    def to_fourier(values, matrix, scale):
        out = lax.dot_general(
            matrix, values, (((0,), (0,)), ((), ())), preferred_element_type=jnp.float32
        )
        if scale is not None:
            out = out * scale
        return out.astype(jnp.bfloat16).reshape(lat_count, rows, width)

    def from_fourier(values, matrix, scale):
        values = values.reshape(lat_count, rows * width)
        out = jnp.dot(matrix, values, preferred_element_type=jnp.float32)
        if scale is not None:
            out = out * scale
        out = out.astype(jnp.bfloat16).reshape(lon_count, lon_rows, rows * width)
        out = jnp.sum(swap_blocks(out, "lon").astype(jnp.float32), axis=0)
        return out.reshape(lon_rows, rows, width).transpose(1, 0, 2).reshape(-1, width)

    def analyze(values):
        out = jnp.dot(table, values.reshape(total_lat, width), preferred_element_type=jnp.float32)
        return out.astype(jnp.bfloat16).reshape(lat_count, rows, width)

    def synthesize(values):
        out = lax.dot_general(
            table,
            values.reshape(total_lat, width),
            (((0,), (0,)), ((), ())),
            preferred_element_type=jnp.float32,
        )
        return out.astype(jnp.bfloat16).reshape(lat_count, rows, width)

    def complex_product(values, weights, sign):
        out = jnp.einsum("plc,lcn->pln", values, weights, preferred_element_type=jnp.float32)
        by_re, by_im = out[:, :, :width], out[:, :, width:]
        out_re = by_re[:half] + sign * by_im[half:]
        out_im = by_re[half:] - sign * by_im[:half]
        return jnp.concatenate([out_re, out_im]).astype(jnp.bfloat16)

    with jax.named_scope("forward_analysis"):
        four = to_fourier(lon_gather(grid), plain, quad_lanes)
        four, own_weight = lax.optimization_barrier((four, spectral_weight))
        four = swap_blocks(four, "lat")
    with jax.named_scope("weights"):
        weights = lon_gather_async(own_weight, lon_index, lon_count)
        mix_weights = weights.transpose(2, 3, 1, 0, 4).reshape(rows, width, 2 * width)
        unmix_weights = weights.transpose(2, 0, 4, 1, 3).reshape(rows, width, 2 * width)
    with jax.named_scope("forward_analysis"):
        spectrum = swap_blocks(analyze(four), "lat")
    with jax.named_scope("mix"):
        mixed = complex_product(spectrum, mix_weights, -1.0)
    with jax.named_scope("forward_synthesis"):
        fields = swap_blocks(synthesize(swap_blocks(mixed, "lat")), "lat")
        wave_rows = from_fourier(fields, doubled, None)
    with jax.named_scope("pointwise"):
        hidden = (grid.reshape(-1, width).astype(jnp.float32) + wave_rows).astype(jnp.bfloat16)
        back = cotangent.reshape(-1, width)
        act_grad = lax.dot_general(
            back, w_out, (((1,), (1,)), ((), ())), preferred_element_type=jnp.float32
        )
        pre = jnp.dot(hidden, w_in, preferred_element_type=jnp.float32)
        value, slope = gelu_parts(pre)
        act = value.astype(jnp.bfloat16)
        pre_grad = (act_grad * slope).astype(jnp.bfloat16)
        hidden_grad = (
            back.astype(jnp.float32)
            + lax.dot_general(
                pre_grad, w_in, (((1,), (1,)), ((), ())), preferred_element_type=jnp.float32
            )
        ).astype(jnp.bfloat16)
        block_output = (
            hidden.astype(jnp.float32) + jnp.dot(act, w_out, preferred_element_type=jnp.float32)
        ).astype(jnp.bfloat16)
    with jax.named_scope("backward_analysis"):
        gathered = lon_gather(hidden_grad.reshape(grid.shape))
        gathered, hidden, pre_grad, act = lax.optimization_barrier(
            (gathered, hidden, pre_grad, act)
        )
        field_grad = swap_blocks(to_fourier(gathered, doubled, None), "lat")
    with jax.named_scope("pointwise_weights"):
        over_rows = (((0,), (0,)), ((), ()))
        out_part = lax.dot_general(act, back, over_rows, preferred_element_type=jnp.float32)
        in_part = lax.dot_general(hidden, pre_grad, over_rows, preferred_element_type=jnp.float32)
        in_part = in_part.reshape(out_part.shape)
        even = lat_index % 2 == 0
        keep = jnp.where(even, in_part, out_part)
        give = jnp.where(even, out_part, in_part).astype(jnp.bfloat16)
        got = lax.ppermute(give, "lat", [(i, i ^ 1) for i in range(lat_count)])
    with jax.named_scope("backward_analysis"):
        mixed_grad = analyze(field_grad)
        mixed_grad, keep, got = lax.optimization_barrier((mixed_grad, keep, got))
        mixed_grad = swap_blocks(mixed_grad, "lat")
    with jax.named_scope("pointwise_weights"):
        sums = add_swapped((keep, got)).reshape(lat_count, -1)
        keep, got = halve(sums, "lon", lon_index, 3, 1)
    with jax.named_scope("unmix"):
        spectrum_grad = complex_product(mixed_grad, unmix_weights, 1.0)
        spectrum_grad, keep, got, left, right = lax.optimization_barrier(
            (spectrum_grad, keep, got, spectrum, mixed_grad)
        )
    with jax.named_scope("backward_synthesis"):
        spectrum_grad = swap_blocks(spectrum_grad, "lat")
    with jax.named_scope("pointwise_weights"):
        keep, got = halve(add_swapped((keep, got)), "lon", lon_index, 1, 0)
    with jax.named_scope("unmix"):
        turned = jnp.concatenate([right[half:], -right[:half]])
        right = jnp.stack([right, turned])
        high = lon_index >> 1 == 1
        low_rows, high_rows = left[..., : width // 2], left[..., width // 2 :]
        outer = "pli,rpld->rlid"
        spec_keep = jnp.einsum(
            outer,
            jnp.where(high, high_rows, low_rows),
            right,
            preferred_element_type=jnp.float32,
        )
        spec_give = jnp.einsum(
            outer,
            jnp.where(high, low_rows, high_rows),
            right,
            preferred_element_type=jnp.float32,
        ).astype(jnp.bfloat16)
        spec_got = lax.ppermute(
            spec_give, "lon", [(i, lon_count - 1 - i) for i in range(lon_count)]
        )
    with jax.named_scope("backward_synthesis"):
        four_grad = synthesize(spectrum_grad)
        chunk = keep.shape[1]
        room = -(-chunk // (rows * 128)) * rows * 128
        extra = jnp.pad(add_swapped((keep, got)).astype(jnp.bfloat16), ((0, 0), (0, room - chunk)))
        extra = extra.reshape(lat_count, rows, room // rows)
        four_grad = jnp.concatenate([four_grad, extra], axis=2)
        four_grad, spec_keep, spec_got = lax.optimization_barrier((four_grad, spec_keep, spec_got))
        four_grad = swap_blocks(four_grad, "lat")
        wave_grad = from_fourier(four_grad[:, :, :width], plain, quad_lanes)
        grad_input = (hidden_grad.astype(jnp.float32) + wave_grad).astype(jnp.bfloat16)
    with jax.named_scope("unmix"):
        total = spec_keep + spec_got.astype(jnp.float32)
        high = lon_index & 1 == 1
        low_rows, high_rows = total[:, :, :quarter], total[:, :, quarter:]
        spec_give = jnp.where(high, low_rows, high_rows).astype(jnp.bfloat16)
        spec_got = lax.ppermute(spec_give, "lon", [(i, i ^ 1) for i in range(lon_count)])
        grad_spectral = jnp.where(high, high_rows, low_rows) + spec_got.astype(jnp.float32)
    with jax.named_scope("pointwise_weights"):
        sums = four_grad[:, :, width:].reshape(half, 2, room)[:, :, :chunk]
        sums = jnp.sum(sums.astype(jnp.float32), axis=0)
    return (
        block_output.reshape(grid.shape),
        grad_input.reshape(grid.shape),
        grad_spectral,
        sums[0],
        sums[1],
    )


def solution(mesh):
    in_specs = (P("lat", "lon", None), P("lat", "lon", None), P(None, "lat", None, "lon"), P(), P())
    out_specs = (
        P("lat", "lon", None),
        P("lat", "lon", None),
        P(None, "lat", "lon", None),
        P(("lat", "lon")),
        P(("lat", "lon")),
    )

    def call(grid, cotangent, spectral_weight, w_in, w_out):
        nlat, nlon, _ = grid.shape
        table = legendre_table(nlat)
        plain, doubled = fourier_tables(nlon, nlat, mesh.shape["lon"])
        quad = quadrature(nlat, nlon)
        mapped = jax.shard_map(
            body,
            mesh=mesh,
            in_specs=(P(), P(), P(), P()) + in_specs,
            out_specs=out_specs,
            check_vma=False,
        )
        return mapped(table, plain, doubled, quad, grid, cotangent, spectral_weight, w_in, w_out)

    return call
```

```python
import math

import jax
import jax.numpy as jnp
import ml_dtypes
import numpy as np
from jax import lax
from jax.sharding import PartitionSpec as P


def legendre_table(size):
    theta = math.pi * (np.arange(size) + 0.5) / size
    cosv, sinv = np.cos(theta), np.sin(theta)
    order = np.arange(size, dtype=np.float64)[:, None]
    start = np.empty((size, size))
    start[0] = math.sqrt(1.0 / (4.0 * math.pi))
    for m in range(1, size):
        start[m] = start[m - 1] * math.sqrt((2 * m + 1) / (2.0 * m)) * sinv
    table = np.zeros((size, size, size), dtype=ml_dtypes.bfloat16)
    before = np.zeros((size, size))
    now = np.zeros((size, size))
    for level in range(size):
        safe = np.where(order < level, order, 0.0)
        alpha = np.sqrt((4.0 * level * level - 1.0) / (level * level - safe * safe)) if level else 0.0
        beta = (
            np.sqrt(((level - 1.0) ** 2 - safe * safe).clip(0) / (4.0 * (level - 1.0) ** 2 - 1.0))
            if level > 1
            else 0.0
        )
        value = np.where(order < level, alpha * (cosv * now - beta * before), 0.0)
        value[level] = start[level]
        table[:, level, :] = value.astype(np.float32).astype(ml_dtypes.bfloat16)
        before, now = now, value
    return table


def quadrature(nlat, nlon):
    theta = math.pi * (np.arange(nlat) + 0.5) / nlat
    return (math.pi / nlat * np.sin(theta) * (2.0 * math.pi / nlon)).astype(np.float32)


def fourier_tables(nlon, modes, lon_count):
    phase = np.arange(nlon)[:, None] * np.arange(modes)[None, :] % nlon
    angle = 2.0 * math.pi / nlon * phase
    pair = np.stack([np.cos(angle), -np.sin(angle)]).astype(np.float32).astype(ml_dtypes.bfloat16)
    factor = np.where(np.arange(modes) == 0, 1.0, 2.0).astype(np.float32)
    doubled = (pair.astype(np.float32) * factor).astype(ml_dtypes.bfloat16)

    def arrange(values):
        values = values.reshape(2, nlon, lon_count, modes // lon_count).transpose(2, 1, 0, 3)
        return np.ascontiguousarray(values.reshape(lon_count, nlon, -1))

    return arrange(pair), arrange(doubled)


def gelu_parts(values):
    half = 0.5 * (1.0 + lax.erf(values * (1.0 / math.sqrt(2.0))))
    slope = half + values * jnp.exp(-0.5 * values * values) * (1.0 / math.sqrt(2.0 * math.pi))
    return values * half, slope


def swap_blocks(values, axis):
    return lax.all_to_all(values, axis, split_axis=0, concat_axis=0, tiled=True)


def lon_sends(block, lon_count):
    moved = [block]
    for shift in range(1, lon_count):
        pairs = [(i, (i + shift) % lon_count) for i in range(lon_count)]
        moved.append(lax.ppermute(block, "lon", pairs))
    return moved


def in_order(moved, lon_index):
    backwards = jnp.stack(moved[::-1] + moved[:0:-1])
    return lax.dynamic_slice_in_dim(backwards, len(moved) - 1 - lon_index, len(moved), 0)


def scatter_sum(values, axis, index, count, shifted):
    chunk = values.shape[-1] // count
    narrow = values.astype(jnp.bfloat16)
    parts = [lax.dynamic_slice_in_dim(values, index * chunk, chunk, axis=1)]
    for shift in range(1, count):
        to = (index + shift) % count
        block = lax.dynamic_slice_in_dim(narrow, to * chunk, chunk, axis=1)
        parts.append(lax.ppermute(block, axis, shifted(shift)))
    return parts


def add_parts(parts):
    total = parts[0]
    for part in parts[1:]:
        total = total + part.astype(jnp.float32)
    return total


def body(table_all, plain_all, doubled_all, quad, grid, cotangent, spectral_weight, w_in, w_out):
    lat_count = lax.axis_size("lat")
    lon_count = lax.axis_size("lon")
    lat_index = lax.axis_index("lat")
    lon_index = lax.axis_index("lon")
    rows, lon_rows, width = grid.shape
    quarter = width // lon_count
    total_lat = rows * lat_count
    total_lon = lon_rows * lon_count
    half = lat_count // 2
    order = lon_index * half + lat_index % half
    table = lax.dynamic_index_in_dim(table_all, order, 0, keepdims=False)
    plain = lax.dynamic_index_in_dim(plain_all, lon_index, 0, keepdims=False)
    doubled = lax.dynamic_index_in_dim(doubled_all, lon_index, 0, keepdims=False)
    local_quad = lax.dynamic_slice_in_dim(quad, lat_index * rows, rows)
    quad_lanes = jnp.repeat(local_quad, width)[None, :]

    def lon_gather(values):
        values = values.transpose(1, 0, 2).reshape(lon_rows, rows * width)
        return lax.all_gather(values, "lon", axis=0, tiled=True)

    def to_fourier(values, matrix, scale):
        out = lax.dot_general(
            matrix, values, (((0,), (0,)), ((), ())), preferred_element_type=jnp.float32
        )
        if scale is not None:
            out = out * scale
        return out.astype(jnp.bfloat16).reshape(lat_count, rows, width)

    def from_fourier(values, matrix, scale):
        values = values.reshape(lat_count, rows * width)
        out = jnp.dot(matrix, values, preferred_element_type=jnp.float32)
        if scale is not None:
            out = out * scale
        out = out.astype(jnp.bfloat16).reshape(lon_count, lon_rows, rows * width)
        out = jnp.sum(swap_blocks(out, "lon").astype(jnp.float32), axis=0)
        return out.reshape(lon_rows, rows, width).transpose(1, 0, 2).reshape(-1, width)

    def analyze(values):
        out = jnp.dot(table, values.reshape(total_lat, width), preferred_element_type=jnp.float32)
        return out.astype(jnp.bfloat16).reshape(lat_count, rows, width)

    def synthesize(values):
        out = lax.dot_general(
            table,
            values.reshape(total_lat, width),
            (((0,), (0,)), ((), ())),
            preferred_element_type=jnp.float32,
        )
        return out.astype(jnp.bfloat16).reshape(lat_count, rows, width)

    def complex_product(values, weights, sign):
        out = jnp.einsum("plc,lcn->pln", values, weights, preferred_element_type=jnp.float32)
        by_re, by_im = out[:, :, :width], out[:, :, width:]
        out_re = by_re[:half] + sign * by_im[half:]
        out_im = by_re[half:] - sign * by_im[:half]
        return jnp.concatenate([out_re, out_im]).astype(jnp.bfloat16)

    with jax.named_scope("forward_analysis"):
        four = to_fourier(lon_gather(grid), plain, quad_lanes)
        four = analyze(swap_blocks(four, "lat"))
        four, *moved = lax.optimization_barrier((four, *lon_sends(spectral_weight, lon_count)))
    with jax.named_scope("weights"):
        weights = in_order(moved, lon_index)
        mix_weights = weights.transpose(2, 3, 1, 0, 4).reshape(rows, width, 2 * width)
        unmix_weights = weights.transpose(2, 0, 4, 1, 3).reshape(rows, width, 2 * width)
    with jax.named_scope("forward_analysis"):
        spectrum = swap_blocks(four, "lat")
    with jax.named_scope("mix"):
        mixed = complex_product(spectrum, mix_weights, -1.0)
    with jax.named_scope("forward_synthesis"):
        fields = swap_blocks(synthesize(swap_blocks(mixed, "lat")), "lat")
        wave_rows = from_fourier(fields, doubled, None)
    with jax.named_scope("pointwise"):
        hidden = (grid.reshape(-1, width).astype(jnp.float32) + wave_rows).astype(jnp.bfloat16)
        back = cotangent.reshape(-1, width)
        act_grad = lax.dot_general(
            back, w_out, (((1,), (1,)), ((), ())), preferred_element_type=jnp.float32
        )
        pre = jnp.dot(hidden, w_in, preferred_element_type=jnp.float32)
        value, slope = gelu_parts(pre)
        act = value.astype(jnp.bfloat16)
        pre_grad = (act_grad * slope).astype(jnp.bfloat16)
        hidden_grad = (
            back.astype(jnp.float32)
            + lax.dot_general(
                pre_grad, w_in, (((1,), (1,)), ((), ())), preferred_element_type=jnp.float32
            )
        ).astype(jnp.bfloat16)
        block_output = (
            hidden.astype(jnp.float32) + jnp.dot(act, w_out, preferred_element_type=jnp.float32)
        ).astype(jnp.bfloat16)
    with jax.named_scope("backward_analysis"):
        gathered = lon_gather(hidden_grad.reshape(grid.shape))
        gathered, hidden, pre_grad, act = lax.optimization_barrier(
            (gathered, hidden, pre_grad, act)
        )
        field_grad = swap_blocks(to_fourier(gathered, doubled, None), "lat")
    with jax.named_scope("pointwise_weights"):
        over_rows = (((0,), (0,)), ((), ()))
        out_part = lax.dot_general(act, back, over_rows, preferred_element_type=jnp.float32)
        in_part = lax.dot_general(hidden, pre_grad, over_rows, preferred_element_type=jnp.float32)
        in_part = in_part.reshape(out_part.shape)
        even = lat_index % 2 == 0
        keep = jnp.where(even, in_part, out_part)
        give = jnp.where(even, out_part, in_part).astype(jnp.bfloat16)
        got = lax.ppermute(give, "lat", [(i, i ^ 1) for i in range(lat_count)])
    with jax.named_scope("backward_analysis"):
        mixed_grad = analyze(field_grad)
        mixed_grad, keep, got = lax.optimization_barrier((mixed_grad, keep, got))
        mixed_grad = swap_blocks(mixed_grad, "lat")
    with jax.named_scope("pointwise_weights"):
        sums = add_parts([keep, got]).reshape(lat_count, -1)
        parts = scatter_sum(
            sums,
            "lon",
            lon_index,
            lon_count,
            lambda s: [(i, (i + s) % lon_count) for i in range(lon_count)],
        )
    with jax.named_scope("unmix"):
        spectrum_grad = complex_product(mixed_grad, unmix_weights, 1.0)
        spectrum_grad, left, right, *parts = lax.optimization_barrier(
            (spectrum_grad, spectrum, mixed_grad, *parts)
        )
    with jax.named_scope("backward_synthesis"):
        spectrum_grad = swap_blocks(spectrum_grad, "lat")
    with jax.named_scope("pointwise_weights"):
        parts = scatter_sum(
            add_parts(parts),
            "lat",
            (lat_index >> 1) & 3,
            4,
            lambda s: [(i, (i & ~6) | ((i + 2 * s) & 6)) for i in range(lat_count)],
        )
    with jax.named_scope("unmix"):
        turned = jnp.concatenate([right[half:], -right[:half]])
        right = jnp.stack([right, turned])
        high = lon_index >> 1 == 1
        low_rows, high_rows = left[..., : width // 2], left[..., width // 2 :]
        outer = "pli,rpld->rlid"
        spec_keep = jnp.einsum(
            outer,
            jnp.where(high, high_rows, low_rows),
            right,
            preferred_element_type=jnp.float32,
        )
        spec_give = jnp.einsum(
            outer,
            jnp.where(high, low_rows, high_rows),
            right,
            preferred_element_type=jnp.float32,
        ).astype(jnp.bfloat16)
        spec_got = lax.ppermute(
            spec_give, "lon", [(i, lon_count - 1 - i) for i in range(lon_count)]
        )
    with jax.named_scope("backward_synthesis"):
        four_grad = synthesize(spectrum_grad)
        extra = add_parts(parts).astype(jnp.bfloat16)
        chunk = extra.shape[1]
        room = -(-chunk // (rows * 128)) * rows * 128
        extra = jnp.pad(extra, ((0, 0), (0, room - chunk)))
        extra = extra.reshape(lat_count, rows, room // rows)
        four_grad = jnp.concatenate([four_grad, extra], axis=2)
        four_grad, spec_keep, spec_got = lax.optimization_barrier((four_grad, spec_keep, spec_got))
        four_grad = swap_blocks(four_grad, "lat")
        wave_grad = from_fourier(four_grad[:, :, :width], plain, quad_lanes)
        grad_input = (hidden_grad.astype(jnp.float32) + wave_grad).astype(jnp.bfloat16)
    with jax.named_scope("unmix"):
        total = spec_keep + spec_got.astype(jnp.float32)
        high = lon_index & 1 == 1
        low_rows, high_rows = total[:, :, :quarter], total[:, :, quarter:]
        spec_give = jnp.where(high, low_rows, high_rows).astype(jnp.bfloat16)
        spec_got = lax.ppermute(spec_give, "lon", [(i, i ^ 1) for i in range(lon_count)])
        grad_spectral = jnp.where(high, high_rows, low_rows) + spec_got.astype(jnp.float32)
    with jax.named_scope("pointwise_weights"):
        sums = four_grad[:, :, width:].reshape(lat_count // 8, 4, 2, room)[..., :chunk]
        sums = jnp.sum(sums.astype(jnp.float32), axis=0).swapaxes(0, 1).reshape(2, -1)
    return (
        block_output.reshape(grid.shape),
        grad_input.reshape(grid.shape),
        grad_spectral,
        sums[0],
        sums[1],
    )


def solution(mesh):
    in_specs = (P("lat", "lon", None), P("lat", "lon", None), P(None, "lat", None, "lon"), P(), P())
    out_specs = (
        P("lat", "lon", None),
        P("lat", "lon", None),
        P(None, "lat", "lon", None),
        P(("lat", "lon")),
        P(("lat", "lon")),
    )

    def call(grid, cotangent, spectral_weight, w_in, w_out):
        nlat, nlon, _ = grid.shape
        table = legendre_table(nlat)
        plain, doubled = fourier_tables(nlon, nlat, mesh.shape["lon"])
        quad = quadrature(nlat, nlon)
        mapped = jax.shard_map(
            body,
            mesh=mesh,
            in_specs=(P(), P(), P(), P()) + in_specs,
            out_specs=out_specs,
            check_vma=False,
        )
        return mapped(table, plain, doubled, quad, grid, cotangent, spectral_weight, w_in, w_out)

    return call
```

```python
import functools
import math

import jax
import jax.numpy as jnp
import ml_dtypes
import numpy as np
from jax import lax
from jax.experimental import pallas as pl
from jax.experimental.pallas import tpu as pltpu
from jax.sharding import PartitionSpec as P


def legendre_table(size):
    theta = math.pi * (np.arange(size) + 0.5) / size
    cosv, sinv = np.cos(theta), np.sin(theta)
    order = np.arange(size, dtype=np.float64)[:, None]
    start = np.empty((size, size))
    start[0] = math.sqrt(1.0 / (4.0 * math.pi))
    for m in range(1, size):
        start[m] = start[m - 1] * math.sqrt((2 * m + 1) / (2.0 * m)) * sinv
    table = np.zeros((size, size, size), dtype=ml_dtypes.bfloat16)
    before = np.zeros((size, size))
    now = np.zeros((size, size))
    for level in range(size):
        safe = np.where(order < level, order, 0.0)
        alpha = np.sqrt((4.0 * level * level - 1.0) / (level * level - safe * safe)) if level else 0.0
        beta = (
            np.sqrt(((level - 1.0) ** 2 - safe * safe).clip(0) / (4.0 * (level - 1.0) ** 2 - 1.0))
            if level > 1
            else 0.0
        )
        value = np.where(order < level, alpha * (cosv * now - beta * before), 0.0)
        value[level] = start[level]
        table[:, level, :] = value.astype(np.float32).astype(ml_dtypes.bfloat16)
        before, now = now, value
    return table


def quadrature(nlat, nlon):
    theta = math.pi * (np.arange(nlat) + 0.5) / nlat
    return (math.pi / nlat * np.sin(theta) * (2.0 * math.pi / nlon)).astype(np.float32)


def fourier_tables(nlon, modes, lon_count):
    phase = np.arange(nlon)[:, None] * np.arange(modes)[None, :] % nlon
    angle = 2.0 * math.pi / nlon * phase
    pair = np.stack([np.cos(angle), -np.sin(angle)]).astype(np.float32).astype(ml_dtypes.bfloat16)
    factor = np.where(np.arange(modes) == 0, 1.0, 2.0).astype(np.float32)
    doubled = (pair.astype(np.float32) * factor).astype(ml_dtypes.bfloat16)

    def arrange(values):
        values = values.reshape(2, nlon, lon_count, modes // lon_count).transpose(2, 1, 0, 3)
        return np.ascontiguousarray(values.reshape(lon_count, nlon, -1))

    return arrange(pair), arrange(doubled)


def gelu_parts(values):
    half = 0.5 * (1.0 + lax.erf(values * (1.0 / math.sqrt(2.0))))
    slope = half + values * jnp.exp(-0.5 * values * values) * (1.0 / math.sqrt(2.0 * math.pi))
    return values * half, slope


def swap_blocks(values, axis):
    return lax.all_to_all(values, axis, split_axis=0, concat_axis=0, tiled=True)


def fourier_kernel(rows, lon_rows, place_ref, matrix_ref, scale_ref, values_ref, out_ref):
    width = values_ref.shape[2]
    for row in range(rows):
        longitudes = values_ref[:, row * lon_rows : (row + 1) * lon_rows, :]
        out = jnp.dot(
            matrix_ref[0],
            longitudes.reshape(-1, width),
            preferred_element_type=jnp.float32,
        )
        lanes = slice(row * width, (row + 1) * width)
        out_ref[:, lanes] = (out * scale_ref[:, lanes]).astype(jnp.bfloat16)


def to_fourier(values, matrices, scale, lon_index, rows, lon_rows):
    lon_count, _, width = values.shape
    _, orders, longitudes = matrices.shape
    return pl.pallas_call(
        functools.partial(fourier_kernel, rows, lon_rows),
        grid_spec=pltpu.PrefetchScalarGridSpec(
            num_scalar_prefetch=1,
            grid=(1,),
            in_specs=[
                pl.BlockSpec((1, orders, longitudes), lambda i, place: (place[0], 0, 0)),
                pl.BlockSpec((1, rows * width), lambda i, place: (0, 0)),
                pl.BlockSpec((lon_count, rows * lon_rows, width), lambda i, place: (0, 0, 0)),
            ],
            out_specs=pl.BlockSpec((orders, rows * width), lambda i, place: (0, 0)),
        ),
        out_shape=jax.ShapeDtypeStruct((orders, rows * width), jnp.bfloat16),
        compiler_params=pltpu.CompilerParams(vmem_limit_bytes=16 * 1024 * 1024),
        cost_estimate=pl.CostEstimate(
            flops=2 * orders * longitudes * rows * width,
            bytes_accessed=2 * (longitudes + orders) * rows * width + 2 * orders * longitudes,
            transcendentals=0,
        ),
    )(lon_index.reshape(1).astype(jnp.int32), matrices, scale, values)


def scatter_sum(values, axis, index, count, shifted):
    chunk = values.shape[-1] // count
    narrow = values.astype(jnp.bfloat16)
    parts = [lax.dynamic_slice_in_dim(values, index * chunk, chunk, axis=1)]
    for shift in range(1, count):
        to = (index + shift) % count
        block = lax.dynamic_slice_in_dim(narrow, to * chunk, chunk, axis=1)
        parts.append(lax.ppermute(block, axis, shifted(shift)))
    return parts


def add_parts(parts):
    total = parts[0]
    for part in parts[1:]:
        total = total + part.astype(jnp.float32)
    return total


def body(table_all, plain_all, doubled_all, plain_t, doubled_t, quad, grid, cotangent, spectral_weight, w_in, w_out):
    lat_count = lax.axis_size("lat")
    lon_count = lax.axis_size("lon")
    lat_index = lax.axis_index("lat")
    lon_index = lax.axis_index("lon")
    rows, lon_rows, width = grid.shape
    quarter = width // lon_count
    total_lat = rows * lat_count
    total_lon = lon_rows * lon_count
    half = lat_count // 2
    order = lon_index * half + lat_index % half
    table = lax.dynamic_index_in_dim(table_all, order, 0, keepdims=False)
    plain = lax.dynamic_index_in_dim(plain_all, lon_index, 0, keepdims=False)
    doubled = lax.dynamic_index_in_dim(doubled_all, lon_index, 0, keepdims=False)
    local_quad = lax.dynamic_slice_in_dim(quad, lat_index * rows, rows)
    quad_lanes = jnp.repeat(local_quad, width)[None, :]

    def to_orders(values, matrices, scale):
        out = to_fourier(values, matrices, scale, lon_index, rows, lon_rows)
        return out.reshape(lat_count, rows, width)

    def from_fourier(values, matrix, scale):
        values = values.reshape(lat_count, rows * width)
        out = jnp.dot(matrix, values, preferred_element_type=jnp.float32)
        if scale is not None:
            out = out * scale
        out = out.astype(jnp.bfloat16).reshape(lon_count, lon_rows, rows * width)
        out = jnp.sum(swap_blocks(out, "lon").astype(jnp.float32), axis=0)
        return out.reshape(lon_rows, rows, width).transpose(1, 0, 2).reshape(-1, width)

    def analyze(values):
        out = jnp.dot(table, values.reshape(total_lat, width), preferred_element_type=jnp.float32)
        return out.astype(jnp.bfloat16).reshape(lat_count, rows, width)

    def synthesize(values):
        out = lax.dot_general(
            table,
            values.reshape(total_lat, width),
            (((0,), (0,)), ((), ())),
            preferred_element_type=jnp.float32,
        )
        return out.astype(jnp.bfloat16).reshape(lat_count, rows, width)

    def complex_product(values, dims, sign):
        by_re = jnp.einsum(dims, values, weights[0], preferred_element_type=jnp.float32)
        by_im = jnp.einsum(dims, values, weights[1], preferred_element_type=jnp.float32)
        out_re = by_re[:half] + sign * by_im[half:]
        out_im = by_re[half:] - sign * by_im[:half]
        return jnp.concatenate([out_re, out_im]).astype(jnp.bfloat16)

    with jax.named_scope("forward_analysis"):
        own_weight = spectral_weight.transpose(0, 1, 3, 2).reshape(-1, width)
        sent = jnp.concatenate([grid.reshape(-1, width), own_weight])
        gathered = lax.all_gather(sent, "lon", axis=0)
        four = swap_blocks(to_orders(gathered, plain_t, quad_lanes), "lat")
    with jax.named_scope("weights"):
        weights = gathered[:, rows * lon_rows :].reshape(lon_count, 2, rows, quarter, width)
        weights = weights.transpose(1, 2, 0, 3, 4).reshape(2, rows, width, width)
    with jax.named_scope("forward_analysis"):
        spectrum = swap_blocks(analyze(four), "lat")
    with jax.named_scope("mix"):
        mixed = complex_product(spectrum, "plc,ldc->pld", -1.0)
    with jax.named_scope("forward_synthesis"):
        fields = swap_blocks(synthesize(swap_blocks(mixed, "lat")), "lat")
        wave_rows = from_fourier(fields, doubled, None)
    with jax.named_scope("pointwise"):
        hidden = (grid.reshape(-1, width).astype(jnp.float32) + wave_rows).astype(jnp.bfloat16)
        back = cotangent.reshape(-1, width)
        act_grad = lax.dot_general(
            back, w_out, (((1,), (1,)), ((), ())), preferred_element_type=jnp.float32
        )
        pre = jnp.dot(hidden, w_in, preferred_element_type=jnp.float32)
        value, slope = gelu_parts(pre)
        act = value.astype(jnp.bfloat16)
        pre_grad = (act_grad * slope).astype(jnp.bfloat16)
        hidden_grad = (
            back.astype(jnp.float32)
            + lax.dot_general(
                pre_grad, w_in, (((1,), (1,)), ((), ())), preferred_element_type=jnp.float32
            )
        ).astype(jnp.bfloat16)
        block_output = (
            hidden.astype(jnp.float32) + jnp.dot(act, w_out, preferred_element_type=jnp.float32)
        ).astype(jnp.bfloat16)
    with jax.named_scope("backward_analysis"):
        gathered = lax.all_gather(hidden_grad, "lon", axis=0)
        gathered, hidden, pre_grad, act = lax.optimization_barrier(
            (gathered, hidden, pre_grad, act)
        )
        field_grad = swap_blocks(to_orders(gathered, doubled_t, jnp.ones_like(quad_lanes)), "lat")
    with jax.named_scope("pointwise_weights"):
        over_rows = (((0,), (0,)), ((), ()))
        out_part = lax.dot_general(act, back, over_rows, preferred_element_type=jnp.float32)
        in_part = lax.dot_general(hidden, pre_grad, over_rows, preferred_element_type=jnp.float32)
        in_part = in_part.reshape(out_part.shape)
        even = lat_index % 2 == 0
        keep = jnp.where(even, in_part, out_part)
        give = jnp.where(even, out_part, in_part).astype(jnp.bfloat16)
        got = lax.ppermute(give, "lat", [(i, i ^ 1) for i in range(lat_count)])
    with jax.named_scope("backward_analysis"):
        mixed_grad = analyze(field_grad)
        mixed_grad, keep, got = lax.optimization_barrier((mixed_grad, keep, got))
        mixed_grad = swap_blocks(mixed_grad, "lat")
    with jax.named_scope("pointwise_weights"):
        sums = add_parts([keep, got]).reshape(lat_count, -1)
        parts = scatter_sum(
            sums,
            "lon",
            lon_index,
            lon_count,
            lambda s: [(i, (i + s) % lon_count) for i in range(lon_count)],
        )
    with jax.named_scope("unmix"):
        spectrum_grad = complex_product(mixed_grad, "pld,ldc->plc", 1.0)
    with jax.named_scope("backward_synthesis"):
        spectrum_grad = swap_blocks(spectrum_grad, "lat")
    with jax.named_scope("pointwise_weights"):
        parts = scatter_sum(
            add_parts(parts),
            "lat",
            (lat_index >> 1) & 3,
            4,
            lambda s: [(i, (i & ~6) | ((i + 2 * s) & 6)) for i in range(lat_count)],
        )
    with jax.named_scope("backward_synthesis"):
        four_grad = synthesize(spectrum_grad)
        extra = add_parts(parts).astype(jnp.bfloat16)
        chunk = extra.shape[1]
        room = -(-chunk // (rows * 128)) * rows * 128
        extra = jnp.pad(extra, ((0, 0), (0, room - chunk)))
        extra = extra.reshape(lat_count, rows, room // rows)
        four_grad = jnp.concatenate([four_grad, extra], axis=2)
        four_grad, left, right = lax.optimization_barrier((four_grad, spectrum, mixed_grad))
        four_grad = swap_blocks(four_grad, "lat")
        wave_grad = from_fourier(four_grad[:, :, :width], plain, quad_lanes)
        grad_input = (hidden_grad.astype(jnp.float32) + wave_grad).astype(jnp.bfloat16)
    with jax.named_scope("unmix"):
        right = jnp.stack([right, jnp.concatenate([right[half:], -right[:half]])])
        outer = jnp.einsum("pli,rpld->rlid", left, right, preferred_element_type=jnp.float32)
        outer = outer.reshape(2, rows, lon_count, quarter, width)
        own = lax.dynamic_index_in_dim(outer, lon_index, 2, keepdims=False)
        narrow = outer.astype(jnp.bfloat16)
        grad_spectral = [own]
        for shift in range(1, lon_count):
            to = (lon_index + shift) % lon_count
            block = lax.dynamic_index_in_dim(narrow, to, 2, keepdims=False)
            pairs = [(i, (i + shift) % lon_count) for i in range(lon_count)]
            grad_spectral.append(lax.ppermute(block, "lon", pairs))
        grad_spectral = add_parts(grad_spectral)
    with jax.named_scope("pointwise_weights"):
        sums = four_grad[:, :, width:].reshape(lat_count // 8, 4, 2, room)[..., :chunk]
        sums = jnp.sum(sums.astype(jnp.float32), axis=0).swapaxes(0, 1).reshape(2, -1)
    return (
        block_output.reshape(grid.shape),
        grad_input.reshape(grid.shape),
        grad_spectral,
        sums[0],
        sums[1],
    )


def solution(mesh):
    in_specs = (P("lat", "lon", None), P("lat", "lon", None), P(None, "lat", None, "lon"), P(), P())
    out_specs = (
        P("lat", "lon", None),
        P("lat", "lon", None),
        P(None, "lat", "lon", None),
        P(("lat", "lon")),
        P(("lat", "lon")),
    )

    def call(grid, cotangent, spectral_weight, w_in, w_out):
        nlat, nlon, _ = grid.shape
        table = legendre_table(nlat)
        plain, doubled = fourier_tables(nlon, nlat, mesh.shape["lon"])
        plain_t = np.ascontiguousarray(plain.swapaxes(1, 2))
        doubled_t = np.ascontiguousarray(doubled.swapaxes(1, 2))
        quad = quadrature(nlat, nlon)
        mapped = jax.shard_map(
            body,
            mesh=mesh,
            in_specs=(P(),) * 6 + in_specs,
            out_specs=out_specs,
            check_vma=False,
        )
        tables = (table, plain, doubled, plain_t, doubled_t, quad)
        return mapped(*tables, grid, cotangent, spectral_weight, w_in, w_out)

    return call
```

```python
import functools
import math

import jax
import jax.numpy as jnp
import ml_dtypes
import numpy as np
from jax import lax
from jax.experimental import pallas as pl
from jax.experimental.pallas import tpu as pltpu
from jax.sharding import PartitionSpec as P


def legendre_table(size):
    theta = math.pi * (np.arange(size) + 0.5) / size
    cosv, sinv = np.cos(theta), np.sin(theta)
    order = np.arange(size, dtype=np.float64)[:, None]
    start = np.empty((size, size))
    start[0] = math.sqrt(1.0 / (4.0 * math.pi))
    for m in range(1, size):
        start[m] = start[m - 1] * math.sqrt((2 * m + 1) / (2.0 * m)) * sinv
    table = np.zeros((size, size, size), dtype=ml_dtypes.bfloat16)
    before = np.zeros((size, size))
    now = np.zeros((size, size))
    for level in range(size):
        safe = np.where(order < level, order, 0.0)
        alpha = np.sqrt((4.0 * level * level - 1.0) / (level * level - safe * safe)) if level else 0.0
        beta = (
            np.sqrt(((level - 1.0) ** 2 - safe * safe).clip(0) / (4.0 * (level - 1.0) ** 2 - 1.0))
            if level > 1
            else 0.0
        )
        value = np.where(order < level, alpha * (cosv * now - beta * before), 0.0)
        value[level] = start[level]
        table[:, level, :] = value.astype(np.float32).astype(ml_dtypes.bfloat16)
        before, now = now, value
    return table


def quadrature(nlat, nlon):
    theta = math.pi * (np.arange(nlat) + 0.5) / nlat
    return (math.pi / nlat * np.sin(theta) * (2.0 * math.pi / nlon)).astype(np.float32)


def fourier_tables(nlon, modes, lon_count):
    phase = np.arange(nlon)[:, None] * np.arange(modes)[None, :] % nlon
    angle = 2.0 * math.pi / nlon * phase
    pair = np.stack([np.cos(angle), -np.sin(angle)]).astype(np.float32).astype(ml_dtypes.bfloat16)
    factor = np.where(np.arange(modes) == 0, 1.0, 2.0).astype(np.float32)
    doubled = (pair.astype(np.float32) * factor).astype(ml_dtypes.bfloat16)

    def arrange(values):
        values = values.reshape(2, nlon, lon_count, modes // lon_count).transpose(2, 1, 0, 3)
        return np.ascontiguousarray(values.reshape(lon_count, nlon, -1))

    return arrange(pair), arrange(doubled)


def gelu_parts(values):
    half = 0.5 * (1.0 + lax.erf(values * (1.0 / math.sqrt(2.0))))
    slope = half + values * jnp.exp(-0.5 * values * values) * (1.0 / math.sqrt(2.0 * math.pi))
    return values * half, slope


def swap_blocks(values, axis):
    return lax.all_to_all(values, axis, split_axis=0, concat_axis=0, tiled=True)


def fourier_kernel(rows, lon_rows, place_ref, matrix_ref, scale_ref, values_ref, out_ref):
    width = values_ref.shape[2]
    for row in range(rows):
        longitudes = values_ref[:, row * lon_rows : (row + 1) * lon_rows, :]
        out = jnp.dot(
            matrix_ref[0],
            longitudes.reshape(-1, width),
            preferred_element_type=jnp.float32,
        )
        lanes = slice(row * width, (row + 1) * width)
        out_ref[:, lanes] = (out * scale_ref[:, lanes]).astype(jnp.bfloat16)


def to_fourier(values, matrices, scale, lon_index, rows, lon_rows):
    lon_count, _, width = values.shape
    _, orders, longitudes = matrices.shape
    return pl.pallas_call(
        functools.partial(fourier_kernel, rows, lon_rows),
        grid_spec=pltpu.PrefetchScalarGridSpec(
            num_scalar_prefetch=1,
            grid=(1,),
            in_specs=[
                pl.BlockSpec((1, orders, longitudes), lambda i, place: (place[0], 0, 0)),
                pl.BlockSpec((1, rows * width), lambda i, place: (0, 0)),
                pl.BlockSpec((lon_count, rows * lon_rows, width), lambda i, place: (0, 0, 0)),
            ],
            out_specs=pl.BlockSpec((orders, rows * width), lambda i, place: (0, 0)),
        ),
        out_shape=jax.ShapeDtypeStruct((orders, rows * width), jnp.bfloat16),
        compiler_params=pltpu.CompilerParams(vmem_limit_bytes=16 * 1024 * 1024),
        cost_estimate=pl.CostEstimate(
            flops=2 * orders * longitudes * rows * width,
            bytes_accessed=2 * (longitudes + orders) * rows * width + 2 * orders * longitudes,
            transcendentals=0,
        ),
    )(lon_index.reshape(1).astype(jnp.int32), matrices, scale, values)


def scatter_sum(values, axis, index, count, shifted):
    chunk = values.shape[-1] // count
    narrow = values.astype(jnp.bfloat16)
    parts = [lax.dynamic_slice_in_dim(values, index * chunk, chunk, axis=1)]
    for shift in range(1, count):
        to = (index + shift) % count
        block = lax.dynamic_slice_in_dim(narrow, to * chunk, chunk, axis=1)
        parts.append(lax.ppermute(block, axis, shifted(shift)))
    return parts


def add_parts(parts):
    total = parts[0]
    for part in parts[1:]:
        total = total + part.astype(jnp.float32)
    return total


def body(table_all, plain_all, doubled_all, plain_t, doubled_t, quad, grid, cotangent, spectral_weight, w_in, w_out):
    lat_count = lax.axis_size("lat")
    lon_count = lax.axis_size("lon")
    lat_index = lax.axis_index("lat")
    lon_index = lax.axis_index("lon")
    rows, lon_rows, width = grid.shape
    quarter = width // lon_count
    total_lat = rows * lat_count
    total_lon = lon_rows * lon_count
    half = lat_count // 2
    order = lon_index * half + lat_index % half
    table = lax.dynamic_index_in_dim(table_all, order, 0, keepdims=False)
    plain = lax.dynamic_index_in_dim(plain_all, lon_index, 0, keepdims=False)
    doubled = lax.dynamic_index_in_dim(doubled_all, lon_index, 0, keepdims=False)
    local_quad = lax.dynamic_slice_in_dim(quad, lat_index * rows, rows)
    quad_lanes = jnp.repeat(local_quad, width)[None, :]

    def to_orders(values, matrices, scale):
        out = to_fourier(values, matrices, scale, lon_index, rows, lon_rows)
        return out.reshape(lat_count, rows, width)

    def from_fourier(values, matrix, scale):
        values = values.reshape(lat_count, rows * width)
        out = jnp.dot(matrix, values, preferred_element_type=jnp.float32)
        if scale is not None:
            out = out * scale
        out = out.astype(jnp.bfloat16).reshape(lon_count, lon_rows, rows * width)
        out = jnp.sum(swap_blocks(out, "lon").astype(jnp.float32), axis=0)
        return out.reshape(lon_rows, rows, width).transpose(1, 0, 2).reshape(-1, width)

    def analyze(values):
        out = jnp.dot(table, values.reshape(total_lat, width), preferred_element_type=jnp.float32)
        return out.astype(jnp.bfloat16).reshape(lat_count, rows, width)

    def synthesize(values):
        out = lax.dot_general(
            table,
            values.reshape(total_lat, width),
            (((0,), (0,)), ((), ())),
            preferred_element_type=jnp.float32,
        )
        return out.astype(jnp.bfloat16).reshape(lat_count, rows, width)

    def complex_product(values, dims, sign):
        by_re = jnp.einsum(dims, values, weights[0], preferred_element_type=jnp.float32)
        by_im = jnp.einsum(dims, values, weights[1], preferred_element_type=jnp.float32)
        out_re = by_re[:half] + sign * by_im[half:]
        out_im = by_re[half:] - sign * by_im[:half]
        return jnp.concatenate([out_re, out_im]).astype(jnp.bfloat16)

    with jax.named_scope("forward_analysis"):
        gathered = lax.all_gather(grid.reshape(-1, width), "lon", axis=0)
        gathered, own_weight = lax.optimization_barrier((gathered, spectral_weight))
        four = swap_blocks(to_orders(gathered, plain_t, quad_lanes), "lat")
    with jax.named_scope("weights"):
        own_weight = own_weight.transpose(0, 1, 3, 2).reshape(-1, width)
        weights = lax.all_gather(own_weight, "lon", axis=0)
        weights = weights.reshape(lon_count, 2, rows, quarter, width)
        weights = weights.transpose(1, 2, 0, 3, 4).reshape(2, rows, width, width)
    with jax.named_scope("forward_analysis"):
        spectrum = swap_blocks(analyze(four), "lat")
    with jax.named_scope("mix"):
        mixed = complex_product(spectrum, "plc,ldc->pld", -1.0)
    with jax.named_scope("forward_synthesis"):
        fields = swap_blocks(synthesize(swap_blocks(mixed, "lat")), "lat")
        wave_rows = from_fourier(fields, doubled, None)
    with jax.named_scope("pointwise"):
        hidden = (grid.reshape(-1, width).astype(jnp.float32) + wave_rows).astype(jnp.bfloat16)
        back = cotangent.reshape(-1, width)
        act_grad = lax.dot_general(
            back, w_out, (((1,), (1,)), ((), ())), preferred_element_type=jnp.float32
        )
        pre = jnp.dot(hidden, w_in, preferred_element_type=jnp.float32)
        value, slope = gelu_parts(pre)
        act = value.astype(jnp.bfloat16)
        pre_grad = (act_grad * slope).astype(jnp.bfloat16)
        hidden_grad = (
            back.astype(jnp.float32)
            + lax.dot_general(
                pre_grad, w_in, (((1,), (1,)), ((), ())), preferred_element_type=jnp.float32
            )
        ).astype(jnp.bfloat16)
        block_output = (
            hidden.astype(jnp.float32) + jnp.dot(act, w_out, preferred_element_type=jnp.float32)
        ).astype(jnp.bfloat16)
    with jax.named_scope("backward_analysis"):
        gathered = lax.all_gather(hidden_grad, "lon", axis=0)
        gathered, hidden, pre_grad, act = lax.optimization_barrier(
            (gathered, hidden, pre_grad, act)
        )
        field_grad = swap_blocks(to_orders(gathered, doubled_t, jnp.ones_like(quad_lanes)), "lat")
    with jax.named_scope("pointwise_weights"):
        over_rows = (((0,), (0,)), ((), ()))
        out_part = lax.dot_general(act, back, over_rows, preferred_element_type=jnp.float32)
        in_part = lax.dot_general(hidden, pre_grad, over_rows, preferred_element_type=jnp.float32)
        in_part = in_part.reshape(out_part.shape)
        even = lat_index % 2 == 0
        keep = jnp.where(even, in_part, out_part)
        give = jnp.where(even, out_part, in_part).astype(jnp.bfloat16)
        got = lax.ppermute(give, "lat", [(i, i ^ 1) for i in range(lat_count)])
    with jax.named_scope("backward_analysis"):
        mixed_grad = analyze(field_grad)
        mixed_grad, keep, got = lax.optimization_barrier((mixed_grad, keep, got))
        mixed_grad = swap_blocks(mixed_grad, "lat")
    with jax.named_scope("pointwise_weights"):
        sums = add_parts([keep, got]).reshape(lat_count, -1)
        parts = scatter_sum(
            sums,
            "lon",
            lon_index,
            lon_count,
            lambda s: [(i, (i + s) % lon_count) for i in range(lon_count)],
        )
    with jax.named_scope("unmix"):
        spectrum_grad = complex_product(mixed_grad, "pld,ldc->plc", 1.0)
    with jax.named_scope("backward_synthesis"):
        spectrum_grad = swap_blocks(spectrum_grad, "lat")
    with jax.named_scope("pointwise_weights"):
        parts = scatter_sum(
            add_parts(parts),
            "lat",
            (lat_index >> 1) & 3,
            4,
            lambda s: [(i, (i & ~6) | ((i + 2 * s) & 6)) for i in range(lat_count)],
        )
    with jax.named_scope("backward_synthesis"):
        four_grad = synthesize(spectrum_grad)
        extra = add_parts(parts).astype(jnp.bfloat16)
        chunk = extra.shape[1]
        room = -(-chunk // (rows * 128)) * rows * 128
        extra = jnp.pad(extra, ((0, 0), (0, room - chunk)))
        extra = extra.reshape(lat_count, rows, room // rows)
        four_grad = jnp.concatenate([four_grad, extra], axis=2)
        four_grad, left, right = lax.optimization_barrier((four_grad, spectrum, mixed_grad))
        four_grad = swap_blocks(four_grad, "lat")
        wave_grad = from_fourier(four_grad[:, :, :width], plain, quad_lanes)
        grad_input = (hidden_grad.astype(jnp.float32) + wave_grad).astype(jnp.bfloat16)
    with jax.named_scope("unmix"):
        right = jnp.stack([right, jnp.concatenate([right[half:], -right[:half]])])
        outer = jnp.einsum("pli,rpld->rlid", left, right, preferred_element_type=jnp.float32)
        outer = outer.reshape(2, rows, lon_count, quarter, width)
        own = lax.dynamic_index_in_dim(outer, lon_index, 2, keepdims=False)
        narrow = outer.astype(jnp.bfloat16)
        grad_spectral = [own]
        for shift in range(1, lon_count):
            to = (lon_index + shift) % lon_count
            block = lax.dynamic_index_in_dim(narrow, to, 2, keepdims=False)
            pairs = [(i, (i + shift) % lon_count) for i in range(lon_count)]
            grad_spectral.append(lax.ppermute(block, "lon", pairs))
        grad_spectral = add_parts(grad_spectral)
    with jax.named_scope("pointwise_weights"):
        sums = four_grad[:, :, width:].reshape(lat_count // 8, 4, 2, room)[..., :chunk]
        sums = jnp.sum(sums.astype(jnp.float32), axis=0).swapaxes(0, 1).reshape(2, -1)
    return (
        block_output.reshape(grid.shape),
        grad_input.reshape(grid.shape),
        grad_spectral,
        sums[0],
        sums[1],
    )


def solution(mesh):
    in_specs = (P("lat", "lon", None), P("lat", "lon", None), P(None, "lat", None, "lon"), P(), P())
    out_specs = (
        P("lat", "lon", None),
        P("lat", "lon", None),
        P(None, "lat", "lon", None),
        P(("lat", "lon")),
        P(("lat", "lon")),
    )

    def call(grid, cotangent, spectral_weight, w_in, w_out):
        nlat, nlon, _ = grid.shape
        table = legendre_table(nlat)
        plain, doubled = fourier_tables(nlon, nlat, mesh.shape["lon"])
        plain_t = np.ascontiguousarray(plain.swapaxes(1, 2))
        doubled_t = np.ascontiguousarray(doubled.swapaxes(1, 2))
        quad = quadrature(nlat, nlon)
        mapped = jax.shard_map(
            body,
            mesh=mesh,
            in_specs=(P(),) * 6 + in_specs,
            out_specs=out_specs,
            check_vma=False,
        )
        tables = (table, plain, doubled, plain_t, doubled_t, quad)
        return mapped(*tables, grid, cotangent, spectral_weight, w_in, w_out)

    return call
```

```python
import functools
import math

import jax
import jax.numpy as jnp
import ml_dtypes
import numpy as np
from jax import lax
from jax.experimental import pallas as pl
from jax.experimental.pallas import tpu as pltpu
from jax.sharding import PartitionSpec as P


def legendre_table(size):
    theta = math.pi * (np.arange(size) + 0.5) / size
    cosv, sinv = np.cos(theta), np.sin(theta)
    order = np.arange(size, dtype=np.float64)[:, None]
    start = np.empty((size, size))
    start[0] = math.sqrt(1.0 / (4.0 * math.pi))
    for m in range(1, size):
        start[m] = start[m - 1] * math.sqrt((2 * m + 1) / (2.0 * m)) * sinv
    table = np.zeros((size, size, size), dtype=ml_dtypes.bfloat16)
    before = np.zeros((size, size))
    now = np.zeros((size, size))
    for level in range(size):
        safe = np.where(order < level, order, 0.0)
        alpha = np.sqrt((4.0 * level * level - 1.0) / (level * level - safe * safe)) if level else 0.0
        beta = (
            np.sqrt(((level - 1.0) ** 2 - safe * safe).clip(0) / (4.0 * (level - 1.0) ** 2 - 1.0))
            if level > 1
            else 0.0
        )
        value = np.where(order < level, alpha * (cosv * now - beta * before), 0.0)
        value[level] = start[level]
        table[:, level, :] = value.astype(np.float32).astype(ml_dtypes.bfloat16)
        before, now = now, value
    return table


def quadrature(nlat, nlon):
    theta = math.pi * (np.arange(nlat) + 0.5) / nlat
    return (math.pi / nlat * np.sin(theta) * (2.0 * math.pi / nlon)).astype(np.float32)


def fourier_tables(nlon, modes, lon_count, rows):
    phase = np.arange(nlon)[:, None] * np.arange(modes)[None, :] % nlon
    angle = 2.0 * math.pi / nlon * phase
    pair = np.stack([np.cos(angle), -np.sin(angle)]).astype(np.float32).astype(ml_dtypes.bfloat16)
    factor = np.where(np.arange(modes) == 0, 1.0, 2.0).astype(np.float32)
    doubled = (pair.astype(np.float32) * factor).astype(ml_dtypes.bfloat16)

    def arrange(values):
        values = values.reshape(2, lon_count, nlon // lon_count, lon_count, modes // lon_count)
        values = values.transpose(3, 0, 4, 1, 2)
        out = np.zeros(values.shape[:3] + (rows, lon_count, rows, values.shape[4]), values.dtype)
        for row in range(rows):
            out[:, :, :, row, :, row] = values
        return out.reshape(lon_count, 2 * modes // lon_count * rows, nlon * rows)

    return arrange(pair), arrange(doubled)


def gelu_parts(values):
    half = 0.5 * (1.0 + lax.erf(values * (1.0 / math.sqrt(2.0))))
    slope = half + values * jnp.exp(-0.5 * values * values) * (1.0 / math.sqrt(2.0 * math.pi))
    return values * half, slope


def swap_blocks(values, axis):
    return lax.all_to_all(values, axis, split_axis=0, concat_axis=0, tiled=True)


def product_kernel(dims, matrix_ref, *refs):
    *scale_ref, values_ref, out_ref = refs
    width = out_ref.shape[-1]
    values = values_ref[...].reshape(-1, width)
    out = lax.dot_general(matrix_ref[0], values, dims, preferred_element_type=jnp.float32)
    if scale_ref:
        out = out * scale_ref[0][...]
    out_ref[...] = out.astype(jnp.bfloat16).reshape(out_ref.shape)


def beside_kernel(dims, matrix_ref, values_ref, extra_ref, out_ref):
    width = values_ref.shape[-1]
    values = values_ref[...].reshape(-1, width)
    out = lax.dot_general(matrix_ref[0], values, dims, preferred_element_type=jnp.float32)
    out_ref[:, :, :width] = out.astype(jnp.bfloat16).reshape(values_ref.shape)
    out_ref[:, :, width:] = extra_ref[...]


def mix_kernel(conjugate, weights_ref, values_ref, out_ref):
    rows, width = weights_ref.shape[1], weights_ref.shape[3]
    values = values_ref[...].reshape(-1, width)
    level = lax.broadcasted_iota(jnp.int32, values.shape, 0) & (rows - 1)
    dims = (((1,), (0 if conjugate else 1,)), ((), ()))

    def product(part):
        total = None
        for row in range(rows):
            out = lax.dot_general(
                values, weights_ref[part, row], dims, preferred_element_type=jnp.float32
            )
            total = out if row == 0 else jnp.where(level == row, out, total)
        return total

    by_re, by_im = product(0), product(1)
    if conjugate:
        by_im = -by_im
    half = values.shape[0] // 2
    out = jnp.concatenate([by_re[:half] - by_im[half:], by_re[half:] + by_im[:half]])
    out_ref[...] = out.astype(jnp.bfloat16).reshape(out_ref.shape)


def placed(kernel, place_ref, *refs):
    kernel(*refs)


def whole(shape):
    return pl.BlockSpec(shape, lambda *_: (0,) * len(shape))


def call_kernel(kernel, place, matrices, operands, blocks, out_shape, flops):
    specs = [whole(block) for block in blocks]
    prefetch = ()
    if place is not None:
        specs.insert(0, pl.BlockSpec((1,) + matrices.shape[1:], lambda i, at: (at[0], 0, 0)))
        operands = [matrices] + operands
        prefetch = (place.reshape(1).astype(jnp.int32),)
        kernel = functools.partial(placed, kernel)
    moved = 2 * (math.prod(out_shape) + sum(math.prod(block) for block in blocks))
    return pl.pallas_call(
        kernel,
        grid_spec=pltpu.PrefetchScalarGridSpec(
            num_scalar_prefetch=len(prefetch),
            grid=(1,),
            in_specs=specs,
            out_specs=whole(out_shape),
        ),
        out_shape=jax.ShapeDtypeStruct(out_shape, jnp.bfloat16),
        compiler_params=pltpu.CompilerParams(vmem_limit_bytes=20 * 1024 * 1024),
        cost_estimate=pl.CostEstimate(flops=flops, bytes_accessed=moved, transcendentals=0),
    )(*prefetch, *operands)


PLAIN = (((1,), (0,)), ((), ()))
TURNED = (((0,), (0,)), ((), ()))


def place_product(dims, place, matrices, scale, values, block, out_shape):
    operands, blocks = [values], [block]
    if scale is not None:
        operands, blocks = [scale, values], [scale.shape, block]
    flops = 2 * math.prod(matrices.shape[1:]) * out_shape[-1]
    kernel = functools.partial(product_kernel, dims)
    return call_kernel(kernel, place, matrices, operands, blocks, out_shape, flops)


def scatter_sum(values, axis, index, count, shifted):
    chunk = values.shape[-1] // count
    narrow = values.astype(jnp.bfloat16)
    parts = [lax.dynamic_slice_in_dim(values, index * chunk, chunk, axis=1)]
    for shift in range(1, count):
        to = (index + shift) % count
        block = lax.dynamic_slice_in_dim(narrow, to * chunk, chunk, axis=1)
        parts.append(lax.ppermute(block, axis, shifted(shift)))
    return parts


def add_parts(parts):
    total = parts[0]
    for part in parts[1:]:
        total = total + part.astype(jnp.float32)
    return total


def body(tables, plain, doubled, plain_t, doubled_t, quad, grid, cotangent, *weights_in):
    spectral_weight, w_in, w_out = weights_in
    lat_count = lax.axis_size("lat")
    lon_count = lax.axis_size("lon")
    lat_index = lax.axis_index("lat")
    lon_index = lax.axis_index("lon")
    rows, lon_rows, width = grid.shape
    quarter = width // lon_count
    half = lat_count // 2
    order = lon_index * half + lat_index % half
    local_quad = lax.dynamic_slice_in_dim(quad, lat_index * rows, rows)
    order_quad = jnp.tile(local_quad, lat_count)[:, None]
    row_quad = jnp.tile(jnp.repeat(local_quad, lon_rows), lon_count)[:, None]
    total_lat = rows * lat_count
    spread = (lat_count, rows, width)
    gathered_shape = (lon_count, rows * lon_rows, width)

    def to_orders(values, matrices, scale):
        return place_product(PLAIN, lon_index, matrices, scale, values, gathered_shape, spread)

    def from_orders(values, matrices, scale):
        out = place_product(PLAIN, lon_index, matrices, scale, values, spread, gathered_shape)
        return jnp.sum(swap_blocks(out, "lon").astype(jnp.float32), axis=0)

    def legendre(dims, values):
        kernel = functools.partial(product_kernel, dims)
        flops = 2 * total_lat * total_lat * width
        blocks = [table.shape, spread]
        return call_kernel(kernel, None, None, [table, values], blocks, spread, flops)

    def complex_product(values, conjugate):
        return call_kernel(
            functools.partial(mix_kernel, conjugate),
            None,
            None,
            [weights, values],
            [weights.shape, spread],
            spread,
            8 * rows * values.size * width,
        )

    with jax.named_scope("forward_analysis"):
        gathered = lax.all_gather(grid.reshape(-1, width), "lon", axis=0)
        gathered, order = lax.optimization_barrier((gathered, order))
        table = lax.dynamic_slice_in_dim(tables, order, 1)
        own_weight = spectral_weight
        own_weight = own_weight.transpose(0, 1, 3, 2)[:, :, None]
        four = swap_blocks(to_orders(gathered, plain_t, order_quad), "lat")
    with jax.named_scope("weights"):
        weights = jnp.zeros((2, rows, lon_count, quarter, width), jnp.bfloat16)
        weights = lax.dynamic_update_slice_in_dim(weights, own_weight, lon_index, 2)
        for shift in range(1, lon_count):
            pairs = [(i, (i + shift) % lon_count) for i in range(lon_count)]
            moved = lax.ppermute(own_weight, "lon", pairs)
            source = (lon_index + lon_count - shift) % lon_count
            weights = lax.dynamic_update_slice_in_dim(weights, moved, source, 2)
        weights = weights.reshape(2, rows, width, width)
    with jax.named_scope("forward_analysis"):
        spectrum = swap_blocks(legendre(PLAIN, four), "lat")
    with jax.named_scope("mix"):
        mixed = complex_product(spectrum, False)
    with jax.named_scope("forward_synthesis"):
        fields = swap_blocks(legendre(TURNED, swap_blocks(mixed, "lat")), "lat")
        wave_rows = from_orders(fields, doubled, None)
    with jax.named_scope("pointwise"):
        hidden = (grid.reshape(-1, width).astype(jnp.float32) + wave_rows).astype(jnp.bfloat16)
        back = cotangent.reshape(-1, width)
        act_grad = lax.dot_general(
            back, w_out, (((1,), (1,)), ((), ())), preferred_element_type=jnp.float32
        )
        pre = jnp.dot(hidden, w_in, preferred_element_type=jnp.float32)
        value, slope = gelu_parts(pre)
        act = value.astype(jnp.bfloat16)
        pre_grad = (act_grad * slope).astype(jnp.bfloat16)
        hidden_grad = (
            back.astype(jnp.float32)
            + lax.dot_general(
                pre_grad, w_in, (((1,), (1,)), ((), ())), preferred_element_type=jnp.float32
            )
        ).astype(jnp.bfloat16)
        block_output = (
            hidden.astype(jnp.float32) + jnp.dot(act, w_out, preferred_element_type=jnp.float32)
        ).astype(jnp.bfloat16)
    with jax.named_scope("backward_analysis"):
        gathered = lax.all_gather(hidden_grad, "lon", axis=0)
        gathered, hidden, pre_grad, act = lax.optimization_barrier(
            (gathered, hidden, pre_grad, act)
        )
        field_grad = swap_blocks(to_orders(gathered, doubled_t, None), "lat")
    with jax.named_scope("pointwise_weights"):
        over_rows = (((0,), (0,)), ((), ()))
        out_part = lax.dot_general(act, back, over_rows, preferred_element_type=jnp.float32)
        in_part = lax.dot_general(hidden, pre_grad, over_rows, preferred_element_type=jnp.float32)
        in_part = in_part.reshape(out_part.shape)
        even = lat_index % 2 == 0
        keep = jnp.where(even, in_part, out_part)
        give = jnp.where(even, out_part, in_part).astype(jnp.bfloat16)
        got = lax.ppermute(give, "lat", [(i, i ^ 1) for i in range(lat_count)])
    with jax.named_scope("backward_analysis"):
        mixed_grad = legendre(PLAIN, field_grad)
        mixed_grad, keep, got = lax.optimization_barrier((mixed_grad, keep, got))
        mixed_grad = swap_blocks(mixed_grad, "lat")
    with jax.named_scope("pointwise_weights"):
        sums = add_parts([keep, got]).reshape(lat_count, -1)
        parts = scatter_sum(
            sums,
            "lon",
            lon_index,
            lon_count,
            lambda s: [(i, (i + s) % lon_count) for i in range(lon_count)],
        )
    with jax.named_scope("unmix"):
        spectrum_grad = complex_product(mixed_grad, True)
    with jax.named_scope("backward_synthesis"):
        spectrum_grad = swap_blocks(spectrum_grad, "lat")
    with jax.named_scope("pointwise_weights"):
        parts = scatter_sum(
            add_parts(parts),
            "lat",
            (lat_index >> 1) & 3,
            4,
            lambda s: [(i, (i & ~6) | ((i + 2 * s) & 6)) for i in range(lat_count)],
        )
    with jax.named_scope("backward_synthesis"):
        extra = add_parts(parts).astype(jnp.bfloat16)
        chunk = extra.shape[1]
        room = -(-chunk // (rows * 128)) * rows * 128
        extra = jnp.pad(extra, ((0, 0), (0, room - chunk)))
        extra = extra.reshape(lat_count, rows, room // rows)
        four_grad = call_kernel(
            functools.partial(beside_kernel, TURNED),
            None,
            None,
            [table, spectrum_grad, extra],
            [table.shape, spread, extra.shape],
            (lat_count, rows, width + extra.shape[2]),
            2 * total_lat * total_lat * width,
        )
        four_grad, left, right = lax.optimization_barrier((four_grad, spectrum, mixed_grad))
        four_grad = swap_blocks(four_grad, "lat")
        wave_grad = from_orders(four_grad, plain, row_quad)
        grad_input = (hidden_grad.astype(jnp.float32) + wave_grad).astype(jnp.bfloat16)
    with jax.named_scope("unmix"):
        right = jnp.stack([right, jnp.concatenate([right[half:], -right[:half]])])
        outer = jnp.einsum("pli,rpld->rlid", left, right, preferred_element_type=jnp.float32)
        outer = outer.reshape(2, rows, lon_count, quarter, width)
        own = lax.dynamic_index_in_dim(outer, lon_index, 2, keepdims=False)
        narrow = outer.astype(jnp.bfloat16)
        grad_spectral = [own]
        for shift in range(1, lon_count):
            to = (lon_index + shift) % lon_count
            block = lax.dynamic_index_in_dim(narrow, to, 2, keepdims=False)
            pairs = [(i, (i + shift) % lon_count) for i in range(lon_count)]
            grad_spectral.append(lax.ppermute(block, "lon", pairs))
        grad_spectral = add_parts(grad_spectral)
    with jax.named_scope("pointwise_weights"):
        sums = four_grad[:, :, width:].reshape(lat_count // 8, 4, 2, room)[..., :chunk]
        sums = jnp.sum(sums.astype(jnp.float32), axis=0).swapaxes(0, 1).reshape(2, -1)
    return (
        block_output.reshape(grid.shape),
        grad_input.reshape(grid.shape),
        grad_spectral,
        sums[0],
        sums[1],
    )


def solution(mesh):
    in_specs = (P("lat", "lon", None), P("lat", "lon", None), P(None, "lat", None, "lon"), P(), P())
    out_specs = (
        P("lat", "lon", None),
        P("lat", "lon", None),
        P(None, "lat", "lon", None),
        P(("lat", "lon")),
        P(("lat", "lon")),
    )

    def call(grid, cotangent, spectral_weight, w_in, w_out):
        nlat, nlon, _ = grid.shape
        table = legendre_table(nlat)
        rows = nlat // mesh.shape["lat"]
        plain_t, doubled_t = fourier_tables(nlon, nlat, mesh.shape["lon"], rows)
        plain = np.ascontiguousarray(plain_t.swapaxes(1, 2))
        doubled = np.ascontiguousarray(doubled_t.swapaxes(1, 2))
        quad = quadrature(nlat, nlon)
        mapped = jax.shard_map(
            body,
            mesh=mesh,
            in_specs=(P(),) * 6 + in_specs,
            out_specs=out_specs,
            check_vma=False,
        )
        tables = (table, plain, doubled, plain_t, doubled_t, quad)
        return mapped(*tables, grid, cotangent, spectral_weight, w_in, w_out)

    return call
```

```python
import functools
import math

import jax
import jax.numpy as jnp
import ml_dtypes
import numpy as np
from jax import lax
from jax.experimental import pallas as pl
from jax.experimental.pallas import tpu as pltpu
from jax.sharding import PartitionSpec as P


def legendre_table(size):
    theta = math.pi * (np.arange(size) + 0.5) / size
    cosv, sinv = np.cos(theta), np.sin(theta)
    order = np.arange(size, dtype=np.float64)[:, None]
    start = np.empty((size, size))
    start[0] = math.sqrt(1.0 / (4.0 * math.pi))
    for m in range(1, size):
        start[m] = start[m - 1] * math.sqrt((2 * m + 1) / (2.0 * m)) * sinv
    table = np.zeros((size, size, size), dtype=ml_dtypes.bfloat16)
    before = np.zeros((size, size))
    now = np.zeros((size, size))
    for level in range(size):
        safe = np.where(order < level, order, 0.0)
        alpha = np.sqrt((4.0 * level * level - 1.0) / (level * level - safe * safe)) if level else 0.0
        beta = (
            np.sqrt(((level - 1.0) ** 2 - safe * safe).clip(0) / (4.0 * (level - 1.0) ** 2 - 1.0))
            if level > 1
            else 0.0
        )
        value = np.where(order < level, alpha * (cosv * now - beta * before), 0.0)
        value[level] = start[level]
        table[:, level, :] = value.astype(np.float32).astype(ml_dtypes.bfloat16)
        before, now = now, value
    return table


def quadrature(nlat, nlon):
    theta = math.pi * (np.arange(nlat) + 0.5) / nlat
    return (math.pi / nlat * np.sin(theta) * (2.0 * math.pi / nlon)).astype(np.float32)


def fourier_tables(nlon, modes, lon_count, rows):
    phase = np.arange(nlon)[:, None] * np.arange(modes)[None, :] % nlon
    angle = 2.0 * math.pi / nlon * phase
    pair = np.stack([np.cos(angle), -np.sin(angle)]).astype(np.float32).astype(ml_dtypes.bfloat16)
    factor = np.where(np.arange(modes) == 0, 1.0, 2.0).astype(np.float32)
    doubled = (pair.astype(np.float32) * factor).astype(ml_dtypes.bfloat16)

    def arrange(values):
        values = values.reshape(2, lon_count, nlon // lon_count, lon_count, modes // lon_count)
        values = values.transpose(3, 0, 4, 1, 2)
        out = np.zeros(values.shape[:3] + (rows, lon_count, rows, values.shape[4]), values.dtype)
        for row in range(rows):
            out[:, :, :, row, :, row] = values
        return out.reshape(lon_count, 2 * modes // lon_count * rows, nlon * rows)

    return arrange(pair), arrange(doubled)


def gelu_parts(values):
    half = 0.5 * (1.0 + lax.erf(values * (1.0 / math.sqrt(2.0))))
    slope = half + values * jnp.exp(-0.5 * values * values) * (1.0 / math.sqrt(2.0 * math.pi))
    return values * half, slope


def swap_blocks(values, axis):
    return lax.all_to_all(values, axis, split_axis=0, concat_axis=0, tiled=True)


PLAIN = (((1,), (0,)), ((), ()))
TURNED = (((0,), (0,)), ((), ()))
MIB = 1024 * 1024


def product_kernel(dims, matrix_ref, values_ref, out_ref):
    width = out_ref.shape[-1]
    values = values_ref[...].reshape(-1, width)
    out = lax.dot_general(matrix_ref[0], values, dims, preferred_element_type=jnp.float32)
    out_ref[...] = out.astype(jnp.bfloat16).reshape(out_ref.shape)


def fourier_kernel(period, place_ref, matrix_ref, quad_ref, values_ref, out_ref):
    width = out_ref.shape[-1]
    values = values_ref[...].reshape(-1, width)
    out = lax.dot_general(matrix_ref[0], values, PLAIN, preferred_element_type=jnp.float32)
    row = lax.broadcasted_iota(jnp.int32, out.shape, 0) & (2 * period - 1)
    first = quad_ref[2 * place_ref[1]]
    second = quad_ref[2 * place_ref[1] + 1]
    out = out * jnp.where(row < period, first, second)
    out_ref[...] = out.astype(jnp.bfloat16).reshape(out_ref.shape)


def gradient_kernel(place_ref, act_ref, back_ref, hidden_ref, pre_grad_ref, *refs):
    own_ref, *sent_refs, in_ref, out_ref, flat_ref = refs
    count = len(sent_refs) + 1
    _, lat_count, chunk = own_ref.shape
    dims = (((0,), (0,)), ((), ()))
    pairs = ((hidden_ref, pre_grad_ref, in_ref), (act_ref, back_ref, out_ref))
    for part, (left_ref, right_ref, ref) in enumerate(pairs):
        total = lax.dot_general(
            left_ref[...], right_ref[...], dims, preferred_element_type=jnp.float32
        )
        size, width = total.shape
        step = size // lat_count
        for tile in range(width // 128):
            ref[tile * size : (tile + 1) * size, :] = total[:, tile * 128 : (tile + 1) * 128]
        for i in range(step):
            for tile in range(width // 128):
                lane = i * width + tile * 128
                rows = ref[pl.ds(tile * size + i, lat_count, stride=step), :]
                flat_ref[part, :, lane : lane + 128] = rows
    for place in range(count):

        @pl.when(place_ref[0] == place)
        def _():
            own_ref[...] = flat_ref[:, :, place * chunk : (place + 1) * chunk]
            for shift, ref in enumerate(sent_refs, 1):
                to = (place + shift) % count
                block = flat_ref[:, :, to * chunk : (to + 1) * chunk]
                ref[...] = block.astype(jnp.bfloat16)


def beside_kernel(dims, matrix_ref, values_ref, extra_ref, out_ref):
    width = values_ref.shape[-1]
    values = values_ref[...].reshape(-1, width)
    out = lax.dot_general(matrix_ref[0], values, dims, preferred_element_type=jnp.float32)
    out_ref[:, :, :width] = out.astype(jnp.bfloat16).reshape(values_ref.shape)
    out_ref[:, :, width:] = extra_ref[...]


def mix_kernel(conjugate, weights_ref, values_ref, out_ref):
    rows, width = weights_ref.shape[1], weights_ref.shape[3]
    values = values_ref[...].reshape(-1, width)
    level = lax.broadcasted_iota(jnp.int32, values.shape, 0) & (rows - 1)
    dims = (((1,), (0 if conjugate else 1,)), ((), ()))

    def product(part):
        total = None
        for row in range(rows):
            out = lax.dot_general(
                values, weights_ref[part, row], dims, preferred_element_type=jnp.float32
            )
            total = out if row == 0 else jnp.where(level == row, out, total)
        return total

    by_re, by_im = product(0), product(1)
    if conjugate:
        by_im = -by_im
    half = values.shape[0] // 2
    out = jnp.concatenate([by_re[:half] - by_im[half:], by_re[half:] + by_im[:half]])
    out_ref[...] = out.astype(jnp.bfloat16).reshape(out_ref.shape)


def placed(kernel, place_ref, *refs):
    kernel(*refs)


def whole(shape):
    return pl.BlockSpec(shape, lambda *_: (0,) * len(shape))


def call_kernel(kernel, operands, blocks, out_shape, flops):
    moved = 2 * (math.prod(out_shape) + sum(math.prod(block) for block in blocks))
    return pl.pallas_call(
        kernel,
        grid=(1,),
        in_specs=[whole(block) for block in blocks],
        out_specs=whole(out_shape),
        out_shape=jax.ShapeDtypeStruct(out_shape, jnp.bfloat16),
        compiler_params=pltpu.CompilerParams(vmem_limit_bytes=20 * MIB),
        cost_estimate=pl.CostEstimate(flops=flops, bytes_accessed=moved, transcendentals=0),
    )(*operands)


def fourier_product(period, place, matrices, quad, values, block, out_shape, grant):
    kernel = functools.partial(fourier_kernel, period)
    specs = [
        pl.BlockSpec((1,) + matrices.shape[1:], lambda i, at: (at[0], 0, 0)),
        pl.BlockSpec(memory_space=pltpu.SMEM),
        whole(block),
    ]
    operands = (matrices, quad, values)
    if quad is None:
        kernel = functools.partial(placed, functools.partial(product_kernel, PLAIN))
        specs.pop(1)
        operands = (matrices, values)
    moved = 2 * (math.prod(out_shape) + math.prod(block) + math.prod(matrices.shape[1:]))
    return pl.pallas_call(
        kernel,
        grid_spec=pltpu.PrefetchScalarGridSpec(
            num_scalar_prefetch=1, grid=(1,), in_specs=specs, out_specs=whole(out_shape)
        ),
        out_shape=jax.ShapeDtypeStruct(out_shape, jnp.bfloat16),
        compiler_params=pltpu.CompilerParams(vmem_limit_bytes=grant * MIB),
        cost_estimate=pl.CostEstimate(
            flops=2 * math.prod(matrices.shape[1:]) * out_shape[-1],
            bytes_accessed=moved,
            transcendentals=0,
        ),
    )(place, *operands)


def gradient_blocks(lon_index, lon_count, lat_count, act, back, hidden, pre_grad):
    in_shape = (hidden.shape[1], pre_grad.shape[1])
    size = math.prod(in_shape)
    blocks = (2, lat_count, size // (lat_count * lon_count))
    dtypes = [jnp.float32] + [jnp.bfloat16] * (lon_count - 1)
    operands = (act, back, hidden, pre_grad)
    return pl.pallas_call(
        gradient_kernel,
        grid_spec=pltpu.PrefetchScalarGridSpec(
            num_scalar_prefetch=1,
            grid=(1,),
            in_specs=[whole(operand.shape) for operand in operands],
            out_specs=[whole(blocks)] * lon_count,
            scratch_shapes=[
                pltpu.VMEM((size // 128, 128), jnp.float32),
                pltpu.VMEM((size // 128, 128), jnp.float32),
                pltpu.VMEM((2, lat_count, size // lat_count), jnp.float32),
            ],
        ),
        out_shape=[jax.ShapeDtypeStruct(blocks, dtype) for dtype in dtypes],
        compiler_params=pltpu.CompilerParams(vmem_limit_bytes=24 * MIB),
        cost_estimate=pl.CostEstimate(
            flops=4 * size * act.shape[0], bytes_accessed=8 * size, transcendentals=0
        ),
    )(lon_index.reshape(1).astype(jnp.int32), *operands)


def scatter_sum(values, axis, index, count, shifted):
    last = values.ndim - 1
    chunk = values.shape[last] // count
    narrow = values.astype(jnp.bfloat16)
    parts = [lax.dynamic_slice_in_dim(values, index * chunk, chunk, axis=last)]
    for shift in range(1, count):
        to = (index + shift) % count
        block = lax.dynamic_slice_in_dim(narrow, to * chunk, chunk, axis=last)
        parts.append(lax.ppermute(block, axis, shifted(shift)))
    return parts


def add_parts(parts):
    total = parts[0]
    for part in parts[1:]:
        total = total + part.astype(jnp.float32)
    return total


def body(tables, plain, doubled, plain_t, doubled_t, quad, grid, cotangent, *weights_in):
    spectral_weight, w_in, w_out = weights_in
    lat_count = lax.axis_size("lat")
    lon_count = lax.axis_size("lon")
    lat_index = lax.axis_index("lat")
    lon_index = lax.axis_index("lon")
    rows, lon_rows, width = grid.shape
    quarter = width // lon_count
    half = lat_count // 2
    order = lon_index * half + lat_index % half
    place = jnp.stack([lon_index, lat_index]).astype(jnp.int32)
    total_lat = rows * lat_count
    spread = (lat_count, rows, width)
    gathered_shape = (lon_count, rows * lon_rows, width)

    def to_orders(values, matrices, scale, grant):
        return fourier_product(1, place, matrices, scale, values, gathered_shape, spread, grant)

    def from_orders(values, matrices, scale):
        out = fourier_product(
            lon_rows, place, matrices, scale, values, spread, gathered_shape, 20
        )
        return jnp.sum(swap_blocks(out, "lon").astype(jnp.float32), axis=0)

    def legendre(dims, values):
        kernel = functools.partial(product_kernel, dims)
        flops = 2 * total_lat * total_lat * width
        blocks = [table.shape, spread]
        return call_kernel(kernel, [table, values], blocks, spread, flops)

    def complex_product(values, conjugate):
        return call_kernel(
            functools.partial(mix_kernel, conjugate),
            [weights, values],
            [weights.shape, spread],
            spread,
            8 * rows * values.size * width,
        )

    with jax.named_scope("forward_analysis"):
        gathered = lax.all_gather(grid.reshape(-1, width), "lon", axis=0)
        gathered, order = lax.optimization_barrier((gathered, order))
        table = lax.dynamic_slice_in_dim(tables, order, 1)
        own_weight = spectral_weight
        own_weight = own_weight.transpose(0, 1, 3, 2)[:, :, None]
        four = swap_blocks(to_orders(gathered, plain_t, quad, 60), "lat")
    with jax.named_scope("weights"):
        weights = jnp.zeros((2, rows, lon_count, quarter, width), jnp.bfloat16)
        weights = lax.dynamic_update_slice_in_dim(weights, own_weight, lon_index, 2)
        for shift in range(1, lon_count):
            pairs = [(i, (i + shift) % lon_count) for i in range(lon_count)]
            moved = lax.ppermute(own_weight, "lon", pairs)
            source = (lon_index + lon_count - shift) % lon_count
            weights = lax.dynamic_update_slice_in_dim(weights, moved, source, 2)
        weights = weights.reshape(2, rows, width, width)
    with jax.named_scope("forward_analysis"):
        spectrum = swap_blocks(legendre(PLAIN, four), "lat")
    with jax.named_scope("mix"):
        mixed = complex_product(spectrum, False)
    with jax.named_scope("forward_synthesis"):
        fields = swap_blocks(legendre(TURNED, swap_blocks(mixed, "lat")), "lat")
        wave_rows = from_orders(fields, doubled, None)
    with jax.named_scope("pointwise"):
        hidden = (grid.reshape(-1, width).astype(jnp.float32) + wave_rows).astype(jnp.bfloat16)
        back = cotangent.reshape(-1, width)
        act_grad = lax.dot_general(
            back, w_out, (((1,), (1,)), ((), ())), preferred_element_type=jnp.float32
        )
        pre = jnp.dot(hidden, w_in, preferred_element_type=jnp.float32)
        value, slope = gelu_parts(pre)
        act = value.astype(jnp.bfloat16)
        pre_grad = (act_grad * slope).astype(jnp.bfloat16)
        hidden_grad = (
            back.astype(jnp.float32)
            + lax.dot_general(
                pre_grad, w_in, (((1,), (1,)), ((), ())), preferred_element_type=jnp.float32
            )
        ).astype(jnp.bfloat16)
        block_output = (
            hidden.astype(jnp.float32) + jnp.dot(act, w_out, preferred_element_type=jnp.float32)
        ).astype(jnp.bfloat16)
    with jax.named_scope("backward_analysis"):
        gathered = lax.all_gather(hidden_grad, "lon", axis=0)
        gathered, hidden, pre_grad, act = lax.optimization_barrier(
            (gathered, hidden, pre_grad, act)
        )
        field_grad = swap_blocks(to_orders(gathered, doubled_t, None, 20), "lat")
    with jax.named_scope("pointwise_weights"):
        parts = [*gradient_blocks(lon_index, lon_count, lat_count, act, back, hidden, pre_grad)]
        for shift in range(1, lon_count):
            pairs = [(i, (i + shift) % lon_count) for i in range(lon_count)]
            parts[shift] = lax.ppermute(parts[shift], "lon", pairs)
    with jax.named_scope("backward_analysis"):
        mixed_grad = legendre(PLAIN, field_grad)
        mixed_grad = swap_blocks(mixed_grad, "lat")
    with jax.named_scope("pointwise_weights"):
        parts = scatter_sum(
            add_parts(parts),
            "lat",
            (lat_index >> 1) & 3,
            4,
            lambda s: [(i, (i & ~6) | ((i + 2 * s) & 6)) for i in range(lat_count)],
        )
    with jax.named_scope("unmix"):
        spectrum_grad = complex_product(mixed_grad, True)
        spectrum_grad, *parts = lax.optimization_barrier((spectrum_grad, *parts))
    with jax.named_scope("backward_synthesis"):
        spectrum_grad = swap_blocks(spectrum_grad, "lat")
    with jax.named_scope("pointwise_weights"):
        sums = add_parts(parts)
        even = lat_index % 2 == 0
        give = jnp.where(even, sums[1], sums[0]).astype(jnp.bfloat16)
        got = lax.ppermute(give, "lat", [(i, i ^ 1) for i in range(lat_count)])
        parts = [jnp.where(even, sums[0], sums[1]), got]
    with jax.named_scope("backward_synthesis"):
        extra = add_parts(parts).astype(jnp.bfloat16)
        chunk = extra.shape[1]
        room = -(-chunk // (rows * 128)) * rows * 128
        extra = jnp.pad(extra, ((0, 0), (0, room - chunk)))
        extra = extra.reshape(lat_count, rows, room // rows)
        four_grad = call_kernel(
            functools.partial(beside_kernel, TURNED),
            [table, spectrum_grad, extra],
            [table.shape, spread, extra.shape],
            (lat_count, rows, width + extra.shape[2]),
            2 * total_lat * total_lat * width,
        )
        four_grad, left, right = lax.optimization_barrier((four_grad, spectrum, mixed_grad))
        four_grad = swap_blocks(four_grad, "lat")
        wave_grad = from_orders(four_grad, plain, quad)
        grad_input = (hidden_grad.astype(jnp.float32) + wave_grad).astype(jnp.bfloat16)
    with jax.named_scope("unmix"):
        right = jnp.stack([right, jnp.concatenate([right[half:], -right[:half]])])
        outer = jnp.einsum("pli,rpld->rlid", left, right, preferred_element_type=jnp.float32)
        outer = outer.reshape(2, rows, lon_count, quarter, width)
        own = lax.dynamic_index_in_dim(outer, lon_index, 2, keepdims=False)
        narrow = outer.astype(jnp.bfloat16)
        grad_spectral = [own]
        for shift in range(1, lon_count):
            to = (lon_index + shift) % lon_count
            block = lax.dynamic_index_in_dim(narrow, to, 2, keepdims=False)
            pairs = [(i, (i + shift) % lon_count) for i in range(lon_count)]
            grad_spectral.append(lax.ppermute(block, "lon", pairs))
        grad_spectral = add_parts(grad_spectral)
    with jax.named_scope("pointwise_weights"):
        sums = four_grad[:, :, width:].reshape(lat_count // 8, 4, 2, room)[..., :chunk]
        sums = jnp.sum(sums.astype(jnp.float32), axis=0).swapaxes(0, 1).reshape(2, -1)
    return (
        block_output.reshape(grid.shape),
        grad_input.reshape(grid.shape),
        grad_spectral,
        sums[0],
        sums[1],
    )


def solution(mesh):
    in_specs = (P("lat", "lon", None), P("lat", "lon", None), P(None, "lat", None, "lon"), P(), P())
    out_specs = (
        P("lat", "lon", None),
        P("lat", "lon", None),
        P(None, "lat", "lon", None),
        P(("lat", "lon")),
        P(("lat", "lon")),
    )

    def call(grid, cotangent, spectral_weight, w_in, w_out):
        nlat, nlon, _ = grid.shape
        table = legendre_table(nlat)
        rows = nlat // mesh.shape["lat"]
        plain_t, doubled_t = fourier_tables(nlon, nlat, mesh.shape["lon"], rows)
        plain = np.ascontiguousarray(plain_t.swapaxes(1, 2))
        doubled = np.ascontiguousarray(doubled_t.swapaxes(1, 2))
        quad = quadrature(nlat, nlon)
        mapped = jax.shard_map(
            body,
            mesh=mesh,
            in_specs=(P(),) * 6 + in_specs,
            out_specs=out_specs,
            check_vma=False,
        )
        tables = (table, plain, doubled, plain_t, doubled_t, quad)
        return mapped(*tables, grid, cotangent, spectral_weight, w_in, w_out)

    return call
```

```python
import functools
import math

import jax
import jax.numpy as jnp
import ml_dtypes
import numpy as np
from jax import lax
from jax.experimental import pallas as pl
from jax.experimental.pallas import tpu as pltpu
from jax.sharding import PartitionSpec as P


def legendre_table(size):
    theta = math.pi * (np.arange(size) + 0.5) / size
    cosv, sinv = np.cos(theta), np.sin(theta)
    order = np.arange(size, dtype=np.float64)[:, None]
    start = np.empty((size, size))
    start[0] = math.sqrt(1.0 / (4.0 * math.pi))
    for m in range(1, size):
        start[m] = start[m - 1] * math.sqrt((2 * m + 1) / (2.0 * m)) * sinv
    table = np.zeros((size, size, size), dtype=ml_dtypes.bfloat16)
    before = np.zeros((size, size))
    now = np.zeros((size, size))
    for level in range(size):
        safe = np.where(order < level, order, 0.0)
        alpha = np.sqrt((4.0 * level * level - 1.0) / (level * level - safe * safe)) if level else 0.0
        beta = (
            np.sqrt(((level - 1.0) ** 2 - safe * safe).clip(0) / (4.0 * (level - 1.0) ** 2 - 1.0))
            if level > 1
            else 0.0
        )
        value = np.where(order < level, alpha * (cosv * now - beta * before), 0.0)
        value[level] = start[level]
        table[:, level, :] = value.astype(np.float32).astype(ml_dtypes.bfloat16)
        before, now = now, value
    return table


def quadrature(nlat, nlon):
    theta = math.pi * (np.arange(nlat) + 0.5) / nlat
    return (math.pi / nlat * np.sin(theta) * (2.0 * math.pi / nlon)).astype(np.float32)


def fourier_tables(nlon, modes, lon_count, rows):
    phase = np.arange(nlon)[:, None] * np.arange(modes)[None, :] % nlon
    angle = 2.0 * math.pi / nlon * phase
    pair = np.stack([np.cos(angle), -np.sin(angle)]).astype(np.float32).astype(ml_dtypes.bfloat16)
    factor = np.where(np.arange(modes) == 0, 1.0, 2.0).astype(np.float32)
    doubled = (pair.astype(np.float32) * factor).astype(ml_dtypes.bfloat16)

    def arrange(values):
        values = values.reshape(2, nlon, lon_count, -1).transpose(2, 0, 3, 1)
        values = np.repeat(values[:, :, :, None], rows, axis=3)
        return np.ascontiguousarray(values.reshape(lon_count, -1, nlon))

    return arrange(pair), arrange(doubled)


def gelu_parts(values):
    half = 0.5 * (1.0 + lax.erf(values * (1.0 / math.sqrt(2.0))))
    slope = half + values * jnp.exp(-0.5 * values * values) * (1.0 / math.sqrt(2.0 * math.pi))
    return values * half, slope


def swap_blocks(values, axis):
    return lax.all_to_all(values, axis, split_axis=0, concat_axis=0, tiled=True)


PLAIN = (((1,), (0,)), ((), ()))
TURNED = (((0,), (0,)), ((), ()))
MIB = 1024 * 1024


def product_kernel(dims, matrix_ref, values_ref, out_ref):
    width = out_ref.shape[-1]
    values = values_ref[...].reshape(-1, width)
    out = lax.dot_general(matrix_ref[0], values, dims, preferred_element_type=jnp.float32)
    out_ref[...] = out.astype(jnp.bfloat16).reshape(out_ref.shape)


def split_scale(quad_refs, lat_ref, rows, row):
    return quad_refs[0][rows * lat_ref[0] + row] if quad_refs else 1.0


def to_orders_kernel(lon_ref, lat_ref, matrix_ref, values_ref, *refs):
    *quad_refs, out_ref = refs
    rows, width = out_ref.shape[1:]
    period = values_ref.shape[1] // rows
    total = None
    for row in range(rows):
        values = values_ref[:, row * period : (row + 1) * period, :].reshape(-1, width)
        out = jnp.dot(matrix_ref[0], values, preferred_element_type=jnp.float32)
        if quad_refs:
            out = out * split_scale(quad_refs, lat_ref, rows, row)
        level = lax.broadcasted_iota(jnp.int32, out.shape, 0) & (rows - 1)
        total = out if row == 0 else jnp.where(level == row, out, total)
    out_ref[...] = total.astype(jnp.bfloat16).reshape(out_ref.shape)


def from_orders_kernel(lon_ref, lat_ref, matrix_ref, values_ref, *refs):
    *quad_refs, out_ref = refs
    rows, width = values_ref.shape[1:]
    count, size, _ = out_ref.shape
    period = size // rows
    values = values_ref[...].reshape(-1, width)
    level = lax.broadcasted_iota(jnp.int32, values.shape, 0) & (rows - 1)
    for row in range(rows):
        chosen = jnp.where(level == row, values, jnp.zeros_like(values))
        out = jnp.dot(matrix_ref[0], chosen, preferred_element_type=jnp.float32)
        if quad_refs:
            out = out * split_scale(quad_refs, lat_ref, rows, row)
        out = out.astype(jnp.bfloat16).reshape(count, period, width)
        out_ref[:, row * period : (row + 1) * period, :] = out


def gradient_kernel(core_ref, act_ref, back_ref, hidden_ref, pre_grad_ref, *refs):
    keep_ref, give_ref, in_ref, out_ref, flat_ref = refs
    lat_count = keep_ref.shape[0]
    dims = (((0,), (0,)), ((), ()))
    pairs = ((hidden_ref, pre_grad_ref, in_ref), (act_ref, back_ref, out_ref))
    for part, (left_ref, right_ref, ref) in enumerate(pairs):
        total = lax.dot_general(
            left_ref[...], right_ref[...], dims, preferred_element_type=jnp.float32
        )
        size, width = total.shape
        step = size // lat_count
        for tile in range(width // 128):
            ref[tile * size : (tile + 1) * size, :] = total[:, tile * 128 : (tile + 1) * 128]
        for i in range(step):
            for tile in range(width // 128):
                lane = i * width + tile * 128
                rows = ref[pl.ds(tile * size + i, lat_count, stride=step), :]
                flat_ref[part, :, lane : lane + 128] = rows
    for core in range(2):

        @pl.when(core_ref[0] == core)
        def _():
            keep_ref[...] = flat_ref[core]
            give_ref[...] = flat_ref[1 - core].astype(jnp.bfloat16)


def beside_kernel(dims, matrix_ref, values_ref, extra_ref, out_ref):
    width = values_ref.shape[-1]
    values = values_ref[...].reshape(-1, width)
    out = lax.dot_general(matrix_ref[0], values, dims, preferred_element_type=jnp.float32)
    out_ref[:, :, :width] = out.astype(jnp.bfloat16).reshape(values_ref.shape)
    out_ref[:, :, width:] = extra_ref[...]


def mix_kernel(conjugate, weights_ref, values_ref, out_ref):
    rows, width = weights_ref.shape[1], weights_ref.shape[3]
    values = values_ref[...].reshape(-1, width)
    level = lax.broadcasted_iota(jnp.int32, values.shape, 0) & (rows - 1)
    dims = (((1,), (0 if conjugate else 1,)), ((), ()))

    def product(part):
        total = None
        for row in range(rows):
            out = lax.dot_general(
                values, weights_ref[part, row], dims, preferred_element_type=jnp.float32
            )
            total = out if row == 0 else jnp.where(level == row, out, total)
        return total

    by_re, by_im = product(0), product(1)
    if conjugate:
        by_im = -by_im
    half = values.shape[0] // 2
    out = jnp.concatenate([by_re[:half] - by_im[half:], by_re[half:] + by_im[:half]])
    out_ref[...] = out.astype(jnp.bfloat16).reshape(out_ref.shape)


def whole(shape):
    return pl.BlockSpec(shape, lambda *_: (0,) * len(shape))


def call_kernel(kernel, operands, blocks, out_shape, flops):
    moved = 2 * (math.prod(out_shape) + sum(math.prod(block) for block in blocks))
    return pl.pallas_call(
        kernel,
        grid=(1,),
        in_specs=[whole(block) for block in blocks],
        out_specs=whole(out_shape),
        out_shape=jax.ShapeDtypeStruct(out_shape, jnp.bfloat16),
        compiler_params=pltpu.CompilerParams(vmem_limit_bytes=20 * MIB),
        cost_estimate=pl.CostEstimate(flops=flops, bytes_accessed=moved, transcendentals=0),
    )(*operands)


def fourier_product(kernel, places, matrices, quad, values, block, out_shape):
    specs = [
        pl.BlockSpec((1,) + matrices.shape[1:], lambda i, lon, lat: (lon[0], 0, 0)),
        whole(block),
    ]
    operands = (matrices, values)
    if quad is not None:
        specs.append(pl.BlockSpec(memory_space=pltpu.SMEM))
        operands += (quad,)
    moved = 2 * (math.prod(out_shape) + math.prod(block) + math.prod(matrices.shape[1:]))
    return pl.pallas_call(
        kernel,
        grid_spec=pltpu.PrefetchScalarGridSpec(
            num_scalar_prefetch=2, grid=(1,), in_specs=specs, out_specs=whole(out_shape)
        ),
        out_shape=jax.ShapeDtypeStruct(out_shape, jnp.bfloat16),
        compiler_params=pltpu.CompilerParams(vmem_limit_bytes=20 * MIB),
        cost_estimate=pl.CostEstimate(
            flops=4 * math.prod(matrices.shape[1:]) * out_shape[-1],
            bytes_accessed=moved,
            transcendentals=0,
        ),
    )(*places, *operands)


def gradient_rows(core, lat_count, act, back, hidden, pre_grad):
    size = hidden.shape[1] * pre_grad.shape[1]
    shape = (lat_count, size // lat_count)
    operands = (act, back, hidden, pre_grad)
    return pl.pallas_call(
        gradient_kernel,
        grid_spec=pltpu.PrefetchScalarGridSpec(
            num_scalar_prefetch=1,
            grid=(1,),
            in_specs=[whole(operand.shape) for operand in operands],
            out_specs=[whole(shape)] * 2,
            scratch_shapes=[
                pltpu.VMEM((size // 128, 128), jnp.float32),
                pltpu.VMEM((size // 128, 128), jnp.float32),
                pltpu.VMEM((2,) + shape, jnp.float32),
            ],
        ),
        out_shape=[
            jax.ShapeDtypeStruct(shape, jnp.float32),
            jax.ShapeDtypeStruct(shape, jnp.bfloat16),
        ],
        compiler_params=pltpu.CompilerParams(vmem_limit_bytes=24 * MIB),
        cost_estimate=pl.CostEstimate(
            flops=4 * size * act.shape[0], bytes_accessed=8 * size, transcendentals=0
        ),
    )(core.reshape(1).astype(jnp.int32), *operands)


def scatter_sum(values, axis, index, count, shifted):
    last = values.ndim - 1
    chunk = values.shape[last] // count
    narrow = values.astype(jnp.bfloat16)
    parts = [lax.dynamic_slice_in_dim(values, index * chunk, chunk, axis=last)]
    for shift in range(1, count):
        to = (index + shift) % count
        block = lax.dynamic_slice_in_dim(narrow, to * chunk, chunk, axis=last)
        parts.append(lax.ppermute(block, axis, shifted(shift)))
    return parts


def add_parts(parts):
    total = parts[0]
    for part in parts[1:]:
        total = total + part.astype(jnp.float32)
    return total


def body(tables, plain, doubled, plain_t, doubled_t, quad, grid, cotangent, *weights_in):
    spectral_weight, w_in, w_out = weights_in
    lat_count = lax.axis_size("lat")
    lon_count = lax.axis_size("lon")
    lat_index = lax.axis_index("lat")
    lon_index = lax.axis_index("lon")
    rows, lon_rows, width = grid.shape
    quarter = width // lon_count
    half = lat_count // 2
    order = lon_index * half + lat_index % half
    places = (lon_index.reshape(1).astype(jnp.int32), lat_index.reshape(1).astype(jnp.int32))
    total_lat = rows * lat_count
    spread = (lat_count, rows, width)
    gathered_shape = (lon_count, rows * lon_rows, width)

    def to_orders(values, matrices, scale):
        return fourier_product(
            to_orders_kernel, places, matrices, scale, values, gathered_shape, spread
        )

    def from_orders(values, matrices, scale):
        out = fourier_product(
            from_orders_kernel, places, matrices, scale, values, spread, gathered_shape
        )
        return jnp.sum(swap_blocks(out, "lon").astype(jnp.float32), axis=0)

    def legendre(dims, values):
        kernel = functools.partial(product_kernel, dims)
        flops = 2 * total_lat * total_lat * width
        blocks = [table.shape, spread]
        return call_kernel(kernel, [table, values], blocks, spread, flops)

    def complex_product(values, conjugate):
        return call_kernel(
            functools.partial(mix_kernel, conjugate),
            [weights, values],
            [weights.shape, spread],
            spread,
            8 * rows * values.size * width,
        )

    with jax.named_scope("forward_analysis"):
        gathered = lax.all_gather(grid.reshape(-1, width), "lon", axis=0)
        gathered, order = lax.optimization_barrier((gathered, order))
        table = lax.dynamic_slice_in_dim(tables, order, 1)
        own_weight = spectral_weight
        own_weight = own_weight.transpose(0, 1, 3, 2)[:, :, None]
        four = swap_blocks(to_orders(gathered, plain_t, quad), "lat")
    with jax.named_scope("weights"):
        weights = jnp.zeros((2, rows, lon_count, quarter, width), jnp.bfloat16)
        weights = lax.dynamic_update_slice_in_dim(weights, own_weight, lon_index, 2)
        for shift in range(1, lon_count):
            pairs = [(i, (i + shift) % lon_count) for i in range(lon_count)]
            moved = lax.ppermute(own_weight, "lon", pairs)
            source = (lon_index + lon_count - shift) % lon_count
            weights = lax.dynamic_update_slice_in_dim(weights, moved, source, 2)
        weights = weights.reshape(2, rows, width, width)
    with jax.named_scope("forward_analysis"):
        spectrum = swap_blocks(legendre(PLAIN, four), "lat")
    with jax.named_scope("mix"):
        mixed = complex_product(spectrum, False)
    with jax.named_scope("forward_synthesis"):
        fields = swap_blocks(legendre(TURNED, swap_blocks(mixed, "lat")), "lat")
        wave_rows = from_orders(fields, doubled, None)
    with jax.named_scope("pointwise"):
        hidden = (grid.reshape(-1, width).astype(jnp.float32) + wave_rows).astype(jnp.bfloat16)
        back = cotangent.reshape(-1, width)
        act_grad = lax.dot_general(
            back, w_out, (((1,), (1,)), ((), ())), preferred_element_type=jnp.float32
        )
        pre = jnp.dot(hidden, w_in, preferred_element_type=jnp.float32)
        value, slope = gelu_parts(pre)
        act = value.astype(jnp.bfloat16)
        pre_grad = (act_grad * slope).astype(jnp.bfloat16)
        hidden_grad = (
            back.astype(jnp.float32)
            + lax.dot_general(
                pre_grad, w_in, (((1,), (1,)), ((), ())), preferred_element_type=jnp.float32
            )
        ).astype(jnp.bfloat16)
        block_output = (
            hidden.astype(jnp.float32) + jnp.dot(act, w_out, preferred_element_type=jnp.float32)
        ).astype(jnp.bfloat16)
    with jax.named_scope("backward_analysis"):
        gathered = lax.all_gather(hidden_grad, "lon", axis=0)
        gathered, hidden, pre_grad, act = lax.optimization_barrier(
            (gathered, hidden, pre_grad, act)
        )
        field_grad = swap_blocks(to_orders(gathered, doubled_t, None), "lat")
    with jax.named_scope("pointwise_weights"):
        keep, give = gradient_rows(lat_index & 1, lat_count, act, back, hidden, pre_grad)
        got = lax.ppermute(give, "lat", [(i, i ^ 1) for i in range(lat_count)])
    with jax.named_scope("backward_analysis"):
        mixed_grad = legendre(PLAIN, field_grad)
        mixed_grad, keep, got = lax.optimization_barrier((mixed_grad, keep, got))
        mixed_grad = swap_blocks(mixed_grad, "lat")
    with jax.named_scope("pointwise_weights"):
        parts = scatter_sum(
            add_parts([keep, got]),
            "lon",
            lon_index,
            lon_count,
            lambda s: [(i, (i + s) % lon_count) for i in range(lon_count)],
        )
    with jax.named_scope("unmix"):
        spectrum_grad = complex_product(mixed_grad, True)
    with jax.named_scope("backward_synthesis"):
        spectrum_grad = swap_blocks(spectrum_grad, "lat")
    with jax.named_scope("pointwise_weights"):
        sums = add_parts(parts)
        width_half = sums.shape[1] // 2
        high = (lat_index >> 2) & 1 == 1
        low_part, high_part = sums[:, :width_half], sums[:, width_half:]
        give = jnp.where(high, low_part, high_part).astype(jnp.bfloat16)
        got = lax.ppermute(give, "lat", [(i, i ^ 6) for i in range(lat_count)])
        parts = [jnp.where(high, high_part, low_part), got]
    with jax.named_scope("backward_synthesis"):
        extra = add_parts(parts).astype(jnp.bfloat16)
        chunk = extra.shape[1]
        room = -(-chunk // (rows * 128)) * rows * 128
        extra = jnp.pad(extra, ((0, 0), (0, room - chunk)))
        extra = extra.reshape(lat_count, rows, room // rows)
        four_grad = call_kernel(
            functools.partial(beside_kernel, TURNED),
            [table, spectrum_grad, extra],
            [table.shape, spread, extra.shape],
            (lat_count, rows, width + extra.shape[2]),
            2 * total_lat * total_lat * width,
        )
        four_grad, left, right = lax.optimization_barrier((four_grad, spectrum, mixed_grad))
        four_grad = swap_blocks(four_grad, "lat")
        wave_grad = from_orders(four_grad, plain, quad)
        grad_input = (hidden_grad.astype(jnp.float32) + wave_grad).astype(jnp.bfloat16)
    with jax.named_scope("unmix"):
        right = jnp.stack([right, jnp.concatenate([right[half:], -right[:half]])])
        outer = jnp.einsum("pli,rpld->rlid", left, right, preferred_element_type=jnp.float32)
        outer = outer.reshape(2, rows, lon_count, quarter, width)
        own = lax.dynamic_index_in_dim(outer, lon_index, 2, keepdims=False)
        narrow = outer.astype(jnp.bfloat16)
        grad_spectral = [own]
        for shift in range(1, lon_count):
            to = (lon_index + shift) % lon_count
            block = lax.dynamic_index_in_dim(narrow, to, 2, keepdims=False)
            pairs = [(i, (i + shift) % lon_count) for i in range(lon_count)]
            grad_spectral.append(lax.ppermute(block, "lon", pairs))
        grad_spectral = add_parts(grad_spectral)
    with jax.named_scope("pointwise_weights"):
        sums = four_grad[:, :, width:].reshape(lat_count // 8, 2, 2, 2, room)[..., :chunk]
        sums = jnp.sum(sums.astype(jnp.float32), axis=(0, 2)).swapaxes(0, 1).reshape(2, -1)
    return (
        block_output.reshape(grid.shape),
        grad_input.reshape(grid.shape),
        grad_spectral,
        sums[0],
        sums[1],
    )


def solution(mesh):
    in_specs = (P("lat", "lon", None), P("lat", "lon", None), P(None, "lat", None, "lon"), P(), P())
    out_specs = (
        P("lat", "lon", None),
        P("lat", "lon", None),
        P(None, "lat", "lon", None),
        P(("lat", "lon")),
        P(("lat", "lon")),
    )

    def call(grid, cotangent, spectral_weight, w_in, w_out):
        nlat, nlon, _ = grid.shape
        table = legendre_table(nlat)
        rows = nlat // mesh.shape["lat"]
        plain_t, doubled_t = fourier_tables(nlon, nlat, mesh.shape["lon"], rows)
        plain = np.ascontiguousarray(plain_t.swapaxes(1, 2))
        doubled = np.ascontiguousarray(doubled_t.swapaxes(1, 2))
        quad = quadrature(nlat, nlon)
        mapped = jax.shard_map(
            body,
            mesh=mesh,
            in_specs=(P(),) * 6 + in_specs,
            out_specs=out_specs,
            check_vma=False,
        )
        tables = (table, plain, doubled, plain_t, doubled_t, quad)
        return mapped(*tables, grid, cotangent, spectral_weight, w_in, w_out)

    return call
```

```python
import functools
import math

import jax
import jax.numpy as jnp
import ml_dtypes
import numpy as np
from jax import lax
from jax.experimental import pallas as pl
from jax.experimental.pallas import tpu as pltpu
from jax.sharding import PartitionSpec as P


def legendre_table(size):
    theta = math.pi * (np.arange(size) + 0.5) / size
    cosv, sinv = np.cos(theta), np.sin(theta)
    order = np.arange(size, dtype=np.float64)[:, None]
    start = np.empty((size, size))
    start[0] = math.sqrt(1.0 / (4.0 * math.pi))
    for m in range(1, size):
        start[m] = start[m - 1] * math.sqrt((2 * m + 1) / (2.0 * m)) * sinv
    table = np.zeros((size, size, size), dtype=ml_dtypes.bfloat16)
    before = np.zeros((size, size))
    now = np.zeros((size, size))
    for level in range(size):
        safe = np.where(order < level, order, 0.0)
        alpha = np.sqrt((4.0 * level * level - 1.0) / (level * level - safe * safe)) if level else 0.0
        beta = (
            np.sqrt(((level - 1.0) ** 2 - safe * safe).clip(0) / (4.0 * (level - 1.0) ** 2 - 1.0))
            if level > 1
            else 0.0
        )
        value = np.where(order < level, alpha * (cosv * now - beta * before), 0.0)
        value[level] = start[level]
        table[:, level, :] = value.astype(np.float32).astype(ml_dtypes.bfloat16)
        before, now = now, value
    return table


def quadrature(nlat, nlon):
    theta = math.pi * (np.arange(nlat) + 0.5) / nlat
    return (math.pi / nlat * np.sin(theta) * (2.0 * math.pi / nlon)).astype(np.float32)


def fourier_tables(nlon, modes, lon_count, rows):
    phase = np.arange(nlon)[:, None] * np.arange(modes)[None, :] % nlon
    angle = 2.0 * math.pi / nlon * phase
    pair = np.stack([np.cos(angle), -np.sin(angle)]).astype(np.float32).astype(ml_dtypes.bfloat16)
    factor = np.where(np.arange(modes) == 0, 1.0, 2.0).astype(np.float32)
    doubled = (pair.astype(np.float32) * factor).astype(ml_dtypes.bfloat16)

    def arrange(values):
        values = values.reshape(2, nlon, lon_count, -1).transpose(2, 0, 3, 1)
        values = np.repeat(values[:, :, :, None], rows, axis=3)
        return np.ascontiguousarray(values.reshape(lon_count, -1, nlon))

    return arrange(pair), arrange(doubled)


def gelu_parts(values):
    half = 0.5 * (1.0 + lax.erf(values * (1.0 / math.sqrt(2.0))))
    slope = half + values * jnp.exp(-0.5 * values * values) * (1.0 / math.sqrt(2.0 * math.pi))
    return values * half, slope


def swap_blocks(values, axis):
    return lax.all_to_all(values, axis, split_axis=0, concat_axis=0, tiled=True)


PLAIN = (((1,), (0,)), ((), ()))
TURNED = (((0,), (0,)), ((), ()))
MIB = 1024 * 1024


def product_kernel(dims, matrix_ref, values_ref, out_ref):
    width = out_ref.shape[-1]
    values = values_ref[...].reshape(-1, width)
    out = lax.dot_general(matrix_ref[0], values, dims, preferred_element_type=jnp.float32)
    out_ref[...] = out.astype(jnp.bfloat16).reshape(out_ref.shape)


def to_orders_kernel(lon_ref, matrix_ref, values_ref, out_ref):
    rows, width = out_ref.shape[1:]
    period = values_ref.shape[1] // rows
    total = None
    for row in range(rows):
        values = values_ref[:, row * period : (row + 1) * period, :].reshape(-1, width)
        out = jnp.dot(matrix_ref[0], values, preferred_element_type=jnp.float32)
        level = lax.broadcasted_iota(jnp.int32, out.shape, 0) & (rows - 1)
        total = out if row == 0 else jnp.where(level == row, out, total)
    out_ref[...] = total.astype(jnp.bfloat16).reshape(out_ref.shape)


def from_orders_kernel(lon_ref, matrix_ref, values_ref, out_ref):
    rows = values_ref.shape[1]
    count, size, width = out_ref.shape
    period = size // rows
    values = values_ref[:, :, :width].reshape(-1, width)
    level = lax.broadcasted_iota(jnp.int32, values.shape, 0) & (rows - 1)
    for row in range(rows):
        chosen = jnp.where(level == row, values, jnp.zeros_like(values))
        out = jnp.dot(matrix_ref[0], chosen, preferred_element_type=jnp.float32)
        out = out.astype(jnp.bfloat16).reshape(count, period, width)
        out_ref[:, row * period : (row + 1) * period, :] = out


def gradient_kernel(core_ref, act_ref, back_ref, hidden_ref, pre_grad_ref, *refs):
    keep_ref, give_ref, in_ref, out_ref, flat_ref = refs
    lat_count = keep_ref.shape[0]
    dims = (((0,), (0,)), ((), ()))
    pairs = ((hidden_ref, pre_grad_ref, in_ref), (act_ref, back_ref, out_ref))
    for part, (left_ref, right_ref, ref) in enumerate(pairs):
        total = lax.dot_general(
            left_ref[...], right_ref[...], dims, preferred_element_type=jnp.float32
        )
        size, width = total.shape
        step = size // lat_count
        for tile in range(width // 128):
            ref[tile * size : (tile + 1) * size, :] = total[:, tile * 128 : (tile + 1) * 128]
        for i in range(step):
            for tile in range(width // 128):
                lane = i * width + tile * 128
                rows = ref[pl.ds(tile * size + i, lat_count, stride=step), :]
                flat_ref[part, :, lane : lane + 128] = rows
    for core in range(2):

        @pl.when(core_ref[0] == core)
        def _():
            keep_ref[...] = flat_ref[core]
            give_ref[...] = flat_ref[1 - core].astype(jnp.bfloat16)


def weighted_kernel(matrix_ref, quad_ref, values_ref, out_ref):
    width = out_ref.shape[-1]
    values = values_ref[...].reshape(-1, width).astype(jnp.float32) * quad_ref[...]
    values = values.astype(jnp.bfloat16)
    out = jnp.dot(matrix_ref[0], values, preferred_element_type=jnp.float32)
    out_ref[...] = out.astype(jnp.bfloat16).reshape(out_ref.shape)


def beside_kernel(matrix_ref, quad_ref, values_ref, extra_ref, out_ref):
    width = values_ref.shape[-1]
    values = values_ref[...].reshape(-1, width)
    out = lax.dot_general(matrix_ref[0], values, TURNED, preferred_element_type=jnp.float32)
    out = out * quad_ref[...]
    out_ref[:, :, :width] = out.astype(jnp.bfloat16).reshape(values_ref.shape)
    out_ref[:, :, width:] = extra_ref[...]


def mix_kernel(conjugate, weights_ref, values_ref, out_ref):
    rows, width = weights_ref.shape[1], weights_ref.shape[3]
    values = values_ref[...].reshape(-1, width)
    level = lax.broadcasted_iota(jnp.int32, values.shape, 0) & (rows - 1)
    dims = (((1,), (0 if conjugate else 1,)), ((), ()))

    def product(part):
        total = None
        for row in range(rows):
            out = lax.dot_general(
                values, weights_ref[part, row], dims, preferred_element_type=jnp.float32
            )
            total = out if row == 0 else jnp.where(level == row, out, total)
        return total

    by_re, by_im = product(0), product(1)
    if conjugate:
        by_im = -by_im
    half = values.shape[0] // 2
    out = jnp.concatenate([by_re[:half] - by_im[half:], by_re[half:] + by_im[:half]])
    out_ref[...] = out.astype(jnp.bfloat16).reshape(out_ref.shape)


def whole(shape):
    return pl.BlockSpec(shape, lambda *_: (0,) * len(shape))


def call_kernel(kernel, operands, blocks, out_shape, flops):
    moved = 2 * (math.prod(out_shape) + sum(math.prod(block) for block in blocks))
    return pl.pallas_call(
        kernel,
        grid=(1,),
        in_specs=[whole(block) for block in blocks],
        out_specs=whole(out_shape),
        out_shape=jax.ShapeDtypeStruct(out_shape, jnp.bfloat16),
        compiler_params=pltpu.CompilerParams(vmem_limit_bytes=20 * MIB),
        cost_estimate=pl.CostEstimate(flops=flops, bytes_accessed=moved, transcendentals=0),
    )(*operands)


def fourier_product(kernel, place, matrices, values, block, out_shape):
    specs = [
        pl.BlockSpec((1,) + matrices.shape[1:], lambda i, lon: (lon[0], 0, 0)),
        whole(block),
    ]
    moved = 2 * (math.prod(out_shape) + math.prod(block) + math.prod(matrices.shape[1:]))
    return pl.pallas_call(
        kernel,
        grid_spec=pltpu.PrefetchScalarGridSpec(
            num_scalar_prefetch=1, grid=(1,), in_specs=specs, out_specs=whole(out_shape)
        ),
        out_shape=jax.ShapeDtypeStruct(out_shape, jnp.bfloat16),
        compiler_params=pltpu.CompilerParams(vmem_limit_bytes=20 * MIB),
        cost_estimate=pl.CostEstimate(
            flops=4 * math.prod(matrices.shape[1:]) * out_shape[-1],
            bytes_accessed=moved,
            transcendentals=0,
        ),
    )(place.reshape(1).astype(jnp.int32), matrices, values)


def gradient_rows(core, lat_count, act, back, hidden, pre_grad):
    size = hidden.shape[1] * pre_grad.shape[1]
    shape = (lat_count, size // lat_count)
    operands = (act, back, hidden, pre_grad)
    return pl.pallas_call(
        gradient_kernel,
        grid_spec=pltpu.PrefetchScalarGridSpec(
            num_scalar_prefetch=1,
            grid=(1,),
            in_specs=[whole(operand.shape) for operand in operands],
            out_specs=[whole(shape)] * 2,
            scratch_shapes=[
                pltpu.VMEM((size // 128, 128), jnp.float32),
                pltpu.VMEM((size // 128, 128), jnp.float32),
                pltpu.VMEM((2,) + shape, jnp.float32),
            ],
        ),
        out_shape=[
            jax.ShapeDtypeStruct(shape, jnp.float32),
            jax.ShapeDtypeStruct(shape, jnp.bfloat16),
        ],
        compiler_params=pltpu.CompilerParams(vmem_limit_bytes=24 * MIB),
        cost_estimate=pl.CostEstimate(
            flops=4 * size * act.shape[0], bytes_accessed=8 * size, transcendentals=0
        ),
    )(core.reshape(1).astype(jnp.int32), *operands)


def scatter_sum(values, axis, index, count, shifted):
    last = values.ndim - 1
    chunk = values.shape[last] // count
    narrow = values.astype(jnp.bfloat16)
    parts = [lax.dynamic_slice_in_dim(values, index * chunk, chunk, axis=last)]
    for shift in range(1, count):
        to = (index + shift) % count
        block = lax.dynamic_slice_in_dim(narrow, to * chunk, chunk, axis=last)
        parts.append(lax.ppermute(block, axis, shifted(shift)))
    return parts


def add_parts(parts):
    total = parts[0]
    for part in parts[1:]:
        total = total + part.astype(jnp.float32)
    return total


def body(tables, plain, doubled, plain_t, doubled_t, quad, grid, cotangent, *weights_in):
    spectral_weight, w_in, w_out = weights_in
    lat_count = lax.axis_size("lat")
    lon_count = lax.axis_size("lon")
    lat_index = lax.axis_index("lat")
    lon_index = lax.axis_index("lon")
    rows, lon_rows, width = grid.shape
    quarter = width // lon_count
    half = lat_count // 2
    order = lon_index * half + lat_index % half
    total_lat = rows * lat_count
    spread = (lat_count, rows, width)
    gathered_shape = (lon_count, rows * lon_rows, width)

    def to_orders(values, matrices):
        return fourier_product(
            to_orders_kernel, lon_index, matrices, values, gathered_shape, spread
        )

    def from_orders(values, matrices):
        out = fourier_product(
            from_orders_kernel, lon_index, matrices, values, values.shape, gathered_shape
        )
        return jnp.sum(swap_blocks(out, "lon").astype(jnp.float32), axis=0)

    def legendre(dims, values):
        kernel = functools.partial(product_kernel, dims)
        flops = 2 * total_lat * total_lat * width
        blocks = [table.shape, spread]
        return call_kernel(kernel, [table, values], blocks, spread, flops)

    def complex_product(values, conjugate):
        return call_kernel(
            functools.partial(mix_kernel, conjugate),
            [weights, values],
            [weights.shape, spread],
            spread,
            8 * rows * values.size * width,
        )

    with jax.named_scope("forward_analysis"):
        gathered = lax.all_gather(grid.reshape(-1, width), "lon", axis=0)
        gathered, order = lax.optimization_barrier((gathered, order))
        table = lax.dynamic_slice_in_dim(tables, order, 1)
        own_weight = spectral_weight
        own_weight = own_weight.transpose(0, 1, 3, 2)[:, :, None]
        four = swap_blocks(to_orders(gathered, plain_t), "lat")
    with jax.named_scope("weights"):
        weights = jnp.zeros((2, rows, lon_count, quarter, width), jnp.bfloat16)
        weights = lax.dynamic_update_slice_in_dim(weights, own_weight, lon_index, 2)
        for shift in range(1, lon_count):
            pairs = [(i, (i + shift) % lon_count) for i in range(lon_count)]
            moved = lax.ppermute(own_weight, "lon", pairs)
            source = (lon_index + lon_count - shift) % lon_count
            weights = lax.dynamic_update_slice_in_dim(weights, moved, source, 2)
        weights = weights.reshape(2, rows, width, width)
    with jax.named_scope("forward_analysis"):
        spectrum = call_kernel(
            weighted_kernel,
            [table, quad, four],
            [table.shape, quad.shape, spread],
            spread,
            2 * total_lat * total_lat * width,
        )
        spectrum = swap_blocks(spectrum, "lat")
    with jax.named_scope("mix"):
        mixed = complex_product(spectrum, False)
    with jax.named_scope("forward_synthesis"):
        fields = swap_blocks(legendre(TURNED, swap_blocks(mixed, "lat")), "lat")
        wave_rows = from_orders(fields, doubled)
    with jax.named_scope("pointwise"):
        hidden = (grid.reshape(-1, width).astype(jnp.float32) + wave_rows).astype(jnp.bfloat16)
        back = cotangent.reshape(-1, width)
        act_grad = lax.dot_general(
            back, w_out, (((1,), (1,)), ((), ())), preferred_element_type=jnp.float32
        )
        pre = jnp.dot(hidden, w_in, preferred_element_type=jnp.float32)
        value, slope = gelu_parts(pre)
        act = value.astype(jnp.bfloat16)
        pre_grad = (act_grad * slope).astype(jnp.bfloat16)
        hidden_grad = (
            back.astype(jnp.float32)
            + lax.dot_general(
                pre_grad, w_in, (((1,), (1,)), ((), ())), preferred_element_type=jnp.float32
            )
        ).astype(jnp.bfloat16)
        block_output = (
            hidden.astype(jnp.float32) + jnp.dot(act, w_out, preferred_element_type=jnp.float32)
        ).astype(jnp.bfloat16)
    with jax.named_scope("backward_analysis"):
        gathered = lax.all_gather(hidden_grad, "lon", axis=0)
        gathered, hidden, pre_grad, act = lax.optimization_barrier(
            (gathered, hidden, pre_grad, act)
        )
        field_grad = swap_blocks(to_orders(gathered, doubled_t), "lat")
    with jax.named_scope("pointwise_weights"):
        keep, give = gradient_rows(lat_index & 1, lat_count, act, back, hidden, pre_grad)
        got = lax.ppermute(give, "lat", [(i, i ^ 1) for i in range(lat_count)])
    with jax.named_scope("backward_analysis"):
        mixed_grad = legendre(PLAIN, field_grad)
        mixed_grad, keep, got = lax.optimization_barrier((mixed_grad, keep, got))
        mixed_grad = swap_blocks(mixed_grad, "lat")
    with jax.named_scope("pointwise_weights"):
        parts = scatter_sum(
            add_parts([keep, got]),
            "lon",
            lon_index,
            lon_count,
            lambda s: [(i, (i + s) % lon_count) for i in range(lon_count)],
        )
    with jax.named_scope("unmix"):
        spectrum_grad = complex_product(mixed_grad, True)
    with jax.named_scope("backward_synthesis"):
        spectrum_grad = swap_blocks(spectrum_grad, "lat")
    with jax.named_scope("pointwise_weights"):
        sums = add_parts(parts)
        width_half = sums.shape[1] // 2
        high = (lat_index >> 2) & 1 == 1
        low_part, high_part = sums[:, :width_half], sums[:, width_half:]
        give = jnp.where(high, low_part, high_part).astype(jnp.bfloat16)
        got = lax.ppermute(give, "lat", [(i, i ^ 6) for i in range(lat_count)])
        parts = [jnp.where(high, high_part, low_part), got]
    with jax.named_scope("backward_synthesis"):
        extra = add_parts(parts).astype(jnp.bfloat16)
        chunk = extra.shape[1]
        room = -(-chunk // (rows * 128)) * rows * 128
        extra = jnp.pad(extra, ((0, 0), (0, room - chunk)))
        extra = extra.reshape(lat_count, rows, room // rows)
        four_grad = call_kernel(
            beside_kernel,
            [table, quad, spectrum_grad, extra],
            [table.shape, quad.shape, spread, extra.shape],
            (lat_count, rows, width + extra.shape[2]),
            2 * total_lat * total_lat * width,
        )
        four_grad, left, right = lax.optimization_barrier((four_grad, spectrum, mixed_grad))
        four_grad = swap_blocks(four_grad, "lat")
        wave_grad = from_orders(four_grad, plain)
        grad_input = (hidden_grad.astype(jnp.float32) + wave_grad).astype(jnp.bfloat16)
    with jax.named_scope("unmix"):
        right = jnp.stack([right, jnp.concatenate([right[half:], -right[:half]])])
        outer = jnp.einsum("pli,rpld->rlid", left, right, preferred_element_type=jnp.float32)
        outer = outer.reshape(2, rows, lon_count, quarter, width)
        own = lax.dynamic_index_in_dim(outer, lon_index, 2, keepdims=False)
        narrow = outer.astype(jnp.bfloat16)
        grad_spectral = [own]
        for shift in range(1, lon_count):
            to = (lon_index + shift) % lon_count
            block = lax.dynamic_index_in_dim(narrow, to, 2, keepdims=False)
            pairs = [(i, (i + shift) % lon_count) for i in range(lon_count)]
            grad_spectral.append(lax.ppermute(block, "lon", pairs))
        grad_spectral = add_parts(grad_spectral)
    with jax.named_scope("pointwise_weights"):
        sums = four_grad[:, :, width:].reshape(lat_count // 8, 2, 2, 2, room)[..., :chunk]
        sums = jnp.sum(sums.astype(jnp.float32), axis=(0, 2)).swapaxes(0, 1).reshape(2, -1)
    return (
        block_output.reshape(grid.shape),
        grad_input.reshape(grid.shape),
        grad_spectral,
        sums[0],
        sums[1],
    )


def solution(mesh):
    in_specs = (P("lat", "lon", None), P("lat", "lon", None), P(None, "lat", None, "lon"), P(), P())
    out_specs = (
        P("lat", "lon", None),
        P("lat", "lon", None),
        P(None, "lat", "lon", None),
        P(("lat", "lon")),
        P(("lat", "lon")),
    )

    def call(grid, cotangent, spectral_weight, w_in, w_out):
        nlat, nlon, _ = grid.shape
        table = legendre_table(nlat)
        rows = nlat // mesh.shape["lat"]
        plain_t, doubled_t = fourier_tables(nlon, nlat, mesh.shape["lon"], rows)
        plain = np.ascontiguousarray(plain_t.swapaxes(1, 2))
        doubled = np.ascontiguousarray(doubled_t.swapaxes(1, 2))
        quad = quadrature(nlat, nlon)[:, None]
        mapped = jax.shard_map(
            body,
            mesh=mesh,
            in_specs=(P(),) * 6 + in_specs,
            out_specs=out_specs,
            check_vma=False,
        )
        tables = (table, plain, doubled, plain_t, doubled_t, quad)
        return mapped(*tables, grid, cotangent, spectral_weight, w_in, w_out)

    return call
```

```python
import functools
import math

import jax
import jax.numpy as jnp
import ml_dtypes
import numpy as np
from jax import lax
from jax.experimental import pallas as pl
from jax.experimental.pallas import tpu as pltpu
from jax.sharding import PartitionSpec as P


def legendre_table(size):
    theta = math.pi * (np.arange(size) + 0.5) / size
    cosv, sinv = np.cos(theta), np.sin(theta)
    order = np.arange(size, dtype=np.float64)[:, None]
    start = np.empty((size, size))
    start[0] = math.sqrt(1.0 / (4.0 * math.pi))
    for m in range(1, size):
        start[m] = start[m - 1] * math.sqrt((2 * m + 1) / (2.0 * m)) * sinv
    table = np.zeros((size, size, size), dtype=ml_dtypes.bfloat16)
    before = np.zeros((size, size))
    now = np.zeros((size, size))
    for level in range(size):
        safe = np.where(order < level, order, 0.0)
        alpha = np.sqrt((4.0 * level * level - 1.0) / (level * level - safe * safe)) if level else 0.0
        beta = (
            np.sqrt(((level - 1.0) ** 2 - safe * safe).clip(0) / (4.0 * (level - 1.0) ** 2 - 1.0))
            if level > 1
            else 0.0
        )
        value = np.where(order < level, alpha * (cosv * now - beta * before), 0.0)
        value[level] = start[level]
        table[:, level, :] = value.astype(np.float32).astype(ml_dtypes.bfloat16)
        before, now = now, value
    return table


def quadrature(nlat, nlon):
    theta = math.pi * (np.arange(nlat) + 0.5) / nlat
    return (math.pi / nlat * np.sin(theta) * (2.0 * math.pi / nlon)).astype(np.float32)


def fourier_tables(nlon, modes, lon_count, rows):
    phase = np.arange(nlon)[:, None] * np.arange(modes)[None, :] % nlon
    angle = 2.0 * math.pi / nlon * phase
    pair = np.stack([np.cos(angle), -np.sin(angle)]).astype(np.float32).astype(ml_dtypes.bfloat16)
    factor = np.where(np.arange(modes) == 0, 1.0, 2.0).astype(np.float32)
    doubled = (pair.astype(np.float32) * factor).astype(ml_dtypes.bfloat16)

    def arrange(values):
        values = values.reshape(2, nlon, lon_count, -1).transpose(2, 0, 3, 1)
        values = np.repeat(values[:, :, :, None], rows, axis=3)
        return np.ascontiguousarray(values.reshape(lon_count, -1, nlon))

    return arrange(pair), arrange(doubled)


def gelu_parts(values):
    half = 0.5 * (1.0 + lax.erf(values * (1.0 / math.sqrt(2.0))))
    slope = half + values * jnp.exp(-0.5 * values * values) * (1.0 / math.sqrt(2.0 * math.pi))
    return values * half, slope


def swap_blocks(values, axis):
    return lax.all_to_all(values, axis, split_axis=0, concat_axis=0, tiled=True)


PLAIN = (((1,), (0,)), ((), ()))
TURNED = (((0,), (0,)), ((), ()))
MIB = 1024 * 1024


def product_kernel(dims, matrix_ref, values_ref, out_ref):
    width = out_ref.shape[-1]
    values = values_ref[...].reshape(-1, width)
    out = lax.dot_general(matrix_ref[0], values, dims, preferred_element_type=jnp.float32)
    out_ref[...] = out.astype(jnp.bfloat16).reshape(out_ref.shape)


def to_orders_kernel(lon_ref, matrix_ref, values_ref, out_ref):
    rows, width = out_ref.shape[1:]
    period = values_ref.shape[1] // rows
    total = None
    for row in range(rows):
        values = values_ref[:, row * period : (row + 1) * period, :].reshape(-1, width)
        out = jnp.dot(matrix_ref[0], values, preferred_element_type=jnp.float32)
        level = lax.broadcasted_iota(jnp.int32, out.shape, 0) & (rows - 1)
        total = out if row == 0 else jnp.where(level == row, out, total)
    out_ref[...] = total.astype(jnp.bfloat16).reshape(out_ref.shape)


def from_orders_kernel(lon_ref, matrix_ref, values_ref, out_ref):
    rows = values_ref.shape[1]
    count, size, width = out_ref.shape
    period = size // rows
    values = values_ref[:, :, :width].reshape(-1, width)
    level = lax.broadcasted_iota(jnp.int32, values.shape, 0) & (rows - 1)
    for row in range(rows):
        chosen = jnp.where(level == row, values, jnp.zeros_like(values))
        out = jnp.dot(matrix_ref[0], chosen, preferred_element_type=jnp.float32)
        out = out.astype(jnp.bfloat16).reshape(count, period, width)
        out_ref[:, row * period : (row + 1) * period, :] = out


def gradient_kernel(core_ref, act_ref, back_ref, hidden_ref, pre_grad_ref, *refs):
    keep_ref, give_ref, in_ref, out_ref, flat_ref = refs
    lat_count = keep_ref.shape[0]
    dims = (((0,), (0,)), ((), ()))
    pairs = ((hidden_ref, pre_grad_ref, in_ref), (act_ref, back_ref, out_ref))
    for part, (left_ref, right_ref, ref) in enumerate(pairs):
        total = lax.dot_general(
            left_ref[...], right_ref[...], dims, preferred_element_type=jnp.float32
        )
        size, width = total.shape
        step = size // lat_count
        for tile in range(width // 128):
            ref[tile * size : (tile + 1) * size, :] = total[:, tile * 128 : (tile + 1) * 128]
        for i in range(step):
            for tile in range(width // 128):
                lane = i * width + tile * 128
                rows = ref[pl.ds(tile * size + i, lat_count, stride=step), :]
                flat_ref[part, :, lane : lane + 128] = rows
    for core in range(2):

        @pl.when(core_ref[0] == core)
        def _():
            keep_ref[...] = flat_ref[core]
            give_ref[...] = flat_ref[1 - core].astype(jnp.bfloat16)


def weighted_kernel(matrix_ref, quad_ref, values_ref, out_ref):
    width = out_ref.shape[-1]
    values = values_ref[...].reshape(-1, width).astype(jnp.float32) * quad_ref[...]
    values = values.astype(jnp.bfloat16)
    out = jnp.dot(matrix_ref[0], values, preferred_element_type=jnp.float32)
    out_ref[...] = out.astype(jnp.bfloat16).reshape(out_ref.shape)


def beside_kernel(matrix_ref, quad_ref, values_ref, extra_ref, out_ref):
    width = values_ref.shape[-1]
    values = values_ref[...].reshape(-1, width)
    out = lax.dot_general(matrix_ref[0], values, TURNED, preferred_element_type=jnp.float32)
    out = out * quad_ref[...]
    out_ref[:, :, :width] = out.astype(jnp.bfloat16).reshape(values_ref.shape)
    out_ref[:, :, width:] = extra_ref[...]


def mix_kernel(conjugate, weights_ref, values_ref, out_ref):
    rows, width = weights_ref.shape[1], weights_ref.shape[3]
    values = values_ref[...].reshape(-1, width)
    level = lax.broadcasted_iota(jnp.int32, values.shape, 0) & (rows - 1)
    dims = (((1,), (0 if conjugate else 1,)), ((), ()))

    def product(part):
        total = None
        for row in range(rows):
            out = lax.dot_general(
                values, weights_ref[part, row], dims, preferred_element_type=jnp.float32
            )
            total = out if row == 0 else jnp.where(level == row, out, total)
        return total

    by_re, by_im = product(0), product(1)
    half = values.shape[0] // 2
    out = jnp.concatenate([by_re[:half] - by_im[half:], by_re[half:] + by_im[:half]])
    out_ref[...] = out.astype(jnp.bfloat16).reshape(out_ref.shape)


def whole(shape):
    return pl.BlockSpec(shape, lambda *_: (0,) * len(shape))


def call_kernel(kernel, operands, blocks, out_shape, flops):
    moved = 2 * (math.prod(out_shape) + sum(math.prod(block) for block in blocks))
    return pl.pallas_call(
        kernel,
        grid=(1,),
        in_specs=[whole(block) for block in blocks],
        out_specs=whole(out_shape),
        out_shape=jax.ShapeDtypeStruct(out_shape, jnp.bfloat16),
        compiler_params=pltpu.CompilerParams(vmem_limit_bytes=20 * MIB),
        cost_estimate=pl.CostEstimate(flops=flops, bytes_accessed=moved, transcendentals=0),
    )(*operands)


def fourier_product(kernel, place, matrices, values, block, out_shape):
    specs = [
        pl.BlockSpec((1,) + matrices.shape[1:], lambda i, lon: (lon[0], 0, 0)),
        whole(block),
    ]
    moved = 2 * (math.prod(out_shape) + math.prod(block) + math.prod(matrices.shape[1:]))
    return pl.pallas_call(
        kernel,
        grid_spec=pltpu.PrefetchScalarGridSpec(
            num_scalar_prefetch=1, grid=(1,), in_specs=specs, out_specs=whole(out_shape)
        ),
        out_shape=jax.ShapeDtypeStruct(out_shape, jnp.bfloat16),
        compiler_params=pltpu.CompilerParams(vmem_limit_bytes=20 * MIB),
        cost_estimate=pl.CostEstimate(
            flops=4 * math.prod(matrices.shape[1:]) * out_shape[-1],
            bytes_accessed=moved,
            transcendentals=0,
        ),
    )(place.reshape(1).astype(jnp.int32), matrices, values)


def gradient_rows(core, lat_count, act, back, hidden, pre_grad):
    size = hidden.shape[1] * pre_grad.shape[1]
    shape = (lat_count, size // lat_count)
    operands = (act, back, hidden, pre_grad)
    return pl.pallas_call(
        gradient_kernel,
        grid_spec=pltpu.PrefetchScalarGridSpec(
            num_scalar_prefetch=1,
            grid=(1,),
            in_specs=[whole(operand.shape) for operand in operands],
            out_specs=[whole(shape)] * 2,
            scratch_shapes=[
                pltpu.VMEM((size // 128, 128), jnp.float32),
                pltpu.VMEM((size // 128, 128), jnp.float32),
                pltpu.VMEM((2,) + shape, jnp.float32),
            ],
        ),
        out_shape=[
            jax.ShapeDtypeStruct(shape, jnp.float32),
            jax.ShapeDtypeStruct(shape, jnp.bfloat16),
        ],
        compiler_params=pltpu.CompilerParams(vmem_limit_bytes=24 * MIB),
        cost_estimate=pl.CostEstimate(
            flops=4 * size * act.shape[0], bytes_accessed=8 * size, transcendentals=0
        ),
    )(core.reshape(1).astype(jnp.int32), *operands)


def scatter_sum(values, axis, index, count, shifted):
    last = values.ndim - 1
    chunk = values.shape[last] // count
    narrow = values.astype(jnp.bfloat16)
    parts = [lax.dynamic_slice_in_dim(values, index * chunk, chunk, axis=last)]
    for shift in range(1, count):
        to = (index + shift) % count
        block = lax.dynamic_slice_in_dim(narrow, to * chunk, chunk, axis=last)
        parts.append(lax.ppermute(block, axis, shifted(shift)))
    return parts


def add_parts(parts):
    total = parts[0]
    for part in parts[1:]:
        total = total + part.astype(jnp.float32)
    return total


def body(tables, plain, doubled, plain_t, doubled_t, quad, grid, cotangent, *weights_in):
    spectral_weight, w_in, w_out = weights_in
    lat_count = lax.axis_size("lat")
    lon_count = lax.axis_size("lon")
    lat_index = lax.axis_index("lat")
    lon_index = lax.axis_index("lon")
    rows, lon_rows, width = grid.shape
    quarter = width // lon_count
    half = lat_count // 2
    order = lon_index * half + lat_index % half
    total_lat = rows * lat_count
    spread = (lat_count, rows, width)
    gathered_shape = (lon_count, rows * lon_rows, width)

    def to_orders(values, matrices):
        return fourier_product(
            to_orders_kernel, lon_index, matrices, values, gathered_shape, spread
        )

    def from_orders(values, matrices):
        out = fourier_product(
            from_orders_kernel, lon_index, matrices, values, values.shape, gathered_shape
        )
        return jnp.sum(swap_blocks(out, "lon").astype(jnp.float32), axis=0)

    def legendre(dims, values):
        kernel = functools.partial(product_kernel, dims)
        flops = 2 * total_lat * total_lat * width
        blocks = [table.shape, spread]
        return call_kernel(kernel, [table, values], blocks, spread, flops)

    def complex_product(values, weights, conjugate):
        return call_kernel(
            functools.partial(mix_kernel, conjugate),
            [weights, values],
            [weights.shape, spread],
            spread,
            8 * rows * values.size * width,
        )

    with jax.named_scope("forward_analysis"):
        gathered = lax.all_gather(grid.reshape(-1, width), "lon", axis=0)
        gathered, order = lax.optimization_barrier((gathered, order))
        table = lax.dynamic_slice_in_dim(tables, order, 1)
        own_weight = spectral_weight
        own_weight = own_weight.transpose(0, 1, 3, 2)[:, :, None]
        four = swap_blocks(to_orders(gathered, plain_t), "lat")
    with jax.named_scope("weights"):
        weights = jnp.zeros((2, rows, lon_count, quarter, width), jnp.bfloat16)
        weights = lax.dynamic_update_slice_in_dim(weights, own_weight, lon_index, 2)
        for shift in range(1, lon_count):
            pairs = [(i, (i + shift) % lon_count) for i in range(lon_count)]
            moved = lax.ppermute(own_weight, "lon", pairs)
            source = (lon_index + lon_count - shift) % lon_count
            weights = lax.dynamic_update_slice_in_dim(weights, moved, source, 2)
        weights = weights.reshape(2, rows, width, width)
    with jax.named_scope("forward_analysis"):
        spectrum = call_kernel(
            weighted_kernel,
            [table, quad, four],
            [table.shape, quad.shape, spread],
            spread,
            2 * total_lat * total_lat * width,
        )
        spectrum = swap_blocks(spectrum, "lat")
    with jax.named_scope("mix"):
        mixed = complex_product(spectrum, weights, False)
    with jax.named_scope("forward_synthesis"):
        fields = swap_blocks(legendre(TURNED, swap_blocks(mixed, "lat")), "lat")
        wave_rows = from_orders(fields, doubled)
    with jax.named_scope("pointwise"):
        hidden = (grid.reshape(-1, width).astype(jnp.float32) + wave_rows).astype(jnp.bfloat16)
        back = cotangent.reshape(-1, width)
        act_grad = lax.dot_general(
            back, w_out, (((1,), (1,)), ((), ())), preferred_element_type=jnp.float32
        )
        pre = jnp.dot(hidden, w_in, preferred_element_type=jnp.float32)
        value, slope = gelu_parts(pre)
        act = value.astype(jnp.bfloat16)
        pre_grad = (act_grad * slope).astype(jnp.bfloat16)
        hidden_grad = (
            back.astype(jnp.float32)
            + lax.dot_general(
                pre_grad, w_in, (((1,), (1,)), ((), ())), preferred_element_type=jnp.float32
            )
        ).astype(jnp.bfloat16)
        block_output = (
            hidden.astype(jnp.float32) + jnp.dot(act, w_out, preferred_element_type=jnp.float32)
        ).astype(jnp.bfloat16)
    with jax.named_scope("backward_analysis"):
        gathered = lax.all_gather(hidden_grad, "lon", axis=0)
        gathered, hidden, pre_grad, act = lax.optimization_barrier(
            (gathered, hidden, pre_grad, act)
        )
        field_grad = swap_blocks(to_orders(gathered, doubled_t), "lat")
    with jax.named_scope("pointwise_weights"):
        keep, give = gradient_rows(lat_index & 1, lat_count, act, back, hidden, pre_grad)
        got = lax.ppermute(give, "lat", [(i, i ^ 1) for i in range(lat_count)])
    with jax.named_scope("backward_analysis"):
        mixed_grad = legendre(PLAIN, field_grad)
        mixed_grad, keep, got, late = lax.optimization_barrier((mixed_grad, keep, got, weights))
        mixed_grad = swap_blocks(mixed_grad, "lat")
    with jax.named_scope("pointwise_weights"):
        parts = scatter_sum(
            add_parts([keep, got]),
            "lon",
            lon_index,
            lon_count,
            lambda s: [(i, (i + s) % lon_count) for i in range(lon_count)],
        )
    with jax.named_scope("unmix"):
        conjugate = jnp.stack([late[0], -late[1]])
        spectrum_grad = complex_product(mixed_grad, conjugate, True)
    with jax.named_scope("backward_synthesis"):
        spectrum_grad = swap_blocks(spectrum_grad, "lat")
    with jax.named_scope("pointwise_weights"):
        sums = add_parts(parts)
        width_half = sums.shape[1] // 2
        high = (lat_index >> 2) & 1 == 1
        low_part, high_part = sums[:, :width_half], sums[:, width_half:]
        give = jnp.where(high, low_part, high_part).astype(jnp.bfloat16)
        got = lax.ppermute(give, "lat", [(i, i ^ 6) for i in range(lat_count)])
        parts = [jnp.where(high, high_part, low_part), got]
    with jax.named_scope("backward_synthesis"):
        extra = add_parts(parts).astype(jnp.bfloat16)
        chunk = extra.shape[1]
        room = -(-chunk // (rows * 128)) * rows * 128
        extra = jnp.pad(extra, ((0, 0), (0, room - chunk)))
        extra = extra.reshape(lat_count, rows, room // rows)
        four_grad = call_kernel(
            beside_kernel,
            [table, quad, spectrum_grad, extra],
            [table.shape, quad.shape, spread, extra.shape],
            (lat_count, rows, width + extra.shape[2]),
            2 * total_lat * total_lat * width,
        )
        four_grad, left, right = lax.optimization_barrier((four_grad, spectrum, mixed_grad))
        four_grad = swap_blocks(four_grad, "lat")
        wave_grad = from_orders(four_grad, plain)
        grad_input = (hidden_grad.astype(jnp.float32) + wave_grad).astype(jnp.bfloat16)
    with jax.named_scope("unmix"):
        right = jnp.stack([right, jnp.concatenate([right[half:], -right[:half]])])
        outer = jnp.einsum("pli,rpld->rlid", left, right, preferred_element_type=jnp.float32)
        outer = outer.reshape(2, rows, lon_count, quarter, width)
        own = lax.dynamic_index_in_dim(outer, lon_index, 2, keepdims=False)
        narrow = outer.astype(jnp.bfloat16)
        grad_spectral = [own]
        for shift in range(1, lon_count):
            to = (lon_index + shift) % lon_count
            block = lax.dynamic_index_in_dim(narrow, to, 2, keepdims=False)
            pairs = [(i, (i + shift) % lon_count) for i in range(lon_count)]
            grad_spectral.append(lax.ppermute(block, "lon", pairs))
        grad_spectral = add_parts(grad_spectral)
    with jax.named_scope("pointwise_weights"):
        sums = four_grad[:, :, width:].reshape(lat_count // 8, 2, 2, 2, room)[..., :chunk]
        sums = jnp.sum(sums.astype(jnp.float32), axis=(0, 2)).swapaxes(0, 1).reshape(2, -1)
    return (
        block_output.reshape(grid.shape),
        grad_input.reshape(grid.shape),
        grad_spectral,
        sums[0],
        sums[1],
    )


def solution(mesh):
    in_specs = (P("lat", "lon", None), P("lat", "lon", None), P(None, "lat", None, "lon"), P(), P())
    out_specs = (
        P("lat", "lon", None),
        P("lat", "lon", None),
        P(None, "lat", "lon", None),
        P(("lat", "lon")),
        P(("lat", "lon")),
    )

    def call(grid, cotangent, spectral_weight, w_in, w_out):
        nlat, nlon, _ = grid.shape
        table = legendre_table(nlat)
        rows = nlat // mesh.shape["lat"]
        plain_t, doubled_t = fourier_tables(nlon, nlat, mesh.shape["lon"], rows)
        plain = np.ascontiguousarray(plain_t.swapaxes(1, 2))
        doubled = np.ascontiguousarray(doubled_t.swapaxes(1, 2))
        quad = quadrature(nlat, nlon)[:, None]
        mapped = jax.shard_map(
            body,
            mesh=mesh,
            in_specs=(P(),) * 6 + in_specs,
            out_specs=out_specs,
            check_vma=False,
        )
        tables = (table, plain, doubled, plain_t, doubled_t, quad)
        return mapped(*tables, grid, cotangent, spectral_weight, w_in, w_out)

    return call
```
